128 devices in a mesh: gx: 4 (over y), gy: 4 (over x), gz: 8 (over z, core).
Axes of the slice: x: 4, y: 4, z: 4, core: 2. Of those that a mesh axis runs over, the one named last changes fastest.
Arguments:
- right_side: float32 [128, 128, 1024], P('gx', 'gy', 'gz'), may hold values from -30 to 30
- screening: float32 [128, 128, 1024], P('gx', 'gy', 'gz'), may hold values from 0.002 to 0.05
- coarse_inverse: float32 [512, 512], P(('gx', 'gy', 'gz')), may hold values from -1 to 1
Outputs:
- solution_field: float32 [128, 128, 1024], P('gx', 'gy', 'gz')
- residual_norms: float32 [2], replicated
The draws below stay inside these ranges and needn't reach their ends.
All inputs are finite; a program needn't handle non-finite values.
Results may differ from the reference program's by a relative error of at most 0.00011.
Values sent between devices are 32-bit elements; how exact they have to be, the bound alone decides.
No kernel may reach another device: no remote copies, remote signals or barrier semaphores. Data moves between devices by JAX's collectives and lax.ppermute only.
A program may use at most 192 MiB of HBM per device.

```python
import math
import jax
import jax.numpy as jnp
from jax import lax

LEVELS = 5
SWEEPS = 1
CYCLES = 2
NX = 128
NY = 128
NZ = 1024
COARSE = 512
N_GX = 4
N_GY = 4
N_GZ = 8


def draw_right_side(key, part):
    key = jax.random.fold_in(key, 3)
    grid_shape = (NX, NY, NZ)
    across = lax.broadcasted_iota(jnp.float32, grid_shape, 0)
    factor = 1.0 + 2.0 * across / (NX - 1)
    return jnp.clip(jax.random.normal(key, grid_shape, jnp.float32), -6.0, 6.0) * factor


def draw_coarse_inverse(key, part):
    key = jax.random.fold_in(key, 7)
    noise_key, diagonal_key = jax.random.split(key)
    noise = jax.random.normal(noise_key, (COARSE, COARSE), jnp.float32)
    spread_part = (noise + noise.T) * (0.025 / math.sqrt(COARSE))
    diagonal = jnp.exp(jax.random.uniform(diagonal_key, (COARSE,), jnp.float32, math.log(0.04), math.log(0.16)))
    return spread_part + jnp.diag(diagonal)


def levels(key, shape, cuts, low, largest):
    gain = 1.0
    for axis_at, blocks in cuts:
        heights = jax.random.uniform(jax.random.fold_in(jax.random.fold_in(key, 6), axis_at), (blocks,), jnp.float32, low / len(cuts), largest / len(cuts))
        gain = gain * jnp.repeat(jnp.exp(heights), shape[axis_at] // blocks).reshape((-1,) + (1,) * (len(shape) - 1 - axis_at))
    return gain


def setup_inputs(seed: int = 0) -> dict:
    seeds = jax.random.split(jax.random.key(seed), 4)
    right_side = draw_right_side(jax.random.fold_in(seeds[3], 71), 0)
    screening = jnp.clip(jnp.exp(math.log(0.05) - 3.218876 * jax.random.uniform(seeds[1], (NX, NY, NZ), jnp.float32) ** levels(seeds[1], (NX, NY, NZ), ((0, 4), (1, 4), (2, 8)), -0.2, 0.2)), 0.002, 0.05)
    coarse_inverse = draw_coarse_inverse(jax.random.fold_in(seeds[3], 71), 0)
    return dict(right_side=right_side, screening=screening, coarse_inverse=coarse_inverse)


def beside_sum(values):
    summed = jnp.roll(values, -1, 0) + jnp.roll(values, 1, 0)
    summed = summed + jnp.roll(values, -1, 1) + jnp.roll(values, 1, 1)
    return summed + jnp.roll(values, -1, 2) + jnp.roll(values, 1, 2)

def operate(values, screen):
    return (6.0 + screen) * values - beside_sum(values)

def red_cells(grid_shape):
    index_x = lax.broadcasted_iota(jnp.int32, grid_shape, 0)
    index_y = lax.broadcasted_iota(jnp.int32, grid_shape, 1)
    index_z = lax.broadcasted_iota(jnp.int32, grid_shape, 2)
    return (index_x + index_y + index_z) % 2 == 0

def relax_sweep(values, source, screen, red_mask):
    values = jnp.where(red_mask, (source + beside_sum(values)) / (6.0 + screen), values)
    return jnp.where(red_mask, values, (source + beside_sum(values)) / (6.0 + screen))

def coarsen(values):
    size_x, size_y, size_z = values.shape
    return 0.5 * values.reshape(size_x // 2, 2, size_y // 2, 2, size_z // 2, 2).sum(axis=(1, 3, 5))

def refine(values):
    return jnp.repeat(jnp.repeat(jnp.repeat(values, 2, 0), 2, 1), 2, 2)

def reference(right_side, screening, coarse_inverse):
    screens = [screening]
    for level in range(LEVELS):
        screens.append(coarsen(screens[-1]))
    red_masks = [red_cells(screen_level.shape) for screen_level in screens[:LEVELS]]
    solution_field = jnp.zeros_like(right_side)
    norm_list = []
    for cycle_index in range(CYCLES):
        sources = [right_side]
        smoothed = []
        for level in range(LEVELS):
            values = solution_field if level == 0 else jnp.zeros_like(sources[level])
            for sweep_index in range(SWEEPS):
                values = relax_sweep(values, sources[level], screens[level], red_masks[level])
            smoothed.append(values)
            remainder = sources[level] - operate(values, screens[level])
            sources.append(coarsen(remainder))
        coarse = sources[LEVELS]
        block_x = coarse.shape[0] // N_GX
        block_y = coarse.shape[1] // N_GY
        block_z = coarse.shape[2] // N_GZ
        blocks = coarse.reshape(N_GX, block_x, N_GY, block_y, N_GZ, block_z).transpose(0, 2, 4, 1, 3, 5).reshape(-1)
        answer = jnp.dot(coarse_inverse, blocks, precision=lax.Precision.HIGHEST)
        correction = answer.reshape(N_GX, N_GY, N_GZ, block_x, block_y, block_z).transpose(0, 3, 1, 4, 2, 5).reshape(coarse.shape)
        for level in reversed(range(LEVELS)):
            values = smoothed[level] + refine(correction)
            for sweep_index in range(SWEEPS):
                values = relax_sweep(values, sources[level], screens[level], red_masks[level])
            correction = values
        solution_field = correction
        remainder = right_side - operate(solution_field, screening)
        norm_list.append(jnp.sqrt(jnp.sum(remainder * remainder) / remainder.size))
    return (solution_field, jnp.stack(norm_list))
```

```python
import functools

import jax
import jax.numpy as jnp
from jax import lax
from jax.experimental import pallas as pl
from jax.experimental.pallas import tpu as pltpu
from jax.sharding import PartitionSpec as P

AXES = ("gx", "gy", "gz")
F32 = jnp.float32
LANES = 128
OWN = 32
H0 = 8
X0, Y0 = 48, 48
H1 = 14
X1, Y1 = 44, 48
H2 = 6
X2, Y2 = 20, 24
GROUP0 = 8
GROUP1 = 4
CELLS = 16777216.0


def iota(shape, dim):
    return lax.broadcasted_iota(jnp.int32, shape, dim)


def roll(value, shift, axis):
    return pltpu.roll(value, shift % value.shape[axis], axis)


def pick(value, index):
    return jnp.take_along_axis(value, index, axis=1, mode="promise_in_bounds")


def loop(start, stop, body, unroll=2):
    def step(index, carry):
        body(index)
        return carry

    lax.fori_loop(start, stop, step, 0, unroll=unroll)


def call(body, outs, *operands, scratch=()):
    specs = [
        pl.BlockSpec(memory_space=pltpu.SMEM if operand.dtype == jnp.int32 else pltpu.VMEM)
        for operand in operands
    ]
    return pl.pallas_call(
        body,
        out_shape=[jax.ShapeDtypeStruct(shape, F32) for shape in outs],
        in_specs=specs,
        out_specs=[pl.BlockSpec(memory_space=pltpu.VMEM)] * len(outs),
        scratch_shapes=[pltpu.VMEM(shape, F32) for shape in scratch],
        compiler_params=pltpu.CompilerParams(vmem_limit_bytes=56 * 1024 * 1024),
    )(*operands)


def beside(values, plane):
    mid = values[plane]
    total = values[plane + 1] + values[plane - 1]
    return mid, total + roll(mid, 1, 0) + roll(mid, -1, 0)


def sum_natural(values, plane):
    mid, total = beside(values, plane)
    return total + roll(mid, 1, 1) + roll(mid, -1, 1)


def sum_half(values, plane, onto_red):
    mid, total = beside(values, plane)
    odd = (iota(mid.shape, 0) + plane) % 2 == 1
    high = odd if onto_red else jnp.logical_not(odd)
    return total + mid + jnp.where(high, roll(mid, -1, 1), roll(mid, 1, 1))


def is_red(shape, plane):
    return (iota(shape, 0) + iota(shape, 1) + plane) % 2 == 0


def plane0(own, low, high, below, above, field, plane):
    if plane < H0:
        mid = low[field * H0 + plane]
    elif plane < H0 + 32:
        mid = own[plane - H0]
    else:
        mid = high[field * H0 + plane - H0 - 32]
    return jnp.concatenate([below[field * X0 + plane], mid, above[field * X0 + plane]], axis=0)


def pack_z0(f, s, low, high, below, above, to_high, to_low):
    lane = iota((Y0, LANES), 1)
    for group in range(-(-X0 // GROUP0)):
        up = jnp.zeros((Y0, LANES), F32)
        down = jnp.zeros((Y0, LANES), F32)
        for k in range(min(GROUP0, X0 - group * GROUP0)):
            plane = group * GROUP0 + k
            for field, own in enumerate((f, s)):
                value = plane0(own, low, high, below, above, field, plane)
                at = 16 * k + 8 * field
                here = jnp.logical_and(lane >= at, lane < at + 8)
                up = jnp.where(here, roll(value, at - 120, 1), up)
                down = jnp.where(here, roll(value, at, 1), down)
        to_high[group] = up
        to_low[group] = down


def down0(f, s, low, high, below, above, from_low, from_high, fr, fb, ir, ib, vb, fs1, red, sums):
    shape = (Y0, LANES)
    k_at = iota(shape, 1) - OWN
    for plane in range(X0):
        group, k = divmod(plane, GROUP0)
        odd = (iota(shape, 0) + plane) % 2
        for field, own in enumerate((f, s)):
            value = plane0(own, low, high, below, above, field, plane)
            at = 16 * k + 8 * field
            for colour in (0, 1):
                z = 2 * k_at + (odd if colour == 0 else 1 - odd)
                inner = pick(value, jnp.clip(z, 0, 127))
                left = pick(from_low[group], jnp.clip(z + 8 + at, 0, 127))
                right = pick(from_high[group], jnp.clip(z - 128 + at, 0, 127))
                result = jnp.where(k_at < 0, left, jnp.where(k_at > 63, right, inner))
                if field == 0:
                    (fr, fb)[colour][plane] = result
                else:
                    (ir, ib)[colour][plane] = result
    lane = iota((16, LANES), 1)

    def screen1(i):
        plane = 2 * i + H0
        sums[0] = ir[plane] + ib[plane] + ir[plane + 1] + ib[plane + 1]
        total = sums[0, pl.ds(8, 16, stride=2), :] + sums[0, pl.ds(9, 16, stride=2), :]
        fs1[i] = roll(0.5 * total, 64 - OWN, 1)

    loop(0, 16, screen1)

    def invert(p):
        ir[p] = 1.0 / (6.0 + ir[p])
        ib[p] = 1.0 / (6.0 + ib[p])
        red[p] = fr[p] * ir[p]

    loop(0, X0, invert)

    def black(p):
        vb[p] = (fb[p] + sum_half(red, p, False)) * ib[p]

    loop(1, X0 - 1, black)
    vb[0] = jnp.zeros(shape, F32)
    vb[X0 - 1] = jnp.zeros(shape, F32)

    def restrict(i):
        plane = 2 * i + H0
        sums[0] = sum_half(vb, plane, True) + sum_half(vb, plane + 1, True)
        total = sums[0, pl.ds(8, 16, stride=2), :] + sums[0, pl.ds(9, 16, stride=2), :]
        fs1[i] = jnp.where(lane < 64, roll(0.5 * total, -OWN, 1), fs1[i])

    loop(0, 16, restrict)


def pack_z1(own, below, above, to_high, to_low):
    lane = iota((Y1, LANES), 1)
    for group in range(X1 // GROUP1):
        up = jnp.zeros((Y1, LANES), F32)
        down = jnp.zeros((Y1, LANES), F32)
        for k in range(GROUP1):
            plane = group * GROUP1 + k
            value = jnp.concatenate([below[plane], own[plane], above[plane]], axis=0)
            for field in (0, 1):
                at = 28 * k + 14 * field
                here = jnp.logical_and(lane >= at, lane < at + 14)
                up = jnp.where(here, roll(value, at - 64 * field - 50, 1), up)
                down = jnp.where(here, roll(value, at - 64 * field, 1), down)
        to_high[group] = up
        to_low[group] = down


def unpack1(own, below, above, from_low, from_high, field, plane):
    lane = iota((Y1, LANES), 1)
    group, k = divmod(plane, GROUP1)
    at = 28 * k + 14 * field
    value = jnp.concatenate([below[plane], own[plane], above[plane]], axis=0)
    value = roll(value, OWN - 64 * field, 1)
    left = roll(from_low[group], OWN - 14 - at, 1)
    right = roll(from_high[group], OWN + 64 - at, 1)
    return jnp.where(lane < OWN, left, jnp.where(lane < OWN + 64, value, right))


def pair_index(rows):
    return jnp.clip(2 * iota((rows, LANES), 1) - OWN, 0, 127)


def spread_index(rows):
    return (iota((rows, LANES), 1) - OWN) // 2 + OWN


def sweep_zero(source, inverse, values, count, shape):
    def red(p):
        values[p] = jnp.where(is_red(shape, p), source[p] * inverse[p], 0.0)

    def black(p):
        fresh = (source[p] + sum_natural(values, p)) * inverse[p]
        values[p] = jnp.where(is_red(shape, p), values[p], fresh)

    loop(0, count, red)
    loop(1, count - 1, black)


def down12(f1, i1, v1, f2, i2, v2, sums):
    sweep_zero(f1, i1, v1, X1, (Y1, LANES))
    f2[0] = jnp.zeros((Y2, LANES), F32)
    f2[X2 - 1] = jnp.zeros((Y2, LANES), F32)

    def restrict(i):
        plane = 2 * i + 2
        total = jnp.zeros((Y1, LANES), F32)
        for p in (plane, plane + 1):
            total += jnp.where(is_red((Y1, LANES), p), sum_natural(v1, p), 0.0)
        f2[i] = coarse12(total, sums)

    loop(0, X2, restrict)
    sweep_zero(f2, i2, v2, X2, (Y2, LANES))


def coarse12(total, sums):
    sums[0] = total
    pairs = sums[0, pl.ds(0, Y2, stride=2), :] + sums[0, pl.ds(1, Y2, stride=2), :]
    pairs = pairs + roll(pairs, -1, 1)
    return 0.5 * pick(pairs, pair_index(Y2))


def coarse23(total, sums, x3):
    sums[0, 0:Y2, :] = total
    pairs = sums[0, pl.ds(8, 8, stride=2), :] + sums[0, pl.ds(9, 8, stride=2), :]
    pairs = pairs + roll(pairs, -1, 1)
    lane = iota((8, LANES), 1)
    spread = pick(pairs, OWN + 2 * (lane % 16))
    here = lane // 16 == (x3 % 2) * 4 + iota((8, LANES), 0)
    here = jnp.logical_and(here, iota((8, LANES), 0) < 4)
    return 0.5 * jnp.sum(jnp.where(here, spread, 0.0), axis=0, keepdims=True)


def source3(v2, sums):
    rows = []
    for x3 in range(4):
        plane = 2 * x3 + H2
        total = jnp.zeros((Y2, LANES), F32)
        for p in (plane, plane + 1):
            total += jnp.where(is_red((Y2, LANES), p), sum_natural(v2, p), 0.0)
        rows.append(coarse23(total, sums, x3))
    return [rows[0] + rows[1], rows[2] + rows[3]]


def down12_first(own, below, above, from_low, from_high, f1, i1, v1, f2, i2, v2, message, sums):
    for plane in range(X1):
        f1[plane] = unpack1(own, below, above, from_low, from_high, 0, plane)
        i1[plane] = unpack1(own, below, above, from_low, from_high, 1, plane)

    def screen2(i):
        i2[i] = coarse12(i1[2 * i + 2] + i1[2 * i + 3], sums)

    loop(0, X2, screen2)
    rows = []
    for x3 in range(4):
        plane = 2 * x3 + H2
        rows.append(coarse23(i2[plane] + i2[plane + 1], sums, x3))

    def invert1(p):
        i1[p] = 1.0 / (6.0 + i1[p])

    def invert2(p):
        i2[p] = 1.0 / (6.0 + i2[p])

    loop(0, X1, invert1)
    loop(0, X2, invert2)
    down12(f1, i1, v1, f2, i2, v2, sums)
    tile = jnp.concatenate(source3(v2, sums) + [rows[0] + rows[1], rows[2] + rows[3]], axis=0)
    tile = jnp.concatenate([tile, tile], axis=0)
    for i in range(64):
        message[8 * i : 8 * i + 8, :] = tile


def down12_next(own, below, above, from_low, from_high, i1, i2, f1, v1, f2, v2, message, sums):
    for plane in range(X1):
        f1[plane] = unpack1(own, below, above, from_low, from_high, 0, plane)
    down12(f1, i1, v1, f2, i2, v2, sums)
    tile = jnp.concatenate(source3(v2, sums) * 4, axis=0)
    for i in range(32):
        message[8 * i : 8 * i + 8, :] = tile


def unpack3(message, rows, first, into):
    sub, lane = iota((8, LANES), 0), iota((8, LANES), 1)
    for gx in range(4):
        for gy in range(4):
            for half in range(2):
                start = (gx * 4 + gy) * 8 * rows + first + half
                value = message[pl.ds(start, 8, stride=rows), :]
                for k in (1, 2, 4):
                    sub_high = (sub // k) % 2 == 1
                    lane_high = (lane // (16 * k)) % 2 == 1
                    from_below = roll(roll(value, -k, 0), 16 * k, 1)
                    from_above = roll(roll(value, k, 0), -16 * k, 1)
                    value = jnp.where(
                        sub_high == lane_high, value, jnp.where(sub_high, from_above, from_below)
                    )
                for x in range(2):
                    into[gx * 4 + 2 * half + x, gy * 4 : gy * 4 + 4, :] = value[4 * x : 4 * x + 4, :]


def turn(value, shift, axis):
    if axis == 0:
        return jnp.concatenate([value[-shift:], value[:-shift]], axis=0)
    return roll(value, shift, axis)


def sum_whole(value):
    total = turn(value, 1, 0) + turn(value, -1, 0)
    total = total + turn(value, 1, 1) + turn(value, -1, 1)
    return total + turn(value, 1, 2) + turn(value, -1, 2)


def red_whole(shape):
    return (iota(shape, 0) + iota(shape, 1) + iota(shape, 2)) % 2 == 0


def pick3(value, index):
    flat = value.reshape(-1, LANES)
    return pick(flat, jnp.broadcast_to(index, flat.shape)).reshape(value.shape)


def coarse34(value, wide):
    wide[...] = value.reshape(8, 2, 16, LANES).sum(axis=1)
    pairs = wide[:, pl.ds(0, 8, stride=2), :] + wide[:, pl.ds(1, 8, stride=2), :]
    pairs = pairs + roll(pairs, -1, 2)
    return 0.5 * pick3(pairs, 2 * (iota((1, LANES), 1) % 64))


def coarse_solve(f3, i3, i4, inverse, e3, wide):
    red3, red4 = red_whole((16, 16, LANES)), red_whole((8, 8, LANES))
    v3 = jnp.where(red3, f3 * i3, 0.0)
    v3 = jnp.where(red3, v3, (f3 + sum_whole(v3)) * i3)
    f4 = coarse34(jnp.where(red3, sum_whole(v3), 0.0), wide)
    v4 = jnp.where(red4, f4 * i4, 0.0)
    v4 = jnp.where(red4, v4, (f4 + sum_whole(v4)) * i4)
    r4 = jnp.where(red4, sum_whole(v4), 0.0).reshape(4, 2, 8, LANES).sum(axis=1)
    sub, lane = iota((8, LANES), 0), iota((8, LANES), 1)
    rows = []
    for x5 in range(4):
        pairs = r4[x5] + roll(r4[x5], -1, 1)
        spread = jnp.where(sub // 2 == lane // 32, pick(pairs, 2 * (lane % 32)), 0.0)
        rows.append(0.5 * jnp.sum(spread, axis=0, keepdims=True))
    vector = jnp.broadcast_to(jnp.concatenate(rows, axis=1), (8, 512))
    answer = lax.dot_general(
        vector,
        inverse[...],
        (((1,), (1,)), ((), ())),
        precision=lax.Precision.HIGHEST,
        preferred_element_type=F32,
    )
    planes = []
    for x5 in range(4):
        part = pick(answer[:, 128 * x5 : 128 * x5 + 128], (sub // 2) * 32 + (lane % 64) // 2)
        planes += [part[None], part[None]]
    w4 = v4 + jnp.concatenate(planes, axis=0)
    w4 = jnp.where(red4, (f4 + sum_whole(w4)) * i4, w4)
    e4 = jnp.where(red4, w4, (f4 + sum_whole(w4)) * i4)
    e4 = pick3(e4, iota((1, LANES), 1) // 2)
    wide[:, pl.ds(0, 8, stride=2), :] = e4
    wide[:, pl.ds(1, 8, stride=2), :] = e4
    spread = jnp.broadcast_to(wide[...][:, None], (8, 2, 16, LANES)).reshape(16, 16, LANES)
    w3 = v3 + spread
    w3 = jnp.where(red3, (f3 + sum_whole(w3)) * i3, w3)
    e3[...] = jnp.where(red3, w3, (f3 + sum_whole(w3)) * i3)


def sweep_up(source, inverse, values, first, last, shape):
    def red(p):
        fresh = (source[p] + sum_natural(values, p)) * inverse[p]
        values[p] = jnp.where(is_red(shape, p), fresh, values[p])

    def black(p):
        fresh = (source[p] + sum_natural(values, p)) * inverse[p]
        values[p] = jnp.where(is_red(shape, p), values[p], fresh)

    loop(first, last + 1, red)
    loop(first + 1, last, black)


def up21(place, e3, f2, i2, v2, f1, i1, v1, e2, e1, tall):
    shift_y = lax.rem(20 - 4 * place[1], 16)
    shift_z = lax.rem(160 - 16 * place[2], 128)

    def from3(i):
        value = e3[lax.rem(4 * place[0] + i + 13, 16)]
        value = pltpu.roll(pltpu.roll(value, shift_y, 0), shift_z, 1)
        value = pick(value, spread_index(16))[:12]
        tall[0, pl.ds(0, 12, stride=2), :] = value
        tall[0, pl.ds(1, 12, stride=2), :] = value
        value = tall[0, 0:Y2, :]
        e2[2 * i] = v2[2 * i] + value
        e2[2 * i + 1] = v2[2 * i + 1] + value

    loop(0, X2 // 2, from3, 1)
    sweep_up(f2, i2, e2, 1, X2 - 2, (Y2, LANES))

    def from2(i):
        value = pick(e2[i], spread_index(Y2))
        tall[0, pl.ds(0, Y2, stride=2), :] = value
        tall[0, pl.ds(1, Y2, stride=2), :] = value
        value = tall[0]
        e1[2 * i + 2] = v1[2 * i + 2] + value
        e1[2 * i + 3] = v1[2 * i + 3] + value

    loop(3, 17, from2, 1)
    sweep_up(f1, i1, e1, 9, 34, (Y1, LANES))


def add0(e1, b, w, tall):
    def from1(i):
        value = e1[i + 10, pl.ds(12, 24), :]
        tall[0, pl.ds(0, 24, stride=2), :] = value
        tall[0, pl.ds(1, 24, stride=2), :] = value
        value = tall[0]
        w[2 * i] = b[2 * i] + value
        w[2 * i + 1] = b[2 * i + 1] + value

    loop(0, X0 // 2, from1, 1)


def middle(
    message, place, inverse, f2, i2, v2, f1, i1, v1, fr, fb, ir, ib, vb,
    i3, i4, rnew, bnew, own1, norm,
    f3, e3, wide, tall, e2, e1, w, r,
):
    unpack3(message, 4, 0, f3)
    unpack3(message, 4, 2, e3)
    screen3 = e3[...]
    screen4 = coarse34(screen3, wide)
    i3[...] = 1.0 / (6.0 + screen3)
    i4[...] = 1.0 / (6.0 + screen4)
    coarse_solve(f3[...], i3[...], i4[...], inverse, e3, wide)
    up21(place, e3, f2, i2, v2, f1, i1, v1, e2, e1, tall)
    add0(e1, vb, w, tall)

    def red_up(p):
        r[p] = (fr[p] + sum_half(w, p, True)) * ir[p]

    loop(2, X0 - 2, red_up)

    def black_up(p):
        w[p] = (fb[p] + sum_half(r, p, False)) * ib[p]

    loop(3, X0 - 3, black_up)

    def red_down(p):
        rnew[p] = (fr[p] + sum_half(w, p, True)) * ir[p]

    loop(4, X0 - 4, red_down)

    def squares(p, total):
        part = (rnew[p] - r[p])[8:40] / ir[p, 8:40, :]
        return total + part * part

    total = lax.fori_loop(H0, H0 + 32, squares, jnp.zeros((32, LANES), F32), unroll=2)
    norm[...] = jnp.sum(total.reshape(4, 8, LANES), axis=0)

    def black_down(p):
        fresh = (fb[p] + sum_half(rnew, p, False)) * ib[p]
        bnew[p] = fresh
        r[p] = fresh - w[p]

    loop(5, X0 - 5, black_down)

    def restrict(i):
        plane = 2 * i + H0
        tall[0] = sum_half(r, plane, True) + sum_half(r, plane + 1, True)
        total = tall[0, pl.ds(8, 16, stride=2), :] + tall[0, pl.ds(9, 16, stride=2), :]
        own1[i] = roll(0.5 * total, -OWN, 1)

    loop(0, 16, restrict)


def final(
    message, place, inverse, f2, i2, v2, f1, i1, v1, fr, fb, ir, ib, b, i3, i4, norm,
    field, sums,
    f3, e3, wide, tall, e2, e1, w, r, last,
):
    unpack3(message, 2, 0, f3)
    coarse_solve(f3[...], i3[...], i4[...], inverse, e3, wide)
    up21(place, e3, f2, i2, v2, f1, i1, v1, e2, e1, tall)
    add0(e1, b, w, tall)

    def red_up(p):
        r[p] = (fr[p] + sum_half(w, p, True)) * ir[p]

    loop(6, X0 - 6, red_up)

    def black_up(p):
        fresh = (fb[p] + sum_half(r, p, False)) * ib[p]
        last[p] = fresh
        w[p] = fresh - w[p]

    loop(7, X0 - 7, black_up)

    def finish(p, total):
        part = sum_half(w, p, True)[8:40]
        lane = iota((32, LANES), 1)
        index = OWN + lane // 2
        reds = pick(r[p, 8:40, :], index)
        blacks = pick(last[p, 8:40, :], index)
        here = (iota((32, LANES), 0) + lane + p) % 2 == 0
        field[p - H0] = jnp.where(here, reds, blacks)
        return total + part * part

    total = lax.fori_loop(H0, H0 + 32, finish, jnp.zeros((32, LANES), F32), unroll=2)
    after = jnp.sum(total, axis=0, keepdims=True)
    before = jnp.sum(norm[...], axis=0, keepdims=True)
    low = iota((1, LANES), 1) < 64
    both = jnp.where(low, roll(before, -OWN, 1), roll(after, 64 - OWN, 1))
    for i in range(16):
        sums[8 * i : 8 * i + 8, :] = jnp.broadcast_to(both, (8, LANES))


def exchange(to_high, to_low, axis):
    count = lax.axis_size(axis)
    up = [(i, (i + 1) % count) for i in range(count)]
    down = [(j, i) for i, j in up]
    return lax.ppermute(to_high, axis, up), lax.ppermute(to_low, axis, down)


def exchange1(own):
    low, high = exchange(own[16 - H1 :], own[:H1], "gx")
    own = jnp.concatenate([low, own, high], axis=0)
    below, above = exchange(own, own, "gy")
    groups = X1 // GROUP1
    to_high, to_low = call(pack_z1, [(groups, Y1, LANES)] * 2, own, below, above)
    from_low, from_high = exchange(to_high, to_low, "gz")
    return own, below, above, from_low, from_high


def local(f, s, coarse_inverse):
    inverse = lax.all_gather(coarse_inverse, AXES, axis=0, tiled=True)
    place = jnp.stack([lax.axis_index(axis) for axis in AXES]).astype(jnp.int32)
    low, high = exchange(
        jnp.concatenate([f[32 - H0 :], s[32 - H0 :]], axis=0),
        jnp.concatenate([f[:H0], s[:H0]], axis=0),
        "gx",
    )

    def rows(cut):
        parts = [low[:H0], f, high[:H0], low[H0:], s, high[H0:]]
        return jnp.concatenate([part[:, cut] for part in parts], axis=0)

    below, above = exchange(rows(slice(24, 32)), rows(slice(0, 8)), "gy")
    groups = -(-X0 // GROUP0)
    pieces = (f, s, low, high, below, above)
    to_high, to_low = call(pack_z0, [(groups, Y0, LANES)] * 2, *pieces)
    from_low, from_high = exchange(to_high, to_low, "gz")
    level0, level1, level2 = (X0, Y0, LANES), (X1, Y1, LANES), (X2, Y2, LANES)
    line = (1, Y0, LANES)
    fr, fb, ir, ib, vb, own1 = call(
        down0, [level0] * 5 + [(16, 16, LANES)], *pieces, from_low, from_high, scratch=[level0, line]
    )
    f1, i1, v1, f2, i2, v2, message = call(
        down12_first,
        [level1] * 3 + [level2] * 3 + [(512, LANES)],
        *exchange1(own1),
        scratch=[line],
    )
    message = lax.all_to_all(message, AXES, 0, 0, tiled=True)
    whole = (16, 16, LANES)
    work = [whole, whole, (8, 16, LANES), line, level2, level1, level0, level0]
    i3, i4, rnew, bnew, own1, norm = call(
        middle,
        [whole, (8, 8, LANES), level0, level0, (16, 16, LANES), (8, LANES)],
        message, place, inverse, f2, i2, v2, f1, i1, v1, fr, fb, ir, ib, vb,
        scratch=work,
    )
    f1, v1, f2, v2, message = call(
        down12_next,
        [level1] * 2 + [level2] * 2 + [(256, LANES)],
        *exchange1(own1),
        i1,
        i2,
        scratch=[line],
    )
    message = lax.all_to_all(message, AXES, 0, 0, tiled=True)
    field, sums = call(
        final,
        [(32, 32, LANES), (128, LANES)],
        message, place, inverse, f2, i2, v2, f1, i1, v1, fr, fb, ir, ib, bnew, i3, i4, norm,
        scratch=work + [level0],
    )
    sums = lax.all_to_all(sums, AXES, 0, 0, tiled=True)
    squares = jnp.sum(sums.reshape(128, 2, 64), axis=(0, 2))
    return field, jnp.sqrt(squares / CELLS)


def solution(mesh):
    return jax.shard_map(
        local,
        mesh=mesh,
        in_specs=(P("gx", "gy", "gz"), P("gx", "gy", "gz"), P(("gx", "gy", "gz"), None)),
        out_specs=(P("gx", "gy", "gz"), P()),
        check_vma=False,
    )
```

```python
import jax
import jax.numpy as jnp
import numpy as np
from jax import lax
from jax.experimental import pallas as pl
from jax.experimental.pallas import tpu as pltpu
from jax.sharding import PartitionSpec as P

AXES = ("gx", "gy", "gz")
F32 = jnp.float32
LANES = 128
OWN = 32
H0 = 8
X0, Y0 = 48, 48
H1 = 14
X1, Y1 = 44, 48
H2 = 6
X2, Y2 = 20, 24
GROUP0 = 8
GROUP1 = 4
CELLS = 16777216.0


def iota(shape, dim):
    return lax.broadcasted_iota(jnp.int32, shape, dim)


def roll(value, shift, axis):
    return pltpu.roll(value, shift % value.shape[axis], axis)


def pick(value, index):
    return jnp.take_along_axis(value, index, axis=1, mode="promise_in_bounds")


def loop(start, stop, body, unroll=2):
    def step(index, carry):
        body(index)
        return carry

    lax.fori_loop(start, stop, step, 0, unroll=unroll)


def call(body, outs, *operands, scratch=()):
    specs = [
        pl.BlockSpec(memory_space=pltpu.SMEM if operand.dtype == jnp.int32 else pltpu.VMEM)
        for operand in operands
    ]
    return pl.pallas_call(
        body,
        out_shape=[jax.ShapeDtypeStruct(shape, F32) for shape in outs],
        in_specs=specs,
        out_specs=[pl.BlockSpec(memory_space=pltpu.VMEM)] * len(outs),
        scratch_shapes=[pltpu.VMEM(shape, F32) for shape in scratch],
        compiler_params=pltpu.CompilerParams(vmem_limit_bytes=32 * 1024 * 1024),
    )(*operands)


def lower_matrices():
    matrices = np.zeros((GROUP0, 256, 256), np.float32)
    for k in range(GROUP0):
        for z in range(-8, 136):
            if 0 <= z < 128:
                row = z
            elif z < 0:
                row = 128 + (16 * k + z) % 128
            else:
                row = 128 + 16 * k + z - 128
            matrices[k, row, 128 * (z % 2) + OWN + z // 2] = 1.0
    return matrices


def upper_matrix():
    matrix = np.zeros((256, 128), np.float32)
    for z in range(128):
        matrix[128 * (z % 2) + OWN + z // 2, z] = 1.0
    return matrix


def halo_matrices1():
    matrices = np.zeros((GROUP1, 384, 256), np.float32)
    for k in range(GROUP1):
        for half in (0, 1):
            for z in range(-H1, 64 + H1):
                if 0 <= z < 64:
                    row = (OWN + 64 * half + z) % 128
                elif z < 0:
                    row = 128 + 64 * half + 14 * k + z + H1
                else:
                    row = 256 + 64 * half + 14 * k + z - 64
                matrices[k, row, 128 * half + OWN + z] = 1.0
    return matrices


def thirds(value):
    high = value.astype(jnp.bfloat16)
    rest = value - high.astype(F32)
    mid = rest.astype(jnp.bfloat16)
    return (rest - mid.astype(F32)).astype(jnp.bfloat16), mid, high


def move(pieces, matrix):
    total = None
    for parts in zip(*pieces):
        left = parts[0] if len(parts) == 1 else jnp.concatenate(parts, axis=1)
        term = jnp.dot(left, matrix, preferred_element_type=F32)
        total = term if total is None else total + term
    return total


def plane_pairs(first, last, body, unroll=4):
    def both(i):
        body(2 * i, 0)
        body(2 * i + 1, 1)

    loop(first // 2, last // 2, both, unroll)


def sum0(values, plane, parity, q, onto_red):
    mid, other = values[plane, q], values[plane, 1 - q]
    total = values[plane + 1, q] + values[plane - 1, q] + mid
    total = total + other + roll(other, 1 if q == 0 else -1, 0)
    high = ((parity + q) % 2 == 1) == onto_red
    return total + roll(mid, -1 if high else 1, 1)


def even_lanes(shape, parity):
    return (iota(shape, 1) + parity) % 2 == 0


def sum1(values, plane, parity, onto_red):
    mid = values[plane]
    total = values[plane + 1] + values[plane - 1] + mid
    total = total + roll(mid, 1, 1) + roll(mid, -1, 1)
    less, more = roll(mid, 1, 0), roll(mid, -1, 0)
    first, second = (less, more) if onto_red else (more, less)
    return total + jnp.where(even_lanes(mid.shape, parity), first, second)


def sum2(values, plane):
    mid = values[plane]
    total = values[plane + 1] + values[plane - 1]
    total = total + roll(mid, 1, 0) + roll(mid, -1, 0)
    return total + roll(mid, 1, 1) + roll(mid, -1, 1)


def is_red(shape, plane):
    return (iota(shape, 0) + iota(shape, 1) + plane) % 2 == 0


def pack_z0(f, s, low, high, below, above, split, message, rows):
    block = (iota((Y0, LANES), 1) + 8) % LANES // 16
    for group in range(2 * X0 // GROUP0):
        packed = jnp.zeros((Y0, LANES), F32)
        for k in range(GROUP0):
            item = group * GROUP0 + k
            field, plane = divmod(item, X0)
            own = (f, s)[field]
            slot = item % 16
            rows[slot, 0:8, :] = below[item]
            if plane < H0:
                rows[slot, 8:40, :] = low[field * H0 + plane]
            elif plane < H0 + 32:
                rows[slot, 8:40, :] = own[plane - H0]
            else:
                rows[slot, 8:40, :] = high[field * H0 + plane - H0 - 32]
            rows[slot, 40:48, :] = above[item]
            even = rows[slot, pl.ds(0, 24, stride=2), :]
            odd = rows[slot, pl.ds(1, 24, stride=2), :]
            value = jnp.concatenate([even, odd], axis=0)
            split[item] = value
            packed = jnp.where(block == k, roll(value, 16 * k, 1), packed)
        message[group] = packed


def down0(split, from_low, from_high, matrices, fr, fb, ir, ib, vb, own1, red, screen):
    lane = iota((Y0, LANES), 1)
    groups = 2 * X0 // GROUP0
    merged = [
        jnp.where(lane // 8 % 2 == 1, from_low[group], from_high[group]) for group in range(groups)
    ]
    merged = thirds(jnp.concatenate(merged, axis=0))
    for k in range(GROUP0):
        own = [split[group * GROUP0 + k] for group in range(groups)]
        result = move([thirds(jnp.concatenate(own, axis=0)), merged], matrices[k])
        for group in range(groups):
            field, plane = divmod(group * GROUP0 + k, X0)
            part = result[Y0 * group : Y0 * group + Y0]
            even, odd = part[:, :LANES], part[:, LANES:]
            if field == 1:
                screen[plane] = even[:24] + odd[:24] + even[24:] + odd[24:]
            for q in (0, 1):
                reds, blacks = (even, odd) if (k + q) % 2 == 0 else (odd, even)
                reds, blacks = reds[24 * q : 24 * q + 24], blacks[24 * q : 24 * q + 24]
                if field == 0:
                    fr[plane, q] = reds
                    fb[plane, q] = blacks
                else:
                    ir[plane, q] = 1.0 / (6.0 + reds)
                    ib[plane, q] = 1.0 / (6.0 + blacks)

    def first(p):
        red[p] = fr[p] * ir[p]

    loop(0, X0, first, 4)

    def black(p, parity):
        for q in (0, 1):
            vb[p, q] = (fb[p, q] + sum0(red, p, parity, q, False)) * ib[p, q]

    black(1, 1)
    plane_pairs(2, X0 - 2, black)
    black(X0 - 2, 0)

    def restrict(i):
        plane = 2 * i + H0
        source = 0.5 * below_sum(vb, plane)
        own = (iota((16, LANES), 1) + 128 - OWN) % LANES < 64
        screens = 0.5 * (screen[plane] + screen[plane + 1])[4:20]
        own1[i] = jnp.where(own, source[4:20], roll(screens, 64, 1))

    loop(0, 16, restrict)


def below_sum(values, plane):
    total = sum0(values, plane, 0, 0, True) + sum0(values, plane, 0, 1, True)
    total = total + sum0(values, plane + 1, 1, 0, True)
    return total + sum0(values, plane + 1, 1, 1, True)


def pack_z1(own, below, above, coloured, to_high, to_low):
    block = iota((24, LANES), 1) % 64 // 14
    for group in range(own.shape[0] // GROUP1):
        up = [jnp.zeros((24, LANES), F32)] * 2
        down = [jnp.zeros((24, LANES), F32)] * 2
        for k in range(GROUP1):
            item = group * GROUP1 + k
            even, odd = [
                jnp.concatenate([ref[item, pl.ds(q, 8, stride=2), :] for ref in (below, own, above)], axis=0)
                for q in (0, 1)
            ]
            here = even_lanes((24, LANES), item)
            for colour in (0, 1):
                first, second = (even, odd) if colour == 0 else (odd, even)
                value = jnp.where(here, first, second)
                coloured[item, colour] = value
                up[colour] = jnp.where(block == k, roll(value, 14 * k - 82, 1), up[colour])
                down[colour] = jnp.where(block == k, roll(value, 14 * k - 32, 1), down[colour])
        for colour in (0, 1):
            to_high[group, colour] = up[colour]
            to_low[group, colour] = down[colour]


def unpack1(coloured, from_low, from_high, matrices, store):
    items = coloured.shape[0]
    rows = items // GROUP1 * 48
    halos = [thirds(ref[...].reshape(rows, LANES)) for ref in (from_low, from_high)]
    for k in range(GROUP1):
        own = [coloured[item, colour] for item in range(k, items, GROUP1) for colour in (0, 1)]
        result = move([thirds(jnp.concatenate(own, axis=0)), *halos], matrices[k])
        for at in range(items // GROUP1 * 2):
            part = result[24 * at : 24 * at + 24]
            store(at // 2 * GROUP1 + k, at % 2, (part[:, :LANES], part[:, LANES:]))


def pair_index(rows):
    return jnp.clip(2 * iota((rows, LANES), 1) - OWN, 0, 127)


def spread_index(rows):
    return (iota((rows, LANES), 1) - OWN) // 2 + OWN


def coarse12(total):
    pairs = total + roll(total, -1, 1)
    return 0.5 * pick(pairs, pair_index(Y2))


def down12(f1, i1, b1, f2, i2, v2, red):
    def first(p):
        red[p] = f1[p, 0] * i1[p, 0]

    loop(0, X1, first, 4)

    def black(p, parity):
        b1[p] = (f1[p, 1] + sum1(red, p, parity, False)) * i1[p, 1]

    black(1, 1)
    plane_pairs(2, X1 - 2, black)
    black(X1 - 2, 0)

    def restrict(i):
        plane = 2 * i + 2
        f2[i] = coarse12(sum1(b1, plane, 0, True) + sum1(b1, plane + 1, 1, True))

    loop(0, X2, restrict, 4)

    def red2(p):
        v2[p] = jnp.where(is_red((Y2, LANES), p), f2[p] * i2[p], 0.0)

    def black2(p):
        fresh = (f2[p] + sum2(v2, p)) * i2[p]
        v2[p] = jnp.where(is_red((Y2, LANES), p), v2[p], fresh)

    loop(0, X2, red2, 4)
    loop(1, X2 - 1, black2, 3)


def coarse23(total, sums, x3):
    sums[x3] = total
    pairs = sums[x3, pl.ds(8, 8, stride=2), :] + sums[x3, pl.ds(9, 8, stride=2), :]
    pairs = pairs + roll(pairs, -1, 1)
    lane = iota((8, LANES), 1)
    spread = pick(pairs, OWN + 2 * (lane % 16))
    here = lane // 16 == (x3 % 2) * 4 + iota((8, LANES), 0)
    here = jnp.logical_and(here, iota((8, LANES), 0) < 4)
    return 0.5 * jnp.sum(jnp.where(here, spread, 0.0), axis=0, keepdims=True)


def source3(v2, sums):
    rows = []
    for x3 in range(4):
        plane = 2 * x3 + H2
        total = jnp.zeros((Y2, LANES), F32)
        for p in (plane, plane + 1):
            total += jnp.where(is_red((Y2, LANES), p), sum2(v2, p), 0.0)
        rows.append(coarse23(total, sums, x3))
    return [rows[0] + rows[1], rows[2] + rows[3]]


def down12_first(coloured, from_low, from_high, matrices, f1, i1, b1, f2, i2, v2, message, red, sums):
    def store(plane, colour, halves):
        f1[plane, colour], i1[plane, colour] = halves

    unpack1(coloured, from_low, from_high, matrices, store)

    def screen2(i):
        plane = 2 * i + 2
        total = i1[plane, 0] + i1[plane, 1] + i1[plane + 1, 0] + i1[plane + 1, 1]
        i2[i] = coarse12(total)

    loop(0, X2, screen2, 4)
    rows = []
    for x3 in range(4):
        plane = 2 * x3 + H2
        rows.append(coarse23(i2[plane] + i2[plane + 1], sums, x3))

    def invert1(p):
        i1[p] = 1.0 / (6.0 + i1[p])

    def invert2(p):
        i2[p] = 1.0 / (6.0 + i2[p])

    loop(0, X1, invert1, 4)
    loop(0, X2, invert2, 4)
    down12(f1, i1, b1, f2, i2, v2, red)
    tile = jnp.concatenate(source3(v2, sums) + [rows[0] + rows[1], rows[2] + rows[3]], axis=0)
    tile = jnp.concatenate([tile, tile], axis=0)
    for i in range(64):
        message[8 * i : 8 * i + 8, :] = tile


def down12_next(coloured, from_low, from_high, matrices, i1, i2, f1, b1, f2, v2, message, red, sums):
    def store(item, colour, halves):
        block, i = divmod(item, 8)
        for half in (0, 1):
            plane = H1 + 16 * (block - 1) + 8 * half + i
            if 0 <= plane < X1:
                f1[plane, colour] = halves[half]

    unpack1(coloured, from_low, from_high, matrices, store)
    down12(f1, i1, b1, f2, i2, v2, red)
    tile = jnp.concatenate(source3(v2, sums) * 4, axis=0)
    for i in range(32):
        message[8 * i : 8 * i + 8, :] = tile


def unpack3(message, rows, first, into):
    sub, lane = iota((8, LANES), 0), iota((8, LANES), 1)
    for gx in range(4):
        for gy in range(4):
            for half in range(2):
                start = (gx * 4 + gy) * 8 * rows + first + half
                value = message[pl.ds(start, 8, stride=rows), :]
                for k in (1, 2, 4):
                    sub_high = (sub // k) % 2 == 1
                    lane_high = (lane // (16 * k)) % 2 == 1
                    from_below = roll(roll(value, -k, 0), 16 * k, 1)
                    from_above = roll(roll(value, k, 0), -16 * k, 1)
                    value = jnp.where(
                        sub_high == lane_high, value, jnp.where(sub_high, from_above, from_below)
                    )
                for x in range(2):
                    into[gx * 4 + 2 * half + x, gy * 4 : gy * 4 + 4, :] = value[4 * x : 4 * x + 4, :]


def turn(value, shift, axis):
    if axis == 0:
        return jnp.concatenate([value[-shift:], value[:-shift]], axis=0)
    return roll(value, shift, axis)


def sum_whole(value):
    total = turn(value, 1, 0) + turn(value, -1, 0)
    total = total + turn(value, 1, 1) + turn(value, -1, 1)
    return total + turn(value, 1, 2) + turn(value, -1, 2)


def red_whole(shape):
    return (iota(shape, 0) + iota(shape, 1) + iota(shape, 2)) % 2 == 0


def pick3(value, index):
    flat = value.reshape(-1, LANES)
    return pick(flat, jnp.broadcast_to(index, flat.shape)).reshape(value.shape)


def coarse34(value, wide):
    wide[...] = value.reshape(8, 2, 16, LANES).sum(axis=1)
    pairs = wide[:, pl.ds(0, 8, stride=2), :] + wide[:, pl.ds(1, 8, stride=2), :]
    pairs = pairs + roll(pairs, -1, 2)
    return 0.5 * pick3(pairs, 2 * (iota((1, LANES), 1) % 64))


def coarse_solve(f3, i3, i4, inverse, e3, wide):
    red3, red4 = red_whole((16, 16, LANES)), red_whole((8, 8, LANES))
    v3 = jnp.where(red3, f3 * i3, 0.0)
    v3 = jnp.where(red3, v3, (f3 + sum_whole(v3)) * i3)
    f4 = coarse34(jnp.where(red3, sum_whole(v3), 0.0), wide)
    v4 = jnp.where(red4, f4 * i4, 0.0)
    v4 = jnp.where(red4, v4, (f4 + sum_whole(v4)) * i4)
    r4 = jnp.where(red4, sum_whole(v4), 0.0).reshape(4, 2, 8, LANES).sum(axis=1)
    sub, lane = iota((8, LANES), 0), iota((8, LANES), 1)
    rows = []
    for x5 in range(4):
        pairs = r4[x5] + roll(r4[x5], -1, 1)
        spread = jnp.where(sub // 2 == lane // 32, pick(pairs, 2 * (lane % 32)), 0.0)
        rows.append(0.5 * jnp.sum(spread, axis=0, keepdims=True))
    vector = jnp.broadcast_to(jnp.concatenate(rows, axis=1), (8, 512))
    answer = lax.dot_general(
        vector,
        inverse[...],
        (((1,), (1,)), ((), ())),
        precision=lax.Precision.HIGHEST,
        preferred_element_type=F32,
    )
    planes = []
    for x5 in range(4):
        part = pick(answer[:, 128 * x5 : 128 * x5 + 128], (sub // 2) * 32 + (lane % 64) // 2)
        planes += [part[None], part[None]]
    w4 = v4 + jnp.concatenate(planes, axis=0)
    w4 = jnp.where(red4, (f4 + sum_whole(w4)) * i4, w4)
    e4 = jnp.where(red4, w4, (f4 + sum_whole(w4)) * i4)
    e4 = pick3(e4, iota((1, LANES), 1) // 2)
    wide[:, pl.ds(0, 8, stride=2), :] = e4
    wide[:, pl.ds(1, 8, stride=2), :] = e4
    spread = jnp.broadcast_to(wide[...][:, None], (8, 2, 16, LANES)).reshape(16, 16, LANES)
    w3 = v3 + spread
    w3 = jnp.where(red3, (f3 + sum_whole(w3)) * i3, w3)
    e3[...] = jnp.where(red3, w3, (f3 + sum_whole(w3)) * i3)


def up21(place, e3, f2, i2, v2, f1, i1, b1, e2, er, eb, tall):
    shift_y = lax.rem(20 - 4 * place[1], 16)
    shift_z = lax.rem(160 - 16 * place[2], 128)

    def from3(i):
        value = e3[lax.rem(4 * place[0] + i + 13, 16)]
        value = pltpu.roll(pltpu.roll(value, shift_y, 0), shift_z, 1)
        value = pick(value, spread_index(16))[:12]
        tall[i, pl.ds(0, 12, stride=2), :] = value
        tall[i, pl.ds(1, 12, stride=2), :] = value
        value = tall[i]
        e2[2 * i] = v2[2 * i] + value
        e2[2 * i + 1] = v2[2 * i + 1] + value

    loop(0, X2 // 2, from3, 5)

    def red2(p):
        fresh = (f2[p] + sum2(e2, p)) * i2[p]
        e2[p] = jnp.where(is_red((Y2, LANES), p), fresh, e2[p])

    def black2(p):
        fresh = (f2[p] + sum2(e2, p)) * i2[p]
        e2[p] = jnp.where(is_red((Y2, LANES), p), e2[p], fresh)

    loop(1, X2 - 1, red2, 3)
    loop(2, X2 - 2, black2, 4)

    def from2(i):
        value = pick(e2[i], spread_index(Y2))
        eb[2 * i + 2] = b1[2 * i + 2] + value
        eb[2 * i + 3] = b1[2 * i + 3] + value

    loop(3, 17, from2, 7)

    def red1(p, parity):
        er[p] = (f1[p, 0] + sum1(eb, p, parity, True)) * i1[p, 0]

    def black1(p, parity):
        eb[p] = (f1[p, 1] + sum1(er, p, parity, False)) * i1[p, 1]

    plane_pairs(8, 36, red1)
    plane_pairs(10, 34, black1)


def add0(er, eb, b, w, tall):
    def from1(i):
        reds, blacks = er[i + 10, 6:18], eb[i + 10, 6:18]
        here = (iota((12, LANES), 1) + i) % 2 == 0
        tall[i, pl.ds(0, 12, stride=2), :] = jnp.where(here, reds, blacks)
        tall[i, pl.ds(1, 12, stride=2), :] = jnp.where(here, blacks, reds)
        value = tall[i]
        for p in (2 * i, 2 * i + 1):
            for q in (0, 1):
                w[p, q] = b[p, q] + value

    loop(0, X0 // 2, from1, 4)


def own_sum(total):
    row, lane = iota((24, LANES), 0), iota((24, LANES), 1)
    own = jnp.logical_and((row + 20) % 24 < 16, (lane + 128 - OWN) % LANES < 64)
    return jnp.sum(jnp.where(own, total, 0.0), axis=0, keepdims=True)


def sum_over(body):
    def step(i, total):
        return total + body(2 * i, 0) + body(2 * i + 1, 1)

    return lax.fori_loop(H0 // 2, H0 // 2 + 16, step, jnp.zeros((24, LANES), F32), unroll=2)


def middle(
    message, place, inverse, f2, i2, v2, f1, i1, b1, fr, fb, ir, ib, vb,
    i3, i4, bnew, own1, norm,
    f3, e3, wide, tall, e2, er, eb, w, r, rnew,
):
    unpack3(message, 4, 0, f3)
    unpack3(message, 4, 2, e3)
    screen3 = e3[...]
    screen4 = coarse34(screen3, wide)
    i3[...] = 1.0 / (6.0 + screen3)
    i4[...] = 1.0 / (6.0 + screen4)
    coarse_solve(f3[...], i3[...], i4[...], inverse, e3, wide)
    up21(place, e3, f2, i2, v2, f1, i1, b1, e2, er, eb, tall)
    add0(er, eb, vb, w, tall)

    def red_up(p, parity):
        for q in (0, 1):
            r[p, q] = (fr[p, q] + sum0(w, p, parity, q, True)) * ir[p, q]

    plane_pairs(2, X0 - 2, red_up)

    def black_up(p, parity):
        for q in (0, 1):
            w[p, q] = (fb[p, q] + sum0(r, p, parity, q, False)) * ib[p, q]

    black_up(3, 1)
    plane_pairs(4, X0 - 4, black_up)
    black_up(X0 - 4, 0)

    def red_down(p, parity):
        for q in (0, 1):
            rnew[p, q] = (fr[p, q] + sum0(w, p, parity, q, True)) * ir[p, q]

    plane_pairs(4, X0 - 4, red_down)

    def squares(p, parity):
        total = jnp.zeros((24, LANES), F32)
        for q in (0, 1):
            part = (rnew[p, q] - r[p, q]) / ir[p, q]
            total = total + part * part
        return total

    norm[...] = jnp.broadcast_to(own_sum(sum_over(squares)), (8, LANES))

    def black_down(p, parity):
        for q in (0, 1):
            fresh = (fb[p, q] + sum0(rnew, p, parity, q, False)) * ib[p, q]
            bnew[p, q] = fresh
            r[p, q] = fresh - w[p, q]

    black_down(5, 1)
    plane_pairs(6, X0 - 6, black_down)
    black_down(X0 - 6, 0)

    def restrict(i):
        low = 0.5 * below_sum(r, 2 * i + H0)[4:20]
        high = 0.5 * below_sum(r, 2 * i + H0 + 16)[4:20]
        own = (iota((16, LANES), 1) + 128 - OWN) % LANES < 64
        own1[i] = jnp.where(own, low, roll(high, 64, 1))

    loop(0, 8, restrict)


def final(
    message, place, inverse, f2, i2, v2, f1, i1, b1, fr, fb, ir, ib, b, i3, i4, norm, matrix,
    field, sums,
    f3, e3, wide, tall, e2, er, eb, w, r, last,
):
    unpack3(message, 2, 0, f3)
    coarse_solve(f3[...], i3[...], i4[...], inverse, e3, wide)
    up21(place, e3, f2, i2, v2, f1, i1, b1, e2, er, eb, tall)
    add0(er, eb, b, w, tall)

    def red_up(p, parity):
        for q in (0, 1):
            r[p, q] = (fr[p, q] + sum0(w, p, parity, q, True)) * ir[p, q]

    plane_pairs(6, X0 - 6, red_up)

    def black_up(p, parity):
        for q in (0, 1):
            fresh = (fb[p, q] + sum0(r, p, parity, q, False)) * ib[p, q]
            last[p, q] = fresh
            w[p, q] = fresh - w[p, q]

    black_up(7, 1)
    plane_pairs(8, X0 - 8, black_up)
    black_up(X0 - 8, 0)

    def squares(p, parity):
        total = jnp.zeros((24, LANES), F32)
        for q in (0, 1):
            part = sum0(w, p, parity, q, True)
            total = total + part * part
        return total

    after = own_sum(sum_over(squares))

    def finish(i):
        parts = []
        for x in (0, 1):
            for q in (0, 1):
                order = (r, last) if x == q else (last, r)
                parts.append(jnp.concatenate([ref[2 * i + x, q] for ref in order], axis=1))
        result = move([thirds(jnp.concatenate(parts, axis=0))], matrix[...])
        for at in range(4):
            rows = result[24 * at + 4 : 24 * at + 20]
            field[2 * i + at // 2 - H0, pl.ds(at % 2, 16, stride=2), :] = rows

    loop(H0 // 2, H0 // 2 + 16, finish)
    before = norm[0:1, :]
    low = iota((1, LANES), 1) < 64
    both = jnp.where(low, roll(before, -OWN, 1), roll(after, 64 - OWN, 1))
    for i in range(16):
        sums[8 * i : 8 * i + 8, :] = jnp.broadcast_to(both, (8, LANES))


def exchange(to_high, to_low, axis):
    count = lax.axis_size(axis)
    up = [(i, (i + 1) % count) for i in range(count)]
    down = [(j, i) for i, j in up]
    return lax.ppermute(to_high, axis, up), lax.ppermute(to_low, axis, down)


def exchange1(own, low, high):
    from_low, from_high = exchange(high, low, "gx")
    own = jnp.concatenate([from_low, own, from_high], axis=0)
    below, above = exchange(own, own, "gy")
    items = own.shape[0]
    message = (items // GROUP1, 2, 24, LANES)
    coloured, to_high, to_low = call(
        pack_z1, [(items, 2, 24, LANES), message, message], own, below, above
    )
    return coloured, *exchange(to_high, to_low, "gz")


def local(f, s, coarse_inverse):
    inverse = lax.all_gather(coarse_inverse, AXES, axis=0, tiled=True)
    place = jnp.stack([lax.axis_index(axis) for axis in AXES]).astype(jnp.int32)
    low, high = exchange(
        jnp.concatenate([f[32 - H0 :], s[32 - H0 :]], axis=0),
        jnp.concatenate([f[:H0], s[:H0]], axis=0),
        "gx",
    )

    def rows(cut):
        parts = [low[:H0], f, high[:H0], low[H0:], s, high[H0:]]
        return jnp.concatenate([part[:, cut] for part in parts], axis=0)

    below, above = exchange(rows(slice(24, 32)), rows(slice(0, 8)), "gy")
    groups = 2 * X0 // GROUP0
    line0, line1, line2 = (Y0, LANES), (24, LANES), (Y2, LANES)
    split, message = call(
        pack_z0,
        [(2 * X0, *line0), (groups, *line0)],
        *(f, s, low, high, below, above),
        scratch=[(16, *line0)],
    )
    level0, level1, level2 = (X0, 2, *line1), (X1, *line1), (X2, *line2)
    both1 = (X1, 2, *line1)
    matrices1 = jnp.asarray(halo_matrices1(), jnp.bfloat16)
    fr, fb, ir, ib, vb, own1 = call(
        down0,
        [level0] * 5 + [(16, 16, LANES)],
        split,
        *exchange(message, message, "gz"),
        jnp.asarray(lower_matrices(), jnp.bfloat16),
        scratch=[level0, (X0, *line1)],
    )
    f1, i1, b1, f2, i2, v2, message = call(
        down12_first,
        [both1, both1, level1, level2, level2, level2, (512, LANES)],
        *exchange1(own1, own1[:H1], own1[16 - H1 :]),
        matrices1,
        scratch=[level1, (4, *line2)],
    )
    message = lax.all_to_all(message, AXES, 0, 0, tiled=True)
    whole = (16, 16, LANES)
    work = [whole, whole, (8, 16, LANES), (X0 // 2, *line1), level2, level1, level1]
    work += [level0, level0, level0]
    i3, i4, bnew, own1, norm = call(
        middle,
        [whole, (8, 8, LANES), level0, (8, 16, LANES), (8, LANES)],
        message, place, inverse, f2, i2, v2, f1, i1, b1, fr, fb, ir, ib, vb,
        scratch=work,
    )
    f1, b1, f2, v2, message = call(
        down12_next,
        [both1, level1, level2, level2, (256, LANES)],
        *exchange1(own1, own1, own1),
        matrices1,
        i1,
        i2,
        scratch=[level1, (4, *line2)],
    )
    message = lax.all_to_all(message, AXES, 0, 0, tiled=True)
    field, sums = call(
        final,
        [(32, 32, LANES), (128, LANES)],
        message, place, inverse, f2, i2, v2, f1, i1, b1, fr, fb, ir, ib, bnew, i3, i4, norm,
        jnp.asarray(upper_matrix(), jnp.bfloat16),
        scratch=work,
    )
    sums = lax.all_to_all(sums, AXES, 0, 0, tiled=True)
    squares = jnp.sum(sums.reshape(128, 2, 64), axis=(0, 2))
    return field, jnp.sqrt(squares / CELLS)


def solution(mesh):
    return jax.shard_map(
        local,
        mesh=mesh,
        in_specs=(P("gx", "gy", "gz"), P("gx", "gy", "gz"), P(("gx", "gy", "gz"), None)),
        out_specs=(P("gx", "gy", "gz"), P()),
        check_vma=False,
    )
```

```python
import jax
import jax.numpy as jnp
import numpy as np
from jax import lax
from jax.experimental import pallas as pl
from jax.experimental.pallas import tpu as pltpu
from jax.sharding import PartitionSpec as P

AXES = ("gx", "gy", "gz")
F32 = jnp.float32
LANES = 128
OWN = 32
H0 = 8
X0, Y0 = 48, 48
H1 = 14
X1, Y1 = 44, 48
H2 = 6
X2, Y2 = 20, 24
GROUP0 = 8
GROUP1 = 4
CELLS = 16777216.0


def iota(shape, dim):
    return lax.broadcasted_iota(jnp.int32, shape, dim)


def roll(value, shift, axis):
    return pltpu.roll(value, shift % value.shape[axis], axis)


def pick(value, index):
    return jnp.take_along_axis(value, index, axis=1, mode="promise_in_bounds")


def loop(start, stop, body, unroll=2):
    def step(index, carry):
        body(index)
        return carry

    lax.fori_loop(start, stop, step, 0, unroll=unroll)


class Parked:
    def __init__(self, shape, place, whole=None):
        self.shape, self.place, self.whole = shape, place, whole

    def of(self, whole):
        return Parked(self.shape, self.place, whole)


def call(body, outs, *operands, scratch=(), park=None):
    inputs, input_at = [], []
    for operand in operands:
        array = operand.whole if isinstance(operand, Parked) else operand
        at = next((k for k, other in enumerate(inputs) if other is array), len(inputs))
        if at == len(inputs):
            inputs.append(array)
        input_at.append(at)
    far = [isinstance(item, Parked) for item in (*operands, *outs)]
    parked = [item for item in (*operands, *outs) if isinstance(item, Parked)]
    near_outs = [shape for shape in outs if not isinstance(shape, Parked)]
    far_arrays = [operand.whole for operand in operands if isinstance(operand, Parked)]

    def kernel(*refs):
        refs = list(refs)
        ins = [refs.pop(0) for _ in inputs]
        near = [refs.pop(0) for _ in near_outs]
        store = refs.pop(0) if park else None
        semaphores = refs.pop() if parked else None
        work, nears = refs[: len(scratch)], refs[len(scratch) :]
        ready, copies = [], {}
        for at, item in enumerate((*operands, *outs)):
            inward = at < len(operands)
            if far[at]:
                ref = nears.pop(0)
                place = item.place(ins[input_at[at]] if inward else store)
                ends = (place, ref) if inward else (ref, place)
                copies[at] = pltpu.make_async_copy(*ends, semaphores.at[len(copies)])
                if inward:
                    copies[at].start()
            else:
                ref = ins[input_at[at]] if inward else near.pop(0)
            ready.append(ref)
        body(*ready, *work, copies)
        for at in range(len(operands), len(far)):
            if far[at]:
                copies[at].wait()

    def spec(array):
        if any(array is other for other in far_arrays):
            return pl.BlockSpec(memory_space=pl.ANY)
        return pl.BlockSpec(memory_space=pltpu.SMEM if array.dtype == jnp.int32 else pltpu.VMEM)

    shapes = near_outs + ([park] if park else [])
    spaces = [pltpu.VMEM] * len(near_outs) + ([pl.ANY] if park else [])
    work = [pltpu.VMEM(shape, F32) for shape in scratch]
    work += [pltpu.VMEM(item.shape, F32) for item in parked]
    if parked:
        work.append(pltpu.SemaphoreType.DMA((len(parked),)))
    results = pl.pallas_call(
        kernel,
        out_shape=[jax.ShapeDtypeStruct(shape, F32) for shape in shapes],
        in_specs=[spec(array) for array in inputs],
        out_specs=[pl.BlockSpec(memory_space=space) for space in spaces],
        scratch_shapes=work,
        compiler_params=pltpu.CompilerParams(vmem_limit_bytes=32 * 1024 * 1024),
    )(*inputs)
    results = list(results)
    whole = results.pop() if park else None
    return [out.of(whole) if isinstance(out, Parked) else results.pop(0) for out in outs]


def lower_matrices():
    matrices = np.zeros((GROUP0, 256, 256), np.float32)
    for k in range(GROUP0):
        for z in range(-8, 136):
            if 0 <= z < 128:
                row = z
            elif z < 0:
                row = 128 + (16 * k + z) % 128
            else:
                row = 128 + 16 * k + z - 128
            matrices[k, row, 128 * (z % 2) + OWN + z // 2] = 1.0
    return matrices


def upper_matrix():
    matrix = np.zeros((256, 128), np.float32)
    for z in range(128):
        matrix[128 * (z % 2) + OWN + z // 2, z] = 1.0
    return matrix


def halo_matrices1():
    matrices = np.zeros((GROUP1, 384, 256), np.float32)
    for k in range(GROUP1):
        for half in (0, 1):
            for z in range(-H1, 64 + H1):
                if 0 <= z < 64:
                    row = (OWN + 64 * half + z) % 128
                elif z < 0:
                    row = 128 + 64 * half + 14 * k + z + H1
                else:
                    row = 256 + 64 * half + 14 * k + z - 64
                matrices[k, row, 128 * half + OWN + z] = 1.0
    return matrices


def thirds(value):
    high = value.astype(jnp.bfloat16)
    rest = value - high.astype(F32)
    mid = rest.astype(jnp.bfloat16)
    return (rest - mid.astype(F32)).astype(jnp.bfloat16), mid, high


def move(pieces, matrix):
    total = None
    for parts in zip(*pieces):
        left = parts[0] if len(parts) == 1 else jnp.concatenate(parts, axis=1)
        term = jnp.dot(left, matrix, preferred_element_type=F32)
        total = term if total is None else total + term
    return total


def plane_pairs(first, last, body, unroll=4):
    def both(i):
        body(2 * i, 0)
        body(2 * i + 1, 1)

    loop(first // 2, last // 2, both, unroll)


def sum0(values, plane, parity, q, onto_red):
    mid, other = values[plane, q], values[plane, 1 - q]
    total = values[plane + 1, q] + values[plane - 1, q] + mid
    total = total + other + roll(other, 1 if q == 0 else -1, 0)
    high = ((parity + q) % 2 == 1) == onto_red
    return total + roll(mid, -1 if high else 1, 1)


def even_lanes(shape, parity):
    return (iota(shape, 1) + parity) % 2 == 0


def sum1(values, plane, parity, onto_red):
    mid = values[plane]
    total = values[plane + 1] + values[plane - 1] + mid
    total = total + roll(mid, 1, 1) + roll(mid, -1, 1)
    less, more = roll(mid, 1, 0), roll(mid, -1, 0)
    first, second = (less, more) if onto_red else (more, less)
    return total + jnp.where(even_lanes(mid.shape, parity), first, second)


def sum2(values, plane):
    mid = values[plane]
    total = values[plane + 1] + values[plane - 1]
    total = total + roll(mid, 1, 0) + roll(mid, -1, 0)
    return total + roll(mid, 1, 1) + roll(mid, -1, 1)


def is_red(shape, plane):
    return (iota(shape, 0) + iota(shape, 1) + plane) % 2 == 0


def pack_y0(f, s, low, high, to_high, to_low, _):
    for field, own in enumerate((f, s)):
        at, halo = field * X0, slice(field * H0, field * H0 + H0)
        for cut, message in ((slice(24, 32), to_high), (slice(0, 8), to_low)):
            message[at : at + H0] = low[halo, cut]
            message[at + H0 : at + H0 + 32] = own[:, cut]
            message[at + H0 + 32 : at + X0] = high[halo, cut]


def pack_z0(f, s, low, high, below, above, split, message, rows, _):
    block = (iota((Y0, LANES), 1) + 8) % LANES // 16
    for group in range(2 * X0 // GROUP0):
        packed = jnp.zeros((Y0, LANES), F32)
        for k in range(GROUP0):
            item = group * GROUP0 + k
            field, plane = divmod(item, X0)
            own = (f, s)[field]
            slot = item % 16
            rows[slot, 0:8, :] = below[item]
            if plane < H0:
                rows[slot, 8:40, :] = low[field * H0 + plane]
            elif plane < H0 + 32:
                rows[slot, 8:40, :] = own[plane - H0]
            else:
                rows[slot, 8:40, :] = high[field * H0 + plane - H0 - 32]
            rows[slot, 40:48, :] = above[item]
            even = rows[slot, pl.ds(0, 24, stride=2), :]
            odd = rows[slot, pl.ds(1, 24, stride=2), :]
            value = jnp.concatenate([even, odd], axis=0)
            split[item] = value
            packed = jnp.where(block == k, roll(value, 16 * k, 1), packed)
        message[group] = packed


def down0(split, from_low, from_high, matrices, fr, fb, ir, ib, vb, own1, red, screen, copies):
    lane = iota((Y0, LANES), 1)
    groups = 2 * X0 // GROUP0
    merged = [
        jnp.where(lane // 8 % 2 == 1, from_low[group], from_high[group]) for group in range(groups)
    ]
    merged = thirds(jnp.concatenate(merged, axis=0))
    for k in range(GROUP0):
        own = [split[group * GROUP0 + k] for group in range(groups)]
        result = move([thirds(jnp.concatenate(own, axis=0)), merged], matrices[k])
        for group in range(groups):
            field, plane = divmod(group * GROUP0 + k, X0)
            part = result[Y0 * group : Y0 * group + Y0]
            even, odd = part[:, :LANES], part[:, LANES:]
            if field == 1:
                screen[plane] = even[:24] + odd[:24] + even[24:] + odd[24:]
            for q in (0, 1):
                reds, blacks = (even, odd) if (k + q) % 2 == 0 else (odd, even)
                reds, blacks = reds[24 * q : 24 * q + 24], blacks[24 * q : 24 * q + 24]
                if field == 0:
                    fr[plane, q] = reds
                    fb[plane, q] = blacks
                else:
                    ir[plane, q] = 1.0 / (6.0 + reds)
                    ib[plane, q] = 1.0 / (6.0 + blacks)

    for at in range(4, 8):
        copies[at].start()

    def first(p):
        red[p] = fr[p] * ir[p]

    loop(0, X0, first, 4)

    def black(p, parity):
        for q in (0, 1):
            vb[p, q] = (fb[p, q] + sum0(red, p, parity, q, False)) * ib[p, q]

    black(1, 1)
    plane_pairs(2, X0 - 2, black)
    black(X0 - 2, 0)
    copies[8].start()

    def restrict(i):
        plane = 2 * i + H0
        source = 0.5 * below_sum(vb, plane)
        own = (iota((16, LANES), 1) + 128 - OWN) % LANES < 64
        screens = 0.5 * (screen[plane] + screen[plane + 1])[4:20]
        own1[i] = jnp.where(own, source[4:20], roll(screens, 64, 1))

    loop(0, 16, restrict)


def below_sum(values, plane):
    total = sum0(values, plane, 0, 0, True) + sum0(values, plane, 0, 1, True)
    total = total + sum0(values, plane + 1, 1, 0, True)
    return total + sum0(values, plane + 1, 1, 1, True)


def pack_z1(own, below, above, coloured, to_high, to_low, _):
    block = iota((24, LANES), 1) % 64 // 14
    for group in range(own.shape[0] // GROUP1):
        up = [jnp.zeros((24, LANES), F32)] * 2
        down = [jnp.zeros((24, LANES), F32)] * 2
        for k in range(GROUP1):
            item = group * GROUP1 + k
            even, odd = [
                jnp.concatenate([ref[item, pl.ds(q, 8, stride=2), :] for ref in (below, own, above)], axis=0)
                for q in (0, 1)
            ]
            here = even_lanes((24, LANES), item)
            for colour in (0, 1):
                first, second = (even, odd) if colour == 0 else (odd, even)
                value = jnp.where(here, first, second)
                coloured[item, colour] = value
                up[colour] = jnp.where(block == k, roll(value, 14 * k - 82, 1), up[colour])
                down[colour] = jnp.where(block == k, roll(value, 14 * k - 32, 1), down[colour])
        for colour in (0, 1):
            to_high[group, colour] = up[colour]
            to_low[group, colour] = down[colour]


def unpack1(coloured, from_low, from_high, matrices, store):
    items = coloured.shape[0]
    rows = items // GROUP1 * 48
    halos = [thirds(ref[...].reshape(rows, LANES)) for ref in (from_low, from_high)]
    for k in range(GROUP1):
        own = [coloured[item, colour] for item in range(k, items, GROUP1) for colour in (0, 1)]
        result = move([thirds(jnp.concatenate(own, axis=0)), *halos], matrices[k])
        for at in range(items // GROUP1 * 2):
            part = result[24 * at : 24 * at + 24]
            store(at // 2 * GROUP1 + k, at % 2, (part[:, :LANES], part[:, LANES:]))


def pair_index(rows):
    return jnp.clip(2 * iota((rows, LANES), 1) - OWN, 0, 127)


def spread_index(rows):
    return (iota((rows, LANES), 1) - OWN) // 2 + OWN


def coarse12(total):
    pairs = total + roll(total, -1, 1)
    return 0.5 * pick(pairs, pair_index(Y2))


def down12(f1, i1, b1, f2, i2, v2, red):
    def first(p):
        red[p] = f1[p, 0] * i1[p, 0]

    loop(0, X1, first, 4)

    def black(p, parity):
        b1[p] = (f1[p, 1] + sum1(red, p, parity, False)) * i1[p, 1]

    black(1, 1)
    plane_pairs(2, X1 - 2, black)
    black(X1 - 2, 0)

    def restrict(i):
        plane = 2 * i + 2
        f2[i] = coarse12(sum1(b1, plane, 0, True) + sum1(b1, plane + 1, 1, True))

    loop(0, X2, restrict, 4)

    def red2(p):
        v2[p] = jnp.where(is_red((Y2, LANES), p), f2[p] * i2[p], 0.0)

    def black2(p):
        fresh = (f2[p] + sum2(v2, p)) * i2[p]
        v2[p] = jnp.where(is_red((Y2, LANES), p), v2[p], fresh)

    loop(0, X2, red2, 4)
    loop(1, X2 - 1, black2, 3)


def coarse23(total, sums, x3):
    sums[x3] = total
    pairs = sums[x3, pl.ds(8, 8, stride=2), :] + sums[x3, pl.ds(9, 8, stride=2), :]
    pairs = pairs + roll(pairs, -1, 1)
    lane = iota((8, LANES), 1)
    spread = pick(pairs, OWN + 2 * (lane % 16))
    here = lane // 16 == (x3 % 2) * 4 + iota((8, LANES), 0)
    here = jnp.logical_and(here, iota((8, LANES), 0) < 4)
    return 0.5 * jnp.sum(jnp.where(here, spread, 0.0), axis=0, keepdims=True)


def source3(v2, sums):
    rows = []
    for x3 in range(4):
        plane = 2 * x3 + H2
        total = jnp.zeros((Y2, LANES), F32)
        for p in (plane, plane + 1):
            total += jnp.where(is_red((Y2, LANES), p), sum2(v2, p), 0.0)
        rows.append(coarse23(total, sums, x3))
    return [rows[0] + rows[1], rows[2] + rows[3]]


def down12_first(coloured, from_low, from_high, matrices, f1, i1, b1, f2, i2, v2, message, red, sums, copies):
    def store(plane, colour, halves):
        f1[plane, colour], i1[plane, colour] = halves

    unpack1(coloured, from_low, from_high, matrices, store)

    def screen2(i):
        plane = 2 * i + 2
        total = i1[plane, 0] + i1[plane, 1] + i1[plane + 1, 0] + i1[plane + 1, 1]
        i2[i] = coarse12(total)

    loop(0, X2, screen2, 4)
    rows = []
    for x3 in range(4):
        plane = 2 * x3 + H2
        rows.append(coarse23(i2[plane] + i2[plane + 1], sums, x3))

    def invert1(p):
        i1[p] = 1.0 / (6.0 + i1[p])

    def invert2(p):
        i2[p] = 1.0 / (6.0 + i2[p])

    loop(0, X1, invert1, 4)
    loop(0, X2, invert2, 4)
    for at in (4, 5, 8):
        copies[at].start()
    down12(f1, i1, b1, f2, i2, v2, red)
    for at in (6, 7, 9):
        copies[at].start()
    tile = source3(v2, sums) + [rows[0] + rows[1], rows[2] + rows[3]]
    tile = jnp.concatenate(tile + tile, axis=0)
    for i in range(64):
        message[8 * i : 8 * i + 8, :] = tile


def down12_next(coloured, from_low, from_high, matrices, i1, i2, f1, b1, f2, v2, message, red, sums, copies):
    def store(item, colour, halves):
        block, i = divmod(item, 8)
        for half in (0, 1):
            plane = H1 + 16 * (block - 1) + 8 * half + i
            if 0 <= plane < X1:
                f1[plane, colour] = halves[half]

    unpack1(coloured, from_low, from_high, matrices, store)
    for at in (4, 5):
        copies[at].wait()
    down12(f1, i1, b1, f2, i2, v2, red)
    tile = jnp.concatenate(source3(v2, sums) * 4, axis=0)
    for i in range(32):
        message[8 * i : 8 * i + 8, :] = tile


def unpack3(message, rows, first, into):
    sub, lane = iota((8, LANES), 0), iota((8, LANES), 1)
    for gx in range(4):
        for gy in range(4):
            for half in range(2):
                start = (gx * 4 + gy) * 8 * rows + first + half
                value = message[pl.ds(start, 8, stride=rows), :]
                for k in (1, 2, 4):
                    sub_high = (sub // k) % 2 == 1
                    lane_high = (lane // (16 * k)) % 2 == 1
                    from_below = roll(roll(value, -k, 0), 16 * k, 1)
                    from_above = roll(roll(value, k, 0), -16 * k, 1)
                    value = jnp.where(
                        sub_high == lane_high, value, jnp.where(sub_high, from_above, from_below)
                    )
                for x in range(2):
                    into[gx * 4 + 2 * half + x, gy * 4 : gy * 4 + 4, :] = value[4 * x : 4 * x + 4, :]


def turn(value, shift, axis):
    if axis == 0:
        return jnp.concatenate([value[-shift:], value[:-shift]], axis=0)
    return roll(value, shift, axis)


def sum_whole(value):
    total = turn(value, 1, 0) + turn(value, -1, 0)
    total = total + turn(value, 1, 1) + turn(value, -1, 1)
    return total + turn(value, 1, 2) + turn(value, -1, 2)


def red_whole(shape):
    return (iota(shape, 0) + iota(shape, 1) + iota(shape, 2)) % 2 == 0


def pick3(value, index):
    flat = value.reshape(-1, LANES)
    return pick(flat, jnp.broadcast_to(index, flat.shape)).reshape(value.shape)


def coarse34(value, wide):
    wide[...] = value.reshape(8, 2, 16, LANES).sum(axis=1)
    pairs = wide[:, pl.ds(0, 8, stride=2), :] + wide[:, pl.ds(1, 8, stride=2), :]
    pairs = pairs + roll(pairs, -1, 2)
    return 0.5 * pick3(pairs, 2 * (iota((1, LANES), 1) % 64))


def coarse_solve(f3, i3, i4, place, inverse, e3, wide):
    red3, red4 = red_whole((16, 16, LANES)), red_whole((8, 8, LANES))
    v3 = jnp.where(red3, f3 * i3, 0.0)
    v3 = jnp.where(red3, v3, (f3 + sum_whole(v3)) * i3)
    f4 = coarse34(jnp.where(red3, sum_whole(v3), 0.0), wide)
    v4 = jnp.where(red4, f4 * i4, 0.0)
    v4 = jnp.where(red4, v4, (f4 + sum_whole(v4)) * i4)
    r4 = jnp.where(red4, sum_whole(v4), 0.0).reshape(4, 2, 8, LANES).sum(axis=1)
    sub, lane = iota((8, LANES), 0), iota((8, LANES), 1)
    rows = []
    for x5 in range(4):
        pairs = r4[x5] + roll(r4[x5], -1, 1)
        spread = jnp.where(sub // 2 == lane // 32, pick(pairs, 2 * (lane % 32)), 0.0)
        rows.append(0.5 * jnp.sum(spread, axis=0, keepdims=True))
    vector = jnp.broadcast_to(jnp.concatenate(rows, axis=1), (8, 512))
    answer = lax.dot_general(
        vector,
        jnp.concatenate([ref[...] for ref in inverse] + [jnp.zeros((64, 512), F32)], axis=0),
        (((1,), (1,)), ((), ())),
        precision=lax.Precision.HIGHEST,
        preferred_element_type=F32,
    )
    planes = []
    for x5 in range(4):
        z5 = lane % 64 // 2
        index = (place[1] + 4 - sub // 2) % 4 * 16 + (place[0] + 4 - x5) % 4 * 4 + z5 % 4
        apart = (z5 // 4 + 8 - place[2]) % 8
        same = pick(answer[:, :LANES], index + jnp.where(apart == 7, 64, 0))
        part = jnp.where(apart == 1, pick(answer[:, LANES:], index), same)
        part = jnp.where(jnp.logical_or(apart <= 1, apart == 7), part, 0.0)
        planes += [part[None], part[None]]
    w4 = v4 + jnp.concatenate(planes, axis=0)
    w4 = jnp.where(red4, (f4 + sum_whole(w4)) * i4, w4)
    e4 = jnp.where(red4, w4, (f4 + sum_whole(w4)) * i4)
    e4 = pick3(e4, iota((1, LANES), 1) // 2)
    wide[:, pl.ds(0, 8, stride=2), :] = e4
    wide[:, pl.ds(1, 8, stride=2), :] = e4
    spread = jnp.broadcast_to(wide[...][:, None], (8, 2, 16, LANES)).reshape(16, 16, LANES)
    w3 = v3 + spread
    w3 = jnp.where(red3, (f3 + sum_whole(w3)) * i3, w3)
    e3[...] = jnp.where(red3, w3, (f3 + sum_whole(w3)) * i3)


def up21(place, e3, f2, i2, v2, f1, i1, b1, e2, er, eb, tall):
    shift_y = lax.rem(20 - 4 * place[1], 16)
    shift_z = lax.rem(160 - 16 * place[2], 128)

    def from3(i):
        value = e3[lax.rem(4 * place[0] + i + 13, 16)]
        value = pltpu.roll(pltpu.roll(value, shift_y, 0), shift_z, 1)
        value = pick(value, spread_index(16))[:12]
        tall[i, pl.ds(0, 12, stride=2), :] = value
        tall[i, pl.ds(1, 12, stride=2), :] = value
        value = tall[i]
        e2[2 * i] = v2[2 * i] + value
        e2[2 * i + 1] = v2[2 * i + 1] + value

    loop(0, X2 // 2, from3, 5)

    def red2(p):
        fresh = (f2[p] + sum2(e2, p)) * i2[p]
        e2[p] = jnp.where(is_red((Y2, LANES), p), fresh, e2[p])

    def black2(p):
        fresh = (f2[p] + sum2(e2, p)) * i2[p]
        e2[p] = jnp.where(is_red((Y2, LANES), p), e2[p], fresh)

    loop(1, X2 - 1, red2, 3)
    loop(2, X2 - 2, black2, 4)

    def from2(i):
        value = pick(e2[i], spread_index(Y2))
        eb[2 * i + 2] = b1[2 * i + 2] + value
        eb[2 * i + 3] = b1[2 * i + 3] + value

    loop(3, 17, from2, 7)

    def red1(p, parity):
        er[p] = (f1[p, 0] + sum1(eb, p, parity, True)) * i1[p, 0]

    def black1(p, parity):
        eb[p] = (f1[p, 1] + sum1(er, p, parity, False)) * i1[p, 1]

    plane_pairs(8, 36, red1)
    plane_pairs(10, 34, black1)


def add0(er, eb, b, w, tall):
    def from1(i):
        reds, blacks = er[i + 10, 6:18], eb[i + 10, 6:18]
        here = (iota((12, LANES), 1) + i) % 2 == 0
        tall[i, pl.ds(0, 12, stride=2), :] = jnp.where(here, reds, blacks)
        tall[i, pl.ds(1, 12, stride=2), :] = jnp.where(here, blacks, reds)
        value = tall[i]
        for p in (2 * i, 2 * i + 1):
            for q in (0, 1):
                w[p, q] = b[p, q] + value

    loop(0, X0 // 2, from1, 4)


def own_sum(total):
    row, lane = iota((24, LANES), 0), iota((24, LANES), 1)
    own = jnp.logical_and((row + 20) % 24 < 16, (lane + 128 - OWN) % LANES < 64)
    return jnp.sum(jnp.where(own, total, 0.0), axis=0, keepdims=True)


def sum_over(body):
    def step(i, total):
        return total + body(2 * i, 0) + body(2 * i + 1, 1)

    return lax.fori_loop(H0 // 2, H0 // 2 + 16, step, jnp.zeros((24, LANES), F32), unroll=2)


def middle(
    message, place, near, before, after, f2, i2, v2, f1, i1, b1, fr, fb, ir, ib, vb,
    i3, i4, bnew, own1, norm,
    f3, e3, wide, tall, e2, er, eb, w, r, rnew, copies,
):
    unpack3(message, 4, 0, f3)
    unpack3(message, 4, 2, e3)
    screen3 = e3[...]
    screen4 = coarse34(screen3, wide)
    i3[...] = 1.0 / (6.0 + screen3)
    i4[...] = 1.0 / (6.0 + screen4)
    coarse_solve(f3[...], i3[...], i4[...], place, (near, before, after), e3, wide)
    for at in range(5, 11):
        copies[at].wait()
    up21(place, e3, f2, i2, v2, f1, i1, b1, e2, er, eb, tall)
    for at in range(11, 16):
        copies[at].wait()
    add0(er, eb, vb, w, tall)

    def red_up(p, parity):
        for q in (0, 1):
            r[p, q] = (fr[p, q] + sum0(w, p, parity, q, True)) * ir[p, q]

    plane_pairs(2, X0 - 2, red_up)

    def black_up(p, parity):
        for q in (0, 1):
            w[p, q] = (fb[p, q] + sum0(r, p, parity, q, False)) * ib[p, q]

    black_up(3, 1)
    plane_pairs(4, X0 - 4, black_up)
    black_up(X0 - 4, 0)

    def red_down(p, parity):
        for q in (0, 1):
            rnew[p, q] = (fr[p, q] + sum0(w, p, parity, q, True)) * ir[p, q]

    plane_pairs(4, X0 - 4, red_down)

    def squares(p, parity):
        total = jnp.zeros((24, LANES), F32)
        for q in (0, 1):
            part = (rnew[p, q] - r[p, q]) / ir[p, q]
            total = total + part * part
        return total

    norm[...] = jnp.broadcast_to(own_sum(sum_over(squares)), (8, LANES))

    def black_down(p, parity):
        for q in (0, 1):
            fresh = (fb[p, q] + sum0(rnew, p, parity, q, False)) * ib[p, q]
            bnew[p, q] = fresh
            r[p, q] = fresh - w[p, q]

    black_down(5, 1)
    plane_pairs(6, X0 - 6, black_down)
    black_down(X0 - 6, 0)

    def restrict(i):
        low = 0.5 * below_sum(r, 2 * i + H0)[4:20]
        high = 0.5 * below_sum(r, 2 * i + H0 + 16)[4:20]
        own = (iota((16, LANES), 1) + 128 - OWN) % LANES < 64
        own1[i] = jnp.where(own, low, roll(high, 64, 1))

    loop(0, 8, restrict)


def final(
    message, place, near, before, after, f2, i2, v2, f1, i1, b1, fr, fb, ir, ib, b, i3, i4,
    norm, matrix,
    field, sums,
    f3, e3, wide, tall, e2, er, eb, w, r, last, copies,
):
    unpack3(message, 2, 0, f3)
    coarse_solve(f3[...], i3[...], i4[...], place, (near, before, after), e3, wide)
    for at in (6, 9):
        copies[at].wait()
    up21(place, e3, f2, i2, v2, f1, i1, b1, e2, er, eb, tall)
    for at in range(11, 15):
        copies[at].wait()
    add0(er, eb, b, w, tall)

    def red_up(p, parity):
        for q in (0, 1):
            r[p, q] = (fr[p, q] + sum0(w, p, parity, q, True)) * ir[p, q]

    plane_pairs(6, X0 - 6, red_up)

    def black_up(p, parity):
        for q in (0, 1):
            fresh = (fb[p, q] + sum0(r, p, parity, q, False)) * ib[p, q]
            last[p, q] = fresh
            w[p, q] = fresh - w[p, q]

    black_up(7, 1)
    plane_pairs(8, X0 - 8, black_up)
    black_up(X0 - 8, 0)

    def squares(p, parity):
        total = jnp.zeros((24, LANES), F32)
        for q in (0, 1):
            part = sum0(w, p, parity, q, True)
            total = total + part * part
        return total

    squared = own_sum(sum_over(squares))

    def finish(i):
        parts = []
        for x in (0, 1):
            for q in (0, 1):
                order = (r, last) if x == q else (last, r)
                parts.append(jnp.concatenate([ref[2 * i + x, q] for ref in order], axis=1))
        result = move([thirds(jnp.concatenate(parts, axis=0))], matrix[...])
        for at in range(4):
            rows = result[24 * at + 4 : 24 * at + 20]
            field[2 * i + at // 2 - H0, pl.ds(at % 2, 16, stride=2), :] = rows

    loop(H0 // 2, H0 // 2 + 16, finish)
    low = iota((1, LANES), 1) < 64
    both = jnp.where(low, roll(norm[0:1, :], -OWN, 1), roll(squared, 64 - OWN, 1))
    for i in range(16):
        sums[8 * i : 8 * i + 8, :] = jnp.broadcast_to(both, (8, LANES))


def exchange(to_high, to_low, axis):
    count = lax.axis_size(axis)
    up = [(i, (i + 1) % count) for i in range(count)]
    down = [(j, i) for i, j in up]
    return lax.ppermute(to_high, axis, up), lax.ppermute(to_low, axis, down)


def from_all(own, axis):
    count = lax.axis_size(axis)
    shifts = [[(i, (i + k) % count) for i in range(count)] for k in range(1, count)]
    return [lax.ppermute(own, axis, shift) for shift in shifts]


def together(first, second):
    both = lax.optimization_barrier((*first, *second))
    return both[: len(first)], both[len(first) :]


def exchange1(own, low, high, beside=()):
    from_low, from_high = exchange(high, low, "gx")
    own = jnp.concatenate([from_low, own, from_high], axis=0)
    below, above = exchange(own, own, "gy")
    if beside:
        (below, above), beside = together((below, above), exchange(*beside, "gz"))
    items = own.shape[0]
    message = (items // GROUP1, 2, 24, LANES)
    coloured, to_high, to_low = call(
        pack_z1, [(items, 2, 24, LANES), message, message], own, below, above
    )
    return (coloured, *exchange(to_high, to_low, "gz")), beside


def local(f, s, coarse_inverse):
    place = jnp.stack([lax.axis_index(axis) for axis in AXES]).astype(jnp.int32)
    low, high = exchange(
        jnp.concatenate([f[32 - H0 :], s[32 - H0 :]], axis=0),
        jnp.concatenate([f[:H0], s[:H0]], axis=0),
        "gx",
    )
    (low, high), others = together((low, high), from_all(coarse_inverse, "gx"))
    inverse = jnp.concatenate([coarse_inverse, *others], axis=0)
    messages = call(pack_y0, [(2 * X0, 8, LANES)] * 2, f, s, low, high)
    below, above = exchange(*messages, "gy")
    (below, above), others = together((below, above), from_all(inverse, "gy"))
    inverse = jnp.concatenate([inverse, *others], axis=0)
    groups = 2 * X0 // GROUP0
    line0, line1, line2 = (Y0, LANES), (24, LANES), (Y2, LANES)
    split, message = call(
        pack_z0,
        [(2 * X0, *line0), (groups, *line0)],
        *(f, s, low, high, below, above),
        scratch=[(16, *line0)],
    )
    level0, level1, level2 = (X0, 2, *line1), (X1, *line1), (X2, *line2)
    both1 = (X1, 2, *line1)
    matrices1 = jnp.asarray(halo_matrices1(), jnp.bfloat16)
    fr, fb, ir, ib, vb, own1 = call(
        down0,
        [Parked(level0, lambda ref, k=k: ref.at[k]) for k in range(5)] + [(16, 16, LANES)],
        split,
        *exchange(message, message, "gz"),
        jnp.asarray(lower_matrices(), jnp.bfloat16),
        scratch=[level0, (X0, *line1)],
        park=(56, *level0),
    )
    level1_parts, others = exchange1(own1, own1[:H1], own1[16 - H1 :], (inverse, inverse))
    inverse = (inverse, *others)
    f1, i1, b1, f2, i2, v2, message = call(
        down12_first,
        [
            Parked(both1, lambda ref: ref.at[0]),
            Parked(both1, lambda ref: ref.at[1]),
            Parked(level1, lambda ref: ref.at[2, :, 0]),
            Parked(level2, lambda ref: ref.at[2, 0:X2, 1]),
            Parked(level2, lambda ref: ref.at[3, 0:X2, 0]),
            Parked(level2, lambda ref: ref.at[3, 0:X2, 1]),
            (512, LANES),
        ],
        *level1_parts,
        matrices1,
        scratch=[level1, (4, *line2)],
        park=(60, *both1),
    )
    message = lax.all_to_all(message, AXES, 0, 0, tiled=True)
    whole = (16, 16, LANES)
    work = [whole, whole, (8, 16, LANES), (X0 // 2, *line1), level2, level1, level1]
    work += [level0, level0, level0]
    i3, i4, bnew, own1, norm = call(
        middle,
        [whole, (8, 8, LANES), level0, (8, 16, LANES), (8, LANES)],
        message, place, *inverse, f2, i2, v2, f1, i1, b1, fr, fb, ir, ib, vb,
        scratch=work,
    )
    f1, b1, f2, v2, message = call(
        down12_next,
        [both1, level1, level2, level2, (256, LANES)],
        *exchange1(own1, own1, own1)[0],
        matrices1,
        i1,
        i2,
        scratch=[level1, (4, *line2)],
    )
    message = lax.all_to_all(message, AXES, 0, 0, tiled=True)
    field, sums = call(
        final,
        [(32, 32, LANES), (128, LANES)],
        message, place, *inverse, f2, i2, v2, f1, i1, b1, fr, fb, ir, ib, bnew, i3, i4, norm,
        jnp.asarray(upper_matrix(), jnp.bfloat16),
        scratch=work,
    )
    sums = lax.all_to_all(sums, AXES, 0, 0, tiled=True)
    squares = jnp.sum(sums.reshape(128, 2, 64), axis=(0, 2))
    return field, jnp.sqrt(squares / CELLS)


def solution(mesh):
    return jax.shard_map(
        local,
        mesh=mesh,
        in_specs=(P("gx", "gy", "gz"), P("gx", "gy", "gz"), P(("gx", "gy", "gz"), None)),
        out_specs=(P("gx", "gy", "gz"), P()),
        check_vma=False,
    )
```

```python
import jax
import jax.numpy as jnp
import numpy as np
from jax import lax
from jax.experimental import pallas as pl
from jax.experimental.pallas import tpu as pltpu
from jax.sharding import PartitionSpec as P

AXES = ("gx", "gy", "gz")
F32 = jnp.float32
LANES = 128
OWN = 32
H0 = 8
X0, Y0 = 48, 48
H1 = 14
X1, Y1 = 44, 48
H2 = 6
X2, Y2 = 20, 24
GROUP0 = 8
GROUP1 = 4
BEGIN, END = 8, 36
CELLS = 16777216.0


def iota(shape, dim):
    return lax.broadcasted_iota(jnp.int32, shape, dim)


def roll(value, shift, axis):
    return pltpu.roll(value, shift % value.shape[axis], axis)


def pick(value, index):
    return jnp.take_along_axis(value, index, axis=1, mode="promise_in_bounds")


def loop(start, stop, body, unroll=2):
    def step(index, carry):
        body(index)
        return carry

    lax.fori_loop(start, stop, step, 0, unroll=unroll)


class Parked:
    def __init__(self, shape, place, whole=None):
        self.shape, self.place, self.whole = shape, place, whole

    def of(self, whole):
        return Parked(self.shape, self.place, whole)


def call(body, outs, *operands, scratch=(), park=None):
    inputs, input_at = [], []
    for operand in operands:
        array = operand.whole if isinstance(operand, Parked) else operand
        at = next((k for k, other in enumerate(inputs) if other is array), len(inputs))
        if at == len(inputs):
            inputs.append(array)
        input_at.append(at)
    far = [isinstance(item, Parked) for item in (*operands, *outs)]
    parked = [item for item in (*operands, *outs) if isinstance(item, Parked)]
    near_outs = [shape for shape in outs if not isinstance(shape, Parked)]
    far_arrays = [operand.whole for operand in operands if isinstance(operand, Parked)]

    def kernel(*refs):
        refs = list(refs)
        ins = [refs.pop(0) for _ in inputs]
        near = [refs.pop(0) for _ in near_outs]
        store = refs.pop(0) if park else None
        semaphores = refs.pop() if parked else None
        work, nears = refs[: len(scratch)], refs[len(scratch) :]
        ready, copies = [], {}
        for at, item in enumerate((*operands, *outs)):
            inward = at < len(operands)
            if far[at]:
                ref = nears.pop(0)
                place = item.place(ins[input_at[at]] if inward else store)
                ends = (place, ref) if inward else (ref, place)
                copies[at] = pltpu.make_async_copy(*ends, semaphores.at[len(copies)])
                if inward:
                    copies[at].start()
            else:
                ref = ins[input_at[at]] if inward else near.pop(0)
            ready.append(ref)
        body(*ready, *work, copies)
        for at in range(len(operands), len(far)):
            if far[at]:
                copies[at].wait()

    def spec(array):
        if any(array is other for other in far_arrays):
            return pl.BlockSpec(memory_space=pl.ANY)
        return pl.BlockSpec(memory_space=pltpu.SMEM if array.dtype == jnp.int32 else pltpu.VMEM)

    shapes = near_outs + ([park] if park else [])
    spaces = [pltpu.VMEM] * len(near_outs) + ([pl.ANY] if park else [])
    work = [pltpu.VMEM(shape, F32) for shape in scratch]
    work += [pltpu.VMEM(item.shape, F32) for item in parked]
    if parked:
        work.append(pltpu.SemaphoreType.DMA((len(parked),)))
    results = pl.pallas_call(
        kernel,
        out_shape=[jax.ShapeDtypeStruct(shape, F32) for shape in shapes],
        in_specs=[spec(array) for array in inputs],
        out_specs=[pl.BlockSpec(memory_space=space) for space in spaces],
        scratch_shapes=work,
        compiler_params=pltpu.CompilerParams(vmem_limit_bytes=20 * 1024 * 1024),
    )(*inputs)
    results = list(results)
    whole = results.pop() if park else None
    return [out.of(whole) if isinstance(out, Parked) else results.pop(0) for out in outs]


def lower_matrices():
    matrices = np.zeros((GROUP0, 256, 256), np.float32)
    for k in range(GROUP0):
        for z in range(-8, 136):
            if 0 <= z < 128:
                row = z
            elif z < 0:
                row = 128 + (16 * k + z) % 128
            else:
                row = 128 + 16 * k + z - 128
            matrices[k, row, 128 * (z % 2) + OWN + z // 2] = 1.0
    return matrices


def upper_matrix():
    matrix = np.zeros((256, 128), np.float32)
    for z in range(128):
        matrix[128 * (z % 2) + OWN + z // 2, z] = 1.0
    return matrix


def halo_matrices1():
    matrices = np.zeros((GROUP1, 384, 256), np.float32)
    for k in range(GROUP1):
        for half in (0, 1):
            for z in range(-H1, 64 + H1):
                if 0 <= z < 64:
                    row = (OWN + 64 * half + z) % 128
                elif z < 0:
                    row = 128 + 64 * half + 14 * k + z + H1
                else:
                    row = 256 + 64 * half + 14 * k + z - 64
                matrices[k, row, 128 * half + OWN + z] = 1.0
    return matrices


def thirds(value):
    high = value.astype(jnp.bfloat16)
    rest = value - high.astype(F32)
    mid = rest.astype(jnp.bfloat16)
    return (rest - mid.astype(F32)).astype(jnp.bfloat16), mid, high


def halves(value):
    high = value.astype(jnp.bfloat16)
    return (value - high.astype(F32)).astype(jnp.bfloat16), high


def move(pieces, matrix):
    total = None
    for parts in zip(*pieces):
        left = parts[0] if len(parts) == 1 else jnp.concatenate(parts, axis=1)
        term = jnp.dot(left, matrix, preferred_element_type=F32)
        total = term if total is None else total + term
    return total


def plane_pairs(first, last, body, unroll=4):
    def both(i):
        body(2 * i, 0)
        body(2 * i + 1, 1)

    loop(first // 2, last // 2, both, unroll)


def sum0(values, plane, parity, q, onto_red):
    mid, other = values[plane, q], values[plane, 1 - q]
    total = values[plane + 1, q] + values[plane - 1, q] + mid
    total = total + other + roll(other, 1 if q == 0 else -1, 0)
    high = ((parity + q) % 2 == 1) == onto_red
    return total + roll(mid, -1 if high else 1, 1)


def even_lanes(shape, parity):
    return (iota(shape, 1) + parity) % 2 == 0


def sum1(values, plane, parity, onto_red):
    mid = values[plane]
    total = values[plane + 1] + values[plane - 1] + mid
    total = total + roll(mid, 1, 1) + roll(mid, -1, 1)
    less, more = roll(mid, 1, 0), roll(mid, -1, 0)
    first, second = (less, more) if onto_red else (more, less)
    return total + jnp.where(even_lanes(mid.shape, parity), first, second)


def sum2(values, plane):
    mid = values[plane]
    total = values[plane + 1] + values[plane - 1]
    total = total + roll(mid, 1, 0) + roll(mid, -1, 0)
    return total + roll(mid, 1, 1) + roll(mid, -1, 1)


def is_red(shape, plane):
    return (iota(shape, 0) + iota(shape, 1) + plane) % 2 == 0


def pack_y0(f, s, low, high, to_high, to_low, _):
    for field, own in enumerate((f, s)):
        at, halo = field * X0, slice(field * H0, field * H0 + H0)
        for cut, message in ((slice(24, 32), to_high), (slice(0, 8), to_low)):
            message[at : at + H0] = low[halo, cut]
            message[at + H0 : at + H0 + 32] = own[:, cut]
            message[at + H0 + 32 : at + X0] = high[halo, cut]


def pack_z0(f, s, low, high, below, above, split, to_high, to_low, rows, _):
    lane = iota((Y0, LANES), 1)
    block = (lane + 8) % LANES // 16
    last = lane // 8 % 2 == 1
    pair = []
    for group in range(2 * X0 // GROUP0):
        packed = jnp.zeros((Y0, LANES), F32)
        for k in range(GROUP0):
            item = group * GROUP0 + k
            field, plane = divmod(item, X0)
            own = (f, s)[field]
            slot = item % 16
            rows[slot, 0:8, :] = below[item]
            if plane < H0:
                rows[slot, 8:40, :] = low[field * H0 + plane]
            elif plane < H0 + 32:
                rows[slot, 8:40, :] = own[plane - H0]
            else:
                rows[slot, 8:40, :] = high[field * H0 + plane - H0 - 32]
            rows[slot, 40:48, :] = above[item]
            even = rows[slot, pl.ds(0, 24, stride=2), :]
            odd = rows[slot, pl.ds(1, 24, stride=2), :]
            value = jnp.concatenate([even, odd], axis=0)
            split[item] = value
            packed = jnp.where(block == k, roll(value, 16 * k, 1), packed)
        pair.append(packed)
        if len(pair) == 2:
            to_high[group // 2] = jnp.where(last, pair[0], roll(pair[1], 8, 1))
            to_low[group // 2] = jnp.where(last, roll(pair[1], -8, 1), pair[0])
            pair = []


def down0(split, from_low, from_high, matrices, fr, fb, ir, ib, vb, own1, red, screen, copies):
    lane = iota((Y0, LANES), 1)
    groups = 2 * X0 // GROUP0
    merged = []
    for half in range(groups // 2):
        left, right = from_low[half], from_high[half]
        merged.append(jnp.where(lane // 8 % 2 == 1, left, right))
        merged.append(jnp.where(lane // 8 % 2 == 1, roll(left, -8, 1), roll(right, 8, 1)))
    merged = halves(jnp.concatenate(merged, axis=0))
    for k in range(GROUP0):
        own = [split[group * GROUP0 + k] for group in range(groups)]
        result = move([halves(jnp.concatenate(own, axis=0)), merged], matrices[k])
        for group in range(groups):
            field, plane = divmod(group * GROUP0 + k, X0)
            part = result[Y0 * group : Y0 * group + Y0]
            even, odd = part[:, :LANES], part[:, LANES:]
            if field == 1:
                screen[plane] = even[:24] + odd[:24] + even[24:] + odd[24:]
            for q in (0, 1):
                reds, blacks = (even, odd) if (k + q) % 2 == 0 else (odd, even)
                reds, blacks = reds[24 * q : 24 * q + 24], blacks[24 * q : 24 * q + 24]
                if field == 0:
                    fr[plane, q] = reds
                    fb[plane, q] = blacks
                else:
                    ir[plane, q] = 1.0 / (6.0 + reds)
                    ib[plane, q] = 1.0 / (6.0 + blacks)

    for at in range(4, 8):
        copies[at].start()

    def first(p):
        red[p] = fr[p] * ir[p]

    loop(0, X0, first, 4)

    def black(p, parity):
        for q in (0, 1):
            vb[p, q] = (fb[p, q] + sum0(red, p, parity, q, False)) * ib[p, q]

    black(1, 1)
    plane_pairs(2, X0 - 2, black)
    black(X0 - 2, 0)
    copies[8].start()

    def restrict(i):
        plane = 2 * i + H0
        source = 0.5 * below_sum(vb, plane)
        own = (iota((16, LANES), 1) + 128 - OWN) % LANES < 64
        screens = 0.5 * (screen[plane] + screen[plane + 1])[4:20]
        own1[i] = jnp.where(own, source[4:20], roll(screens, 64, 1))

    loop(0, 16, restrict)


def below_sum(values, plane):
    total = sum0(values, plane, 0, 0, True) + sum0(values, plane, 0, 1, True)
    total = total + sum0(values, plane + 1, 1, 0, True)
    return total + sum0(values, plane + 1, 1, 1, True)


def pack_z1(own, below, above, coloured, to_high, to_low, _):
    block = iota((24, LANES), 1) % 64 // 14
    for group in range(own.shape[0] // GROUP1):
        up = [jnp.zeros((24, LANES), F32)] * 2
        down = [jnp.zeros((24, LANES), F32)] * 2
        for k in range(GROUP1):
            item = group * GROUP1 + k
            even, odd = [
                jnp.concatenate([ref[item, pl.ds(q, 8, stride=2), :] for ref in (below, own, above)], axis=0)
                for q in (0, 1)
            ]
            here = even_lanes((24, LANES), item)
            for colour in (0, 1):
                first, second = (even, odd) if colour == 0 else (odd, even)
                value = jnp.where(here, first, second)
                coloured[item, colour] = value
                up[colour] = jnp.where(block == k, roll(value, 14 * k - 82, 1), up[colour])
                down[colour] = jnp.where(block == k, roll(value, 14 * k - 32, 1), down[colour])
        for colour in (0, 1):
            to_high[group, colour] = up[colour]
            to_low[group, colour] = down[colour]


def unpack1(coloured, from_low, from_high, matrices, store, first, last):
    groups = range(first // GROUP1, last // GROUP1)
    rows = len(groups) * 48
    halos = [
        halves(ref[groups.start : groups.stop].reshape(rows, LANES))
        for ref in (from_low, from_high)
    ]
    for k in range(GROUP1):
        own = [coloured[GROUP1 * g + k, colour] for g in groups for colour in (0, 1)]
        result = move([halves(jnp.concatenate(own, axis=0)), *halos], matrices[k])
        for at in range(2 * len(groups)):
            part = result[24 * at : 24 * at + 24]
            item = GROUP1 * groups[at // 2] + k
            store(item, at % 2, (part[:, :LANES], part[:, LANES:]))


def pair_index(rows):
    return jnp.clip(2 * iota((rows, LANES), 1) - OWN, 0, 127)


def spread_index(rows):
    return (iota((rows, LANES), 1) - OWN) // 2 + OWN


def coarse12(total):
    pairs = total + roll(total, -1, 1)
    return 0.5 * pick(pairs, pair_index(Y2))


def down12(f1, i1, b1, f2, i2, v2, red, begin, end):
    def first(p):
        red[p] = f1[p, 0] * i1[p, 0]

    loop(begin, end, first, 4)

    def black(p, parity):
        b1[p] = (f1[p, 1] + sum1(red, p, parity, False)) * i1[p, 1]

    black(begin + 1, 1)
    plane_pairs(begin + 2, end - 2, black)
    black(end - 2, 0)

    def restrict(i):
        plane = 2 * i + 2
        f2[i] = coarse12(sum1(b1, plane, 0, True) + sum1(b1, plane + 1, 1, True))

    begin2, end2 = begin // 2, end // 2 - 2
    loop(begin2, end2, restrict, 4)

    def red2(p):
        v2[p] = jnp.where(is_red((Y2, LANES), p), f2[p] * i2[p], 0.0)

    def black2(p):
        fresh = (f2[p] + sum2(v2, p)) * i2[p]
        v2[p] = jnp.where(is_red((Y2, LANES), p), v2[p], fresh)

    loop(begin2, end2, red2, 4)
    loop(begin2 + 1, end2 - 1, black2, 3)


def coarse23(total, sums, x3):
    sums[x3] = total
    pairs = sums[x3, pl.ds(8, 8, stride=2), :] + sums[x3, pl.ds(9, 8, stride=2), :]
    pairs = pairs + roll(pairs, -1, 1)
    lane = iota((8, LANES), 1)
    spread = pick(pairs, OWN + 2 * (lane % 16))
    here = lane // 16 == (x3 % 2) * 4 + iota((8, LANES), 0)
    here = jnp.logical_and(here, iota((8, LANES), 0) < 4)
    return 0.5 * jnp.sum(jnp.where(here, spread, 0.0), axis=0, keepdims=True)


def source3(v2, sums):
    rows = []
    for x3 in range(4):
        plane = 2 * x3 + H2
        total = jnp.zeros((Y2, LANES), F32)
        for p in (plane, plane + 1):
            total += jnp.where(is_red((Y2, LANES), p), sum2(v2, p), 0.0)
        rows.append(coarse23(total, sums, x3))
    return [rows[0] + rows[1], rows[2] + rows[3]]


def screens12(coloured, from_low, from_high, matrices, f1, i1, i2, begin, end):
    def store(plane, colour, halves):
        f1[plane, colour], i1[plane, colour] = halves

    unpack1(coloured, from_low, from_high, matrices, store, begin, end)

    def screen2(i):
        plane = 2 * i + 2
        total = i1[plane, 0] + i1[plane, 1] + i1[plane + 1, 0] + i1[plane + 1, 1]
        i2[i] = coarse12(total)

    loop(begin // 2, end // 2 - 2, screen2, 4)


def invert12(i1, i2, begin, end):
    def invert1(p):
        i1[p] = 1.0 / (6.0 + i1[p])

    def invert2(p):
        i2[p] = 1.0 / (6.0 + i2[p])

    loop(begin, end, invert1, 4)
    loop(begin // 2, end // 2 - 2, invert2, 4)


def first_message(
    coloured, from_low, from_high, matrices, message, f1, i1, b1, f2, i2, v2, red, sums, _
):
    screens12(coloured, from_low, from_high, matrices, f1, i1, i2, BEGIN, END)
    rows = []
    for x3 in range(4):
        plane = 2 * x3 + H2
        rows.append(coarse23(i2[plane] + i2[plane + 1], sums, x3))
    invert12(i1, i2, BEGIN, END)
    down12(f1, i1, b1, f2, i2, v2, red, BEGIN, END)
    tile = source3(v2, sums) + [rows[0] + rows[1], rows[2] + rows[3]]
    tile = jnp.concatenate(tile + tile, axis=0)
    for i in range(64):
        message[8 * i : 8 * i + 8, :] = tile


def down12_first(
    coloured, from_low, from_high, matrices, f1, i1, b1, f2, i2, v2, red, copies
):
    screens12(coloured, from_low, from_high, matrices, f1, i1, i2, 0, X1)
    invert12(i1, i2, 0, X1)
    for at in (4, 5, 8):
        copies[at].start()
    down12(f1, i1, b1, f2, i2, v2, red, 0, X1)
    for at in (6, 7, 9):
        copies[at].start()


def sources12(coloured, from_low, from_high, matrices, f1):
    def store(item, colour, halves):
        block, i = divmod(item, 8)
        for half in (0, 1):
            plane = H1 + 16 * (block - 1) + 8 * half + i
            if 0 <= plane < X1:
                f1[plane, colour] = halves[half]

    unpack1(coloured, from_low, from_high, matrices, store, 0, 24)


def down12_next(
    coloured, from_low, from_high, matrices, i1, i2, f1, b1, f2, v2, message, red, sums, copies
):
    sources12(coloured, from_low, from_high, matrices, f1)
    for at in (4, 5):
        copies[at].wait()
    down12(f1, i1, b1, f2, i2, v2, red, 0, X1)
    tile = jnp.concatenate(source3(v2, sums) * 4, axis=0)
    for i in range(32):
        message[8 * i : 8 * i + 8, :] = tile


def unpack3(message, rows, first, into):
    sub, lane = iota((8, LANES), 0), iota((8, LANES), 1)
    for gx in range(4):
        for gy in range(4):
            for half in range(2):
                start = (gx * 4 + gy) * 8 * rows + first + half
                value = message[pl.ds(start, 8, stride=rows), :]
                for k in (1, 2, 4):
                    sub_high = (sub // k) % 2 == 1
                    lane_high = (lane // (16 * k)) % 2 == 1
                    from_below = roll(roll(value, -k, 0), 16 * k, 1)
                    from_above = roll(roll(value, k, 0), -16 * k, 1)
                    value = jnp.where(
                        sub_high == lane_high, value, jnp.where(sub_high, from_above, from_below)
                    )
                for x in range(2):
                    into[gx * 4 + 2 * half + x, gy * 4 : gy * 4 + 4, :] = value[4 * x : 4 * x + 4, :]


def turn(value, shift, axis):
    if axis == 0:
        return jnp.concatenate([value[-shift:], value[:-shift]], axis=0)
    return roll(value, shift, axis)


def sum_whole(value):
    total = turn(value, 1, 0) + turn(value, -1, 0)
    total = total + turn(value, 1, 1) + turn(value, -1, 1)
    return total + turn(value, 1, 2) + turn(value, -1, 2)


def red_whole(shape):
    return (iota(shape, 0) + iota(shape, 1) + iota(shape, 2)) % 2 == 0


def pick3(value, index):
    flat = value.reshape(-1, LANES)
    return pick(flat, jnp.broadcast_to(index, flat.shape)).reshape(value.shape)


def coarse34(value, wide):
    wide[...] = value.reshape(8, 2, 16, LANES).sum(axis=1)
    pairs = wide[:, pl.ds(0, 8, stride=2), :] + wide[:, pl.ds(1, 8, stride=2), :]
    pairs = pairs + roll(pairs, -1, 2)
    return 0.5 * pick3(pairs, 2 * (iota((1, LANES), 1) % 64))


def coarse_solve(f3, i3, i4, place, inverse, e3, wide):
    red3, red4 = red_whole((16, 16, LANES)), red_whole((8, 8, LANES))
    v3 = jnp.where(red3, f3 * i3, 0.0)
    v3 = jnp.where(red3, v3, (f3 + sum_whole(v3)) * i3)
    f4 = coarse34(jnp.where(red3, sum_whole(v3), 0.0), wide)
    v4 = jnp.where(red4, f4 * i4, 0.0)
    v4 = jnp.where(red4, v4, (f4 + sum_whole(v4)) * i4)
    r4 = jnp.where(red4, sum_whole(v4), 0.0).reshape(4, 2, 8, LANES).sum(axis=1)
    sub, lane = iota((8, LANES), 0), iota((8, LANES), 1)
    rows = []
    for x5 in range(4):
        pairs = r4[x5] + roll(r4[x5], -1, 1)
        spread = jnp.where(sub // 2 == lane // 32, pick(pairs, 2 * (lane % 32)), 0.0)
        rows.append(0.5 * jnp.sum(spread, axis=0, keepdims=True))
    vector = jnp.broadcast_to(jnp.concatenate(rows, axis=1), (8, 512))
    answer = lax.dot_general(
        vector,
        jnp.concatenate([ref[...] for ref in inverse] + [jnp.zeros((64, 512), F32)], axis=0),
        (((1,), (1,)), ((), ())),
        precision=lax.Precision.HIGHEST,
        preferred_element_type=F32,
    )
    planes = []
    for x5 in range(4):
        z5 = lane % 64 // 2
        index = (place[0] + 4 - x5) % 4 * 16 + (place[1] + 4 - sub // 2) % 4 * 4 + z5 % 4
        apart = (z5 // 4 + 8 - place[2]) % 8
        same = pick(answer[:, :LANES], index + jnp.where(apart == 7, 64, 0))
        part = jnp.where(apart == 1, pick(answer[:, LANES:], index), same)
        part = jnp.where(jnp.logical_or(apart <= 1, apart == 7), part, 0.0)
        planes += [part[None], part[None]]
    w4 = v4 + jnp.concatenate(planes, axis=0)
    w4 = jnp.where(red4, (f4 + sum_whole(w4)) * i4, w4)
    e4 = jnp.where(red4, w4, (f4 + sum_whole(w4)) * i4)
    e4 = pick3(e4, iota((1, LANES), 1) // 2)
    wide[:, pl.ds(0, 8, stride=2), :] = e4
    wide[:, pl.ds(1, 8, stride=2), :] = e4
    spread = jnp.broadcast_to(wide[...][:, None], (8, 2, 16, LANES)).reshape(16, 16, LANES)
    w3 = v3 + spread
    w3 = jnp.where(red3, (f3 + sum_whole(w3)) * i3, w3)
    e3[...] = jnp.where(red3, w3, (f3 + sum_whole(w3)) * i3)


def up21(place, e3, f2, i2, v2, f1, i1, b1, e2, er, eb, tall):
    shift_y = lax.rem(20 - 4 * place[1], 16)
    shift_z = lax.rem(160 - 16 * place[2], 128)

    def from3(i):
        value = e3[lax.rem(4 * place[0] + i + 13, 16)]
        value = pltpu.roll(pltpu.roll(value, shift_y, 0), shift_z, 1)
        value = pick(value, spread_index(16))[:12]
        tall[i, pl.ds(0, 12, stride=2), :] = value
        tall[i, pl.ds(1, 12, stride=2), :] = value
        value = tall[i]
        e2[2 * i] = v2[2 * i] + value
        e2[2 * i + 1] = v2[2 * i + 1] + value

    loop(0, X2 // 2, from3, 5)

    def red2(p):
        fresh = (f2[p] + sum2(e2, p)) * i2[p]
        e2[p] = jnp.where(is_red((Y2, LANES), p), fresh, e2[p])

    def black2(p):
        fresh = (f2[p] + sum2(e2, p)) * i2[p]
        e2[p] = jnp.where(is_red((Y2, LANES), p), e2[p], fresh)

    loop(1, X2 - 1, red2, 3)
    loop(2, X2 - 2, black2, 4)

    def from2(i):
        value = pick(e2[i], spread_index(Y2))
        eb[2 * i + 2] = b1[2 * i + 2] + value
        eb[2 * i + 3] = b1[2 * i + 3] + value

    loop(3, 17, from2, 7)

    def red1(p, parity):
        er[p] = (f1[p, 0] + sum1(eb, p, parity, True)) * i1[p, 0]

    def black1(p, parity):
        eb[p] = (f1[p, 1] + sum1(er, p, parity, False)) * i1[p, 1]

    plane_pairs(8, 36, red1)
    plane_pairs(10, 34, black1)


def add0(er, eb, b, w, tall):
    def from1(i):
        reds, blacks = er[i + 10, 6:18], eb[i + 10, 6:18]
        here = (iota((12, LANES), 1) + i) % 2 == 0
        tall[i, pl.ds(0, 12, stride=2), :] = jnp.where(here, reds, blacks)
        tall[i, pl.ds(1, 12, stride=2), :] = jnp.where(here, blacks, reds)
        value = tall[i]
        for p in (2 * i, 2 * i + 1):
            for q in (0, 1):
                w[p, q] = b[p, q] + value

    loop(0, X0 // 2, from1, 4)


def own_sum(total):
    row, lane = iota((24, LANES), 0), iota((24, LANES), 1)
    own = jnp.logical_and((row + 20) % 24 < 16, (lane + 128 - OWN) % LANES < 64)
    return jnp.sum(jnp.where(own, total, 0.0), axis=0, keepdims=True)


def sum_over(body):
    def step(i, total):
        return total + body(2 * i, 0) + body(2 * i + 1, 1)

    return lax.fori_loop(H0 // 2, H0 // 2 + 16, step, jnp.zeros((24, LANES), F32), unroll=2)


def middle(
    message, place, near, before, after, f2, i2, v2, f1, i1, b1, fr, fb, ir, ib, vb,
    i3, i4, bnew, own1, norm,
    f3, e3, wide, tall, e2, er, eb, w, r, rnew, copies,
):
    unpack3(message, 4, 0, f3)
    unpack3(message, 4, 2, e3)
    screen3 = e3[...]
    screen4 = coarse34(screen3, wide)
    i3[...] = 1.0 / (6.0 + screen3)
    i4[...] = 1.0 / (6.0 + screen4)
    coarse_solve(f3[...], i3[...], i4[...], place, (near, before, after), e3, wide)
    for at in range(5, 11):
        copies[at].wait()
    up21(place, e3, f2, i2, v2, f1, i1, b1, e2, er, eb, tall)
    for at in range(11, 16):
        copies[at].wait()
    add0(er, eb, vb, w, tall)

    def red_up(p, parity):
        for q in (0, 1):
            r[p, q] = (fr[p, q] + sum0(w, p, parity, q, True)) * ir[p, q]

    plane_pairs(2, X0 - 2, red_up)

    def black_up(p, parity):
        for q in (0, 1):
            w[p, q] = (fb[p, q] + sum0(r, p, parity, q, False)) * ib[p, q]

    black_up(3, 1)
    plane_pairs(4, X0 - 4, black_up)
    black_up(X0 - 4, 0)

    def red_down(p, parity):
        for q in (0, 1):
            rnew[p, q] = (fr[p, q] + sum0(w, p, parity, q, True)) * ir[p, q]

    plane_pairs(4, X0 - 4, red_down)

    def squares(p, parity):
        total = jnp.zeros((24, LANES), F32)
        for q in (0, 1):
            part = (rnew[p, q] - r[p, q]) / ir[p, q]
            total = total + part * part
        return total

    norm[...] = jnp.broadcast_to(own_sum(sum_over(squares)), (8, LANES))

    def black_down(p, parity):
        for q in (0, 1):
            fresh = (fb[p, q] + sum0(rnew, p, parity, q, False)) * ib[p, q]
            bnew[p, q] = fresh
            r[p, q] = fresh - w[p, q]

    black_down(5, 1)
    plane_pairs(6, X0 - 6, black_down)
    black_down(X0 - 6, 0)

    def restrict(i):
        low = 0.5 * below_sum(r, 2 * i + H0)[4:20]
        high = 0.5 * below_sum(r, 2 * i + H0 + 16)[4:20]
        own = (iota((16, LANES), 1) + 128 - OWN) % LANES < 64
        own1[i] = jnp.where(own, low, roll(high, 64, 1))

    loop(0, 8, restrict)


def final(
    message, place, near, before, after, f2, i2, v2, f1, i1, b1, fr, fb, ir, ib, b, i3, i4,
    norm,
    sums, r, last,
    f3, e3, wide, tall, e2, er, eb, w, copies,
):
    unpack3(message, 2, 0, f3)
    coarse_solve(f3[...], i3[...], i4[...], place, (near, before, after), e3, wide)
    for at in (6, 9):
        copies[at].wait()
    up21(place, e3, f2, i2, v2, f1, i1, b1, e2, er, eb, tall)
    for at in range(11, 15):
        copies[at].wait()
    add0(er, eb, b, w, tall)

    def red_up(p, parity):
        for q in (0, 1):
            r[p, q] = (fr[p, q] + sum0(w, p, parity, q, True)) * ir[p, q]

    plane_pairs(6, X0 - 6, red_up)

    def black_up(p, parity):
        for q in (0, 1):
            fresh = (fb[p, q] + sum0(r, p, parity, q, False)) * ib[p, q]
            last[p, q] = fresh
            w[p, q] = fresh - w[p, q]

    black_up(7, 1)
    plane_pairs(8, X0 - 8, black_up)
    black_up(X0 - 8, 0)

    def squares(p, parity):
        total = jnp.zeros((24, LANES), F32)
        for q in (0, 1):
            part = sum0(w, p, parity, q, True)
            total = total + part * part
        return total

    squared = own_sum(sum_over(squares))

    low = iota((1, LANES), 1) < 64
    both = jnp.where(low, roll(norm[0:1, :], -OWN, 1), roll(squared, 64 - OWN, 1))
    for i in range(16):
        sums[8 * i : 8 * i + 8, :] = jnp.broadcast_to(both, (8, LANES))


def weave(r, last, matrix, field, _):
    def finish(i):
        parts = []
        for x in (0, 1):
            for q in (0, 1):
                order = (r, last) if x == q else (last, r)
                parts.append(jnp.concatenate([ref[2 * i + x, q] for ref in order], axis=1))
        result = move([thirds(jnp.concatenate(parts, axis=0))], matrix[...])
        for at in range(4):
            rows = result[24 * at + 4 : 24 * at + 20]
            field[2 * i + at // 2 - H0, pl.ds(at % 2, 16, stride=2), :] = rows

    loop(H0 // 2, H0 // 2 + 16, finish)


def exchange(to_high, to_low, axis):
    count = lax.axis_size(axis)
    up = [(i, (i + 1) % count) for i in range(count)]
    down = [(j, i) for i, j in up]
    return lax.ppermute(to_high, axis, up), lax.ppermute(to_low, axis, down)


def from_all(own, axis):
    count = lax.axis_size(axis)
    shifts = [[(i, (i + k) % count) for i in range(count)] for k in range(1, count)]
    return [lax.ppermute(own, axis, shift) for shift in shifts]


def together(first, second):
    both = lax.optimization_barrier((*first, *second))
    return both[: len(first)], both[len(first) :]


def exchange1(own, low, high, beside=()):
    from_low, from_high = exchange(high, low, "gx")
    own = jnp.concatenate([from_low, own, from_high], axis=0)
    below, above = exchange(own, own, "gy")
    if beside:
        (above,), beside = together((above,), exchange(*beside, "gz"))
    items = own.shape[0]
    message = (items // GROUP1, 2, 24, LANES)
    coloured, to_high, to_low = call(
        pack_z1, [(items, 2, 24, LANES), message, message], own, below, above
    )
    return (coloured, *exchange(to_high, to_low, "gz")), beside


def local(f, s, coarse_inverse):
    place = jnp.stack([lax.axis_index(axis) for axis in AXES]).astype(jnp.int32)
    low, high = exchange(
        jnp.concatenate([f[32 - H0 :], s[32 - H0 :]], axis=0),
        jnp.concatenate([f[:H0], s[:H0]], axis=0),
        "gx",
    )
    messages = call(pack_y0, [(2 * X0, 8, LANES)] * 2, f, s, low, high)
    messages, others = together(messages, from_all(coarse_inverse, "gy"))
    inverse = jnp.concatenate([coarse_inverse, *others], axis=0)
    below, above = exchange(*messages, "gy")
    (below, above), others = together((below, above), from_all(inverse, "gx"))
    inverse = jnp.concatenate([inverse, *others], axis=0)
    groups = 2 * X0 // GROUP0
    line0, line1, line2 = (Y0, LANES), (24, LANES), (Y2, LANES)
    split, to_high, to_low = call(
        pack_z0,
        [(2 * X0, *line0), (groups // 2, *line0), (groups // 2, *line0)],
        *(f, s, low, high, below, above),
        scratch=[(16, *line0)],
    )
    level0, level1, level2 = (X0, 2, *line1), (X1, *line1), (X2, *line2)
    both1 = (X1, 2, *line1)
    matrices1 = jnp.asarray(halo_matrices1(), jnp.bfloat16)
    fr, fb, ir, ib, vb, own1 = call(
        down0,
        [Parked(level0, lambda ref, k=k: ref.at[k]) for k in range(5)] + [(16, 16, LANES)],
        split,
        *exchange(to_high, to_low, "gz"),
        jnp.asarray(lower_matrices(), jnp.bfloat16),
        scratch=[level0, (X0, *line1)],
        park=(56, *level0),
    )
    level1_parts, others = exchange1(own1, own1[:H1], own1[16 - H1 :], (inverse, inverse))
    inverse = (inverse, *others)
    (message,) = call(
        first_message,
        [(512, LANES)],
        *level1_parts,
        matrices1,
        scratch=[both1, both1, level1, level2, level2, level2, level1, (4, *line2)],
    )
    message = lax.all_to_all(message, AXES, 0, 0, tiled=True)
    f1, i1, b1, f2, i2, v2 = call(
        down12_first,
        [
            Parked(both1, lambda ref: ref.at[0]),
            Parked(both1, lambda ref: ref.at[1]),
            Parked(level1, lambda ref: ref.at[2, :, 0]),
            Parked(level2, lambda ref: ref.at[2, 0:X2, 1]),
            Parked(level2, lambda ref: ref.at[3, 0:X2, 0]),
            Parked(level2, lambda ref: ref.at[3, 0:X2, 1]),
        ],
        *level1_parts,
        matrices1,
        scratch=[level1],
        park=(60, *both1),
    )
    whole = (16, 16, LANES)
    work = [whole, whole, (8, 16, LANES), (X0 // 2, *line1), level2, level1, level1]
    work += [level0, level0, level0]
    i3, i4, bnew, own1, norm = call(
        middle,
        [whole, (8, 8, LANES), level0, (8, 16, LANES), (8, LANES)],
        message, place, *inverse, f2, i2, v2, f1, i1, b1, fr, fb, ir, ib, vb,
        scratch=work,
    )
    f1, b1, f2, v2, message = call(
        down12_next,
        [both1, level1, level2, level2, (256, LANES)],
        *exchange1(own1, own1, own1)[0],
        matrices1,
        i1,
        i2,
        scratch=[level1, (4, *line2)],
    )
    message = lax.all_to_all(message, AXES, 0, 0, tiled=True)
    sums, red, black = call(
        final,
        [(128, LANES), level0, level0],
        message, place, *inverse, f2, i2, v2, f1, i1, b1, fr, fb, ir, ib, bnew, i3, i4, norm,
        scratch=work[:-2],
    )
    sums = lax.all_to_all(sums, AXES, 0, 0, tiled=True)
    matrix = jnp.asarray(upper_matrix(), jnp.bfloat16)
    (field,) = call(weave, [(32, 32, LANES)], red, black, matrix)
    squares = jnp.sum(sums.reshape(128, 2, 64), axis=(0, 2))
    return field, jnp.sqrt(squares / CELLS)


def solution(mesh):
    return jax.shard_map(
        local,
        mesh=mesh,
        in_specs=(P("gx", "gy", "gz"), P("gx", "gy", "gz"), P(("gx", "gy", "gz"), None)),
        out_specs=(P("gx", "gy", "gz"), P()),
        check_vma=False,
    )
```

```python
import jax
import jax.numpy as jnp
import numpy as np
from jax import lax
from jax.experimental import pallas as pl
from jax.experimental.pallas import tpu as pltpu
from jax.sharding import PartitionSpec as P

AXES = ("gx", "gy", "gz")
F32 = jnp.float32
LANES = 128
OWN = 32
H0 = 8
X0, Y0 = 48, 48
H1 = 14
X1, Y1 = 44, 48
H2 = 6
X2, Y2 = 20, 24
GROUP0 = 8
GROUP1 = 4
BEGIN, END = 8, 36
CELLS = 16777216.0


def iota(shape, dim):
    return lax.broadcasted_iota(jnp.int32, shape, dim)


def roll(value, shift, axis):
    return pltpu.roll(value, shift % value.shape[axis], axis)


def pick(value, index):
    return jnp.take_along_axis(value, index, axis=1, mode="promise_in_bounds")


def loop(start, stop, body, unroll=2):
    def step(index, carry):
        body(index)
        return carry

    lax.fori_loop(start, stop, step, 0, unroll=unroll)


class Parked:
    def __init__(self, shape, place, whole=None):
        self.shape, self.place, self.whole = shape, place, whole

    def of(self, whole):
        return Parked(self.shape, self.place, whole)


def call(body, outs, *operands, scratch=(), park=None):
    inputs, input_at = [], []
    for operand in operands:
        array = operand.whole if isinstance(operand, Parked) else operand
        at = next((k for k, other in enumerate(inputs) if other is array), len(inputs))
        if at == len(inputs):
            inputs.append(array)
        input_at.append(at)
    far = [isinstance(item, Parked) for item in (*operands, *outs)]
    parked = [item for item in (*operands, *outs) if isinstance(item, Parked)]
    near_outs = [shape for shape in outs if not isinstance(shape, Parked)]
    far_arrays = [operand.whole for operand in operands if isinstance(operand, Parked)]

    def kernel(*refs):
        refs = list(refs)
        ins = [refs.pop(0) for _ in inputs]
        near = [refs.pop(0) for _ in near_outs]
        store = refs.pop(0) if park else None
        semaphores = refs.pop() if parked else None
        work, nears = refs[: len(scratch)], refs[len(scratch) :]
        ready, copies = [], {}
        for at, item in enumerate((*operands, *outs)):
            inward = at < len(operands)
            if far[at]:
                ref = nears.pop(0)
                place = item.place(ins[input_at[at]] if inward else store)
                ends = (place, ref) if inward else (ref, place)
                copies[at] = pltpu.make_async_copy(*ends, semaphores.at[len(copies)])
                if inward:
                    copies[at].start()
            else:
                ref = ins[input_at[at]] if inward else near.pop(0)
            ready.append(ref)
        body(*ready, *work, copies)
        for at in range(len(operands), len(far)):
            if far[at]:
                copies[at].wait()

    def spec(array):
        if any(array is other for other in far_arrays):
            return pl.BlockSpec(memory_space=pl.ANY)
        return pl.BlockSpec(memory_space=pltpu.SMEM if array.dtype == jnp.int32 else pltpu.VMEM)

    shapes = near_outs + ([park] if park else [])
    spaces = [pltpu.VMEM] * len(near_outs) + ([pl.ANY] if park else [])
    work = [pltpu.VMEM(shape, F32) for shape in scratch]
    work += [pltpu.VMEM(item.shape, F32) for item in parked]
    if parked:
        work.append(pltpu.SemaphoreType.DMA((len(parked),)))
    results = pl.pallas_call(
        kernel,
        out_shape=[jax.ShapeDtypeStruct(shape, F32) for shape in shapes],
        in_specs=[spec(array) for array in inputs],
        out_specs=[pl.BlockSpec(memory_space=space) for space in spaces],
        scratch_shapes=work,
        compiler_params=pltpu.CompilerParams(vmem_limit_bytes=20 * 1024 * 1024),
    )(*inputs)
    results = list(results)
    whole = results.pop() if park else None
    return [out.of(whole) if isinstance(out, Parked) else results.pop(0) for out in outs]


def lower_matrices():
    matrices = np.zeros((GROUP0, 256, 256), np.float32)
    for k in range(GROUP0):
        for z in range(-8, 136):
            if 0 <= z < 128:
                row = z
            elif z < 0:
                row = 128 + (16 * k + z) % 128
            else:
                row = 128 + 16 * k + z - 128
            matrices[k, row, 128 * (z % 2) + OWN + z // 2] = 1.0
    return matrices


def upper_matrix():
    matrix = np.zeros((256, 128), np.float32)
    for z in range(128):
        matrix[128 * (z % 2) + OWN + z // 2, z] = 1.0
    return matrix


def halo_matrices1():
    matrices = np.zeros((GROUP1, 384, 256), np.float32)
    for k in range(GROUP1):
        for half in (0, 1):
            for z in range(-H1, 64 + H1):
                if 0 <= z < 64:
                    row = (OWN + 64 * half + z) % 128
                elif z < 0:
                    row = 128 + 64 * half + 14 * k + z + H1
                else:
                    row = 256 + 64 * half + 14 * k + z - 64
                matrices[k, row, 128 * half + OWN + z] = 1.0
    return matrices


def thirds(value):
    high = value.astype(jnp.bfloat16)
    rest = value - high.astype(F32)
    mid = rest.astype(jnp.bfloat16)
    return (rest - mid.astype(F32)).astype(jnp.bfloat16), mid, high


def halves(value):
    high = value.astype(jnp.bfloat16)
    return (value - high.astype(F32)).astype(jnp.bfloat16), high


def move(pieces, matrix):
    total = None
    for parts in zip(*pieces):
        left = parts[0] if len(parts) == 1 else jnp.concatenate(parts, axis=1)
        term = jnp.dot(left, matrix, preferred_element_type=F32)
        total = term if total is None else total + term
    return total


def plane_pairs(first, last, body, unroll=4):
    def both(i):
        body(2 * i, 0)
        body(2 * i + 1, 1)

    loop(first // 2, last // 2, both, unroll)


def sum0(values, plane, parity, q, onto_red):
    mid, other = values[plane, q], values[plane, 1 - q]
    total = values[plane + 1, q] + values[plane - 1, q] + mid
    total = total + other + roll(other, 1 if q == 0 else -1, 0)
    high = ((parity + q) % 2 == 1) == onto_red
    return total + roll(mid, -1 if high else 1, 1)


def even_lanes(shape, parity):
    return (iota(shape, 1) + parity) % 2 == 0


def sum1(values, plane, parity, onto_red):
    mid = values[plane]
    total = values[plane + 1] + values[plane - 1] + mid
    total = total + roll(mid, 1, 1) + roll(mid, -1, 1)
    less, more = roll(mid, 1, 0), roll(mid, -1, 0)
    first, second = (less, more) if onto_red else (more, less)
    return total + jnp.where(even_lanes(mid.shape, parity), first, second)


def sum2(values, plane):
    mid = values[plane]
    total = values[plane + 1] + values[plane - 1]
    total = total + roll(mid, 1, 0) + roll(mid, -1, 0)
    return total + roll(mid, 1, 1) + roll(mid, -1, 1)


def is_red(shape, plane):
    return (iota(shape, 0) + iota(shape, 1) + plane) % 2 == 0


TILES = 40


def pack_y0(f, s, low, high, to_high, to_low, _):
    row = iota((8, LANES), 0)
    for field, own in enumerate((f, s)):
        at = field * TILES
        to_high[at : at + 32] = own[:, 24:32]
        to_low[at : at + 32] = own[:, 0:8]
        for side, halo in enumerate((low, high)):
            first = field * H0 + (H0 if side == 0 else -1)
            step = -1 if side == 0 else 1
            for dx in range(1, 5):
                near, far = first + step * dx, first + step * (8 - dx)
                tile = at + 32 + 4 * side + dx - 1
                above = roll(halo[far, 24:32], dx, 0)
                to_high[tile] = jnp.where(row >= dx, halo[near, 24:32], above)
                below = roll(halo[far, 0:8], 8 - dx, 0)
                to_low[tile] = jnp.where(row < 8 - dx, halo[near, 0:8], below)


def rows_y0(tiles, field, plane, above):
    at = field * TILES
    if H0 <= plane < H0 + 32:
        return tiles[at + plane - H0]
    side = 0 if plane < H0 else 1
    dx = H0 - plane if side == 0 else plane - H0 - 31
    tile = at + 31 + 4 * side
    if dx <= 4:
        return tiles[tile + dx]
    near = max(8 - dx, 1)
    return roll(tiles[tile + near], near - 8 if above else -near, 0)


def pack_z0(f, s, low, high, below, above, split, to_high, to_low, rows, _):
    lane = iota((Y0, LANES), 1)
    block = (lane + 8) % LANES // 16
    last = lane // 8 % 2 == 1
    pair = []
    for group in range(2 * X0 // GROUP0):
        packed = jnp.zeros((Y0, LANES), F32)
        for k in range(GROUP0):
            item = group * GROUP0 + k
            field, plane = divmod(item, X0)
            own = (f, s)[field]
            slot = item % 16
            rows[slot, 0:8, :] = rows_y0(below, field, plane, False)
            if plane < H0:
                rows[slot, 8:40, :] = low[field * H0 + plane]
            elif plane < H0 + 32:
                rows[slot, 8:40, :] = own[plane - H0]
            else:
                rows[slot, 8:40, :] = high[field * H0 + plane - H0 - 32]
            rows[slot, 40:48, :] = rows_y0(above, field, plane, True)
            even = rows[slot, pl.ds(0, 24, stride=2), :]
            odd = rows[slot, pl.ds(1, 24, stride=2), :]
            value = jnp.concatenate([even, odd], axis=0)
            split[item] = value
            packed = jnp.where(block == k, roll(value, 16 * k, 1), packed)
        pair.append(packed)
        if len(pair) == 2:
            to_high[group // 2] = jnp.where(last, pair[0], roll(pair[1], 8, 1))
            to_low[group // 2] = jnp.where(last, roll(pair[1], -8, 1), pair[0])
            pair = []


def down0(split, from_low, from_high, matrices, fr, fb, ir, ib, vb, own1, red, screen, copies):
    lane = iota((Y0, LANES), 1)
    groups = 2 * X0 // GROUP0
    merged = []
    for half in range(groups // 2):
        left, right = from_low[half], from_high[half]
        merged.append(jnp.where(lane // 8 % 2 == 1, left, right))
        merged.append(jnp.where(lane // 8 % 2 == 1, roll(left, -8, 1), roll(right, 8, 1)))
    merged = halves(jnp.concatenate(merged, axis=0))
    for k in range(GROUP0):
        own = [split[group * GROUP0 + k] for group in range(groups)]
        result = move([halves(jnp.concatenate(own, axis=0)), merged], matrices[k])
        for group in range(groups):
            field, plane = divmod(group * GROUP0 + k, X0)
            part = result[Y0 * group : Y0 * group + Y0]
            even, odd = part[:, :LANES], part[:, LANES:]
            if field == 1:
                screen[plane] = even[:24] + odd[:24] + even[24:] + odd[24:]
            for q in (0, 1):
                reds, blacks = (even, odd) if (k + q) % 2 == 0 else (odd, even)
                reds, blacks = reds[24 * q : 24 * q + 24], blacks[24 * q : 24 * q + 24]
                if field == 0:
                    fr[plane, q] = reds
                    fb[plane, q] = blacks
                else:
                    ir[plane, q] = 1.0 / (6.0 + reds)
                    ib[plane, q] = 1.0 / (6.0 + blacks)

    for at in range(4, 8):
        copies[at].start()

    def first(p):
        red[p] = fr[p] * ir[p]

    loop(0, X0, first, 4)

    def black(p, parity):
        for q in (0, 1):
            vb[p, q] = (fb[p, q] + sum0(red, p, parity, q, False)) * ib[p, q]

    black(1, 1)
    plane_pairs(2, X0 - 2, black)
    black(X0 - 2, 0)
    copies[8].start()

    def restrict(i):
        plane = 2 * i + H0
        source = 0.5 * below_sum(vb, plane)
        own = (iota((16, LANES), 1) + 128 - OWN) % LANES < 64
        screens = 0.5 * (screen[plane] + screen[plane + 1])[4:20]
        own1[i] = jnp.where(own, source[4:20], roll(screens, 64, 1))

    loop(0, 16, restrict)


def below_sum(values, plane):
    total = sum0(values, plane, 0, 0, True) + sum0(values, plane, 0, 1, True)
    total = total + sum0(values, plane + 1, 1, 0, True)
    return total + sum0(values, plane + 1, 1, 1, True)


def pack_z1(own, below, above, coloured, to_high, to_low, _):
    block = iota((24, LANES), 1) % 64 // 14
    for group in range(own.shape[0] // GROUP1):
        up = [jnp.zeros((24, LANES), F32)] * 2
        down = [jnp.zeros((24, LANES), F32)] * 2
        for k in range(GROUP1):
            item = group * GROUP1 + k
            even, odd = [
                jnp.concatenate([ref[item, pl.ds(q, 8, stride=2), :] for ref in (below, own, above)], axis=0)
                for q in (0, 1)
            ]
            here = even_lanes((24, LANES), item)
            for colour in (0, 1):
                first, second = (even, odd) if colour == 0 else (odd, even)
                value = jnp.where(here, first, second)
                coloured[item, colour] = value
                up[colour] = jnp.where(block == k, roll(value, 14 * k - 82, 1), up[colour])
                down[colour] = jnp.where(block == k, roll(value, 14 * k - 32, 1), down[colour])
        for colour in (0, 1):
            to_high[group, colour] = up[colour]
            to_low[group, colour] = down[colour]


def unpack1(coloured, from_low, from_high, matrices, store, first, last):
    groups = range(first // GROUP1, last // GROUP1)
    rows = len(groups) * 48
    halos = [
        halves(ref[groups.start : groups.stop].reshape(rows, LANES))
        for ref in (from_low, from_high)
    ]
    for k in range(GROUP1):
        own = [coloured[GROUP1 * g + k, colour] for g in groups for colour in (0, 1)]
        result = move([halves(jnp.concatenate(own, axis=0)), *halos], matrices[k])
        for at in range(2 * len(groups)):
            part = result[24 * at : 24 * at + 24]
            item = GROUP1 * groups[at // 2] + k
            store(item, at % 2, (part[:, :LANES], part[:, LANES:]))


def pair_index(rows):
    return jnp.clip(2 * iota((rows, LANES), 1) - OWN, 0, 127)


def spread_index(rows):
    return (iota((rows, LANES), 1) - OWN) // 2 + OWN


def coarse12(total):
    pairs = total + roll(total, -1, 1)
    return 0.5 * pick(pairs, pair_index(Y2))


def down12(f1, i1, b1, f2, i2, v2, red, begin, end):
    def first(p):
        red[p] = f1[p, 0] * i1[p, 0]

    loop(begin, end, first, 4)

    def black(p, parity):
        b1[p] = (f1[p, 1] + sum1(red, p, parity, False)) * i1[p, 1]

    black(begin + 1, 1)
    plane_pairs(begin + 2, end - 2, black)
    black(end - 2, 0)

    def restrict(i):
        plane = 2 * i + 2
        f2[i] = coarse12(sum1(b1, plane, 0, True) + sum1(b1, plane + 1, 1, True))

    begin2, end2 = begin // 2, end // 2 - 2
    loop(begin2, end2, restrict, 4)

    def red2(p):
        v2[p] = jnp.where(is_red((Y2, LANES), p), f2[p] * i2[p], 0.0)

    def black2(p):
        fresh = (f2[p] + sum2(v2, p)) * i2[p]
        v2[p] = jnp.where(is_red((Y2, LANES), p), v2[p], fresh)

    loop(begin2, end2, red2, 4)
    loop(begin2 + 1, end2 - 1, black2, 3)


def coarse23(total, sums, x3):
    sums[x3] = total
    pairs = sums[x3, pl.ds(8, 8, stride=2), :] + sums[x3, pl.ds(9, 8, stride=2), :]
    pairs = pairs + roll(pairs, -1, 1)
    lane = iota((8, LANES), 1)
    spread = pick(pairs, OWN + 2 * (lane % 16))
    here = lane // 16 == (x3 % 2) * 4 + iota((8, LANES), 0)
    here = jnp.logical_and(here, iota((8, LANES), 0) < 4)
    return 0.5 * jnp.sum(jnp.where(here, spread, 0.0), axis=0, keepdims=True)


def source3(v2, sums):
    rows = []
    for x3 in range(4):
        plane = 2 * x3 + H2
        total = jnp.zeros((Y2, LANES), F32)
        for p in (plane, plane + 1):
            total += jnp.where(is_red((Y2, LANES), p), sum2(v2, p), 0.0)
        rows.append(coarse23(total, sums, x3))
    return [rows[0] + rows[1], rows[2] + rows[3]]


def screens12(coloured, from_low, from_high, matrices, f1, i1, i2, begin, end):
    def store(plane, colour, halves):
        f1[plane, colour], i1[plane, colour] = halves

    unpack1(coloured, from_low, from_high, matrices, store, begin, end)

    def screen2(i):
        plane = 2 * i + 2
        total = i1[plane, 0] + i1[plane, 1] + i1[plane + 1, 0] + i1[plane + 1, 1]
        i2[i] = coarse12(total)

    loop(begin // 2, end // 2 - 2, screen2, 4)


def invert12(i1, i2, begin, end):
    def invert1(p):
        i1[p] = 1.0 / (6.0 + i1[p])

    def invert2(p):
        i2[p] = 1.0 / (6.0 + i2[p])

    loop(begin, end, invert1, 4)
    loop(begin // 2, end // 2 - 2, invert2, 4)


def first_message(
    coloured, from_low, from_high, matrices, message, f1, i1, b1, f2, i2, v2, red, sums, _
):
    screens12(coloured, from_low, from_high, matrices, f1, i1, i2, BEGIN, END)
    rows = []
    for x3 in range(4):
        plane = 2 * x3 + H2
        rows.append(coarse23(i2[plane] + i2[plane + 1], sums, x3))
    invert12(i1, i2, BEGIN, END)
    down12(f1, i1, b1, f2, i2, v2, red, BEGIN, END)
    tile = source3(v2, sums) + [rows[0] + rows[1], rows[2] + rows[3]]
    tile = jnp.concatenate(tile + tile, axis=0)
    for i in range(64):
        message[8 * i : 8 * i + 8, :] = tile


def down12_first(
    coloured, from_low, from_high, matrices, f1, i1, b1, f2, i2, v2, red, copies
):
    screens12(coloured, from_low, from_high, matrices, f1, i1, i2, 0, X1)
    invert12(i1, i2, 0, X1)
    for at in (4, 5, 8):
        copies[at].start()
    down12(f1, i1, b1, f2, i2, v2, red, 0, X1)
    for at in (6, 7, 9):
        copies[at].start()


def sources12(coloured, from_low, from_high, matrices, f1):
    def store(item, colour, halves):
        block, i = divmod(item, 8)
        for half in (0, 1):
            plane = H1 + 16 * (block - 1) + 8 * half + i
            if 0 <= plane < X1:
                f1[plane, colour] = halves[half]

    unpack1(coloured, from_low, from_high, matrices, store, 0, 24)


def down12_next(
    coloured, from_low, from_high, matrices, i1, i2, f1, b1, f2, v2, message, red, sums, copies
):
    sources12(coloured, from_low, from_high, matrices, f1)
    for at in (4, 5):
        copies[at].wait()
    down12(f1, i1, b1, f2, i2, v2, red, 0, X1)
    tile = jnp.concatenate(source3(v2, sums) * 4, axis=0)
    for i in range(32):
        message[8 * i : 8 * i + 8, :] = tile


def unpack3(message, rows, first, into):
    sub, lane = iota((8, LANES), 0), iota((8, LANES), 1)
    for gx in range(4):
        for gy in range(4):
            for half in range(2):
                start = (gx * 4 + gy) * 8 * rows + first + half
                value = message[pl.ds(start, 8, stride=rows), :]
                for k in (1, 2, 4):
                    sub_high = (sub // k) % 2 == 1
                    lane_high = (lane // (16 * k)) % 2 == 1
                    from_below = roll(roll(value, -k, 0), 16 * k, 1)
                    from_above = roll(roll(value, k, 0), -16 * k, 1)
                    value = jnp.where(
                        sub_high == lane_high, value, jnp.where(sub_high, from_above, from_below)
                    )
                for x in range(2):
                    into[gx * 4 + 2 * half + x, gy * 4 : gy * 4 + 4, :] = value[4 * x : 4 * x + 4, :]


def turn(value, shift, axis):
    if axis == 0:
        return jnp.concatenate([value[-shift:], value[:-shift]], axis=0)
    return roll(value, shift, axis)


def sum_whole(value):
    total = turn(value, 1, 0) + turn(value, -1, 0)
    total = total + turn(value, 1, 1) + turn(value, -1, 1)
    return total + turn(value, 1, 2) + turn(value, -1, 2)


def red_whole(shape):
    return (iota(shape, 0) + iota(shape, 1) + iota(shape, 2)) % 2 == 0


def pick3(value, index):
    flat = value.reshape(-1, LANES)
    return pick(flat, jnp.broadcast_to(index, flat.shape)).reshape(value.shape)


def coarse34(value, wide):
    wide[...] = value.reshape(8, 2, 16, LANES).sum(axis=1)
    pairs = wide[:, pl.ds(0, 8, stride=2), :] + wide[:, pl.ds(1, 8, stride=2), :]
    pairs = pairs + roll(pairs, -1, 2)
    return 0.5 * pick3(pairs, 2 * (iota((1, LANES), 1) % 64))


def coarse_solve(f3, i3, i4, place, inverse, e3, wide):
    red3, red4 = red_whole((16, 16, LANES)), red_whole((8, 8, LANES))
    v3 = jnp.where(red3, f3 * i3, 0.0)
    v3 = jnp.where(red3, v3, (f3 + sum_whole(v3)) * i3)
    f4 = coarse34(jnp.where(red3, sum_whole(v3), 0.0), wide)
    v4 = jnp.where(red4, f4 * i4, 0.0)
    v4 = jnp.where(red4, v4, (f4 + sum_whole(v4)) * i4)
    r4 = jnp.where(red4, sum_whole(v4), 0.0).reshape(4, 2, 8, LANES).sum(axis=1)
    sub, lane = iota((8, LANES), 0), iota((8, LANES), 1)
    rows = []
    for x5 in range(4):
        pairs = r4[x5] + roll(r4[x5], -1, 1)
        spread = jnp.where(sub // 2 == lane // 32, pick(pairs, 2 * (lane % 32)), 0.0)
        rows.append(0.5 * jnp.sum(spread, axis=0, keepdims=True))
    vector = jnp.broadcast_to(jnp.concatenate(rows, axis=1), (8, 512))
    answer = lax.dot_general(
        vector,
        jnp.concatenate([ref[...] for ref in inverse] + [jnp.zeros((64, 512), F32)], axis=0),
        (((1,), (1,)), ((), ())),
        precision=lax.Precision.HIGHEST,
        preferred_element_type=F32,
    )
    planes = []
    for x5 in range(4):
        z5 = lane % 64 // 2
        index = (place[0] + 4 - x5) % 4 * 16 + (place[1] + 4 - sub // 2) % 4 * 4 + z5 % 4
        apart = (z5 // 4 + 8 - place[2]) % 8
        same = pick(answer[:, :LANES], index + jnp.where(apart == 7, 64, 0))
        part = jnp.where(apart == 1, pick(answer[:, LANES:], index), same)
        part = jnp.where(jnp.logical_or(apart <= 1, apart == 7), part, 0.0)
        planes += [part[None], part[None]]
    w4 = v4 + jnp.concatenate(planes, axis=0)
    w4 = jnp.where(red4, (f4 + sum_whole(w4)) * i4, w4)
    e4 = jnp.where(red4, w4, (f4 + sum_whole(w4)) * i4)
    e4 = pick3(e4, iota((1, LANES), 1) // 2)
    wide[:, pl.ds(0, 8, stride=2), :] = e4
    wide[:, pl.ds(1, 8, stride=2), :] = e4
    spread = jnp.broadcast_to(wide[...][:, None], (8, 2, 16, LANES)).reshape(16, 16, LANES)
    w3 = v3 + spread
    w3 = jnp.where(red3, (f3 + sum_whole(w3)) * i3, w3)
    e3[...] = jnp.where(red3, w3, (f3 + sum_whole(w3)) * i3)


def up21(place, e3, f2, i2, v2, f1, i1, b1, e2, er, eb, tall):
    shift_y = lax.rem(20 - 4 * place[1], 16)
    shift_z = lax.rem(160 - 16 * place[2], 128)

    def from3(i):
        value = e3[lax.rem(4 * place[0] + i + 13, 16)]
        value = pltpu.roll(pltpu.roll(value, shift_y, 0), shift_z, 1)
        value = pick(value, spread_index(16))[:12]
        tall[i, pl.ds(0, 12, stride=2), :] = value
        tall[i, pl.ds(1, 12, stride=2), :] = value
        value = tall[i]
        e2[2 * i] = v2[2 * i] + value
        e2[2 * i + 1] = v2[2 * i + 1] + value

    loop(0, X2 // 2, from3, 5)

    def red2(p):
        fresh = (f2[p] + sum2(e2, p)) * i2[p]
        e2[p] = jnp.where(is_red((Y2, LANES), p), fresh, e2[p])

    def black2(p):
        fresh = (f2[p] + sum2(e2, p)) * i2[p]
        e2[p] = jnp.where(is_red((Y2, LANES), p), e2[p], fresh)

    loop(1, X2 - 1, red2, 3)
    loop(2, X2 - 2, black2, 4)

    def from2(i):
        value = pick(e2[i], spread_index(Y2))
        eb[2 * i + 2] = b1[2 * i + 2] + value
        eb[2 * i + 3] = b1[2 * i + 3] + value

    loop(3, 17, from2, 7)

    def red1(p, parity):
        er[p] = (f1[p, 0] + sum1(eb, p, parity, True)) * i1[p, 0]

    def black1(p, parity):
        eb[p] = (f1[p, 1] + sum1(er, p, parity, False)) * i1[p, 1]

    plane_pairs(8, 36, red1)
    plane_pairs(10, 34, black1)


def add0(er, eb, b, w, tall):
    def from1(i):
        reds, blacks = er[i + 10, 6:18], eb[i + 10, 6:18]
        here = (iota((12, LANES), 1) + i) % 2 == 0
        tall[i, pl.ds(0, 12, stride=2), :] = jnp.where(here, reds, blacks)
        tall[i, pl.ds(1, 12, stride=2), :] = jnp.where(here, blacks, reds)
        value = tall[i]
        for p in (2 * i, 2 * i + 1):
            for q in (0, 1):
                w[p, q] = b[p, q] + value

    loop(0, X0 // 2, from1, 4)


def own_sum(total):
    row, lane = iota((24, LANES), 0), iota((24, LANES), 1)
    own = jnp.logical_and((row + 20) % 24 < 16, (lane + 128 - OWN) % LANES < 64)
    return jnp.sum(jnp.where(own, total, 0.0), axis=0, keepdims=True)


def sum_over(body):
    def step(i, total):
        return total + body(2 * i, 0) + body(2 * i + 1, 1)

    return lax.fori_loop(H0 // 2, H0 // 2 + 16, step, jnp.zeros((24, LANES), F32), unroll=2)


def middle(
    message, place, near, before, after, f2, i2, v2, f1, i1, b1, fr, fb, ir, ib, vb,
    i3, i4, bnew, own1, norm,
    f3, e3, wide, tall, e2, er, eb, w, r, rnew, copies,
):
    unpack3(message, 4, 0, f3)
    unpack3(message, 4, 2, e3)
    screen3 = e3[...]
    screen4 = coarse34(screen3, wide)
    i3[...] = 1.0 / (6.0 + screen3)
    i4[...] = 1.0 / (6.0 + screen4)
    coarse_solve(f3[...], i3[...], i4[...], place, (near, before, after), e3, wide)
    for at in range(5, 11):
        copies[at].wait()
    up21(place, e3, f2, i2, v2, f1, i1, b1, e2, er, eb, tall)
    for at in range(11, 16):
        copies[at].wait()
    add0(er, eb, vb, w, tall)

    def red_up(p, parity):
        for q in (0, 1):
            r[p, q] = (fr[p, q] + sum0(w, p, parity, q, True)) * ir[p, q]

    plane_pairs(2, X0 - 2, red_up)

    def black_up(p, parity):
        for q in (0, 1):
            w[p, q] = (fb[p, q] + sum0(r, p, parity, q, False)) * ib[p, q]

    black_up(3, 1)
    plane_pairs(4, X0 - 4, black_up)
    black_up(X0 - 4, 0)

    def red_down(p, parity):
        for q in (0, 1):
            rnew[p, q] = (fr[p, q] + sum0(w, p, parity, q, True)) * ir[p, q]

    plane_pairs(4, X0 - 4, red_down)

    def squares(p, parity):
        total = jnp.zeros((24, LANES), F32)
        for q in (0, 1):
            part = (rnew[p, q] - r[p, q]) / ir[p, q]
            total = total + part * part
        return total

    norm[...] = jnp.broadcast_to(own_sum(sum_over(squares)), (8, LANES))

    def black_down(p, parity):
        for q in (0, 1):
            fresh = (fb[p, q] + sum0(rnew, p, parity, q, False)) * ib[p, q]
            bnew[p, q] = fresh
            r[p, q] = fresh - w[p, q]

    black_down(5, 1)
    plane_pairs(6, X0 - 6, black_down)
    black_down(X0 - 6, 0)

    def restrict(i):
        low = 0.5 * below_sum(r, 2 * i + H0)[4:20]
        high = 0.5 * below_sum(r, 2 * i + H0 + 16)[4:20]
        own = (iota((16, LANES), 1) + 128 - OWN) % LANES < 64
        own1[i] = jnp.where(own, low, roll(high, 64, 1))

    loop(0, 8, restrict)


def final(
    message, place, near, before, after, f2, i2, v2, f1, i1, b1, fr, fb, ir, ib, b, i3, i4,
    norm,
    sums, r, last,
    f3, e3, wide, tall, e2, er, eb, w, copies,
):
    unpack3(message, 2, 0, f3)
    coarse_solve(f3[...], i3[...], i4[...], place, (near, before, after), e3, wide)
    for at in (6, 9):
        copies[at].wait()
    up21(place, e3, f2, i2, v2, f1, i1, b1, e2, er, eb, tall)
    for at in range(11, 15):
        copies[at].wait()
    add0(er, eb, b, w, tall)

    def red_up(p, parity):
        for q in (0, 1):
            r[p, q] = (fr[p, q] + sum0(w, p, parity, q, True)) * ir[p, q]

    plane_pairs(6, X0 - 6, red_up)

    def black_up(p, parity):
        for q in (0, 1):
            fresh = (fb[p, q] + sum0(r, p, parity, q, False)) * ib[p, q]
            last[p, q] = fresh
            w[p, q] = fresh - w[p, q]

    black_up(7, 1)
    plane_pairs(8, X0 - 8, black_up)
    black_up(X0 - 8, 0)

    def squares(p, parity):
        total = jnp.zeros((24, LANES), F32)
        for q in (0, 1):
            part = sum0(w, p, parity, q, True)
            total = total + part * part
        return total

    squared = own_sum(sum_over(squares))

    low = iota((1, LANES), 1) < 64
    both = jnp.where(low, roll(norm[0:1, :], -OWN, 1), roll(squared, 64 - OWN, 1))
    for i in range(16):
        sums[8 * i : 8 * i + 8, :] = jnp.broadcast_to(both, (8, LANES))


def weave(r, last, matrix, field, _):
    def finish(i):
        parts = []
        for x in (0, 1):
            for q in (0, 1):
                order = (r, last) if x == q else (last, r)
                parts.append(jnp.concatenate([ref[2 * i + x, q] for ref in order], axis=1))
        result = move([thirds(jnp.concatenate(parts, axis=0))], matrix[...])
        for at in range(4):
            rows = result[24 * at + 4 : 24 * at + 20]
            field[2 * i + at // 2 - H0, pl.ds(at % 2, 16, stride=2), :] = rows

    loop(H0 // 2, H0 // 2 + 16, finish)


def exchange(to_high, to_low, axis):
    count = lax.axis_size(axis)
    up = [(i, (i + 1) % count) for i in range(count)]
    down = [(j, i) for i, j in up]
    return lax.ppermute(to_high, axis, up), lax.ppermute(to_low, axis, down)


def from_all(own, axis):
    count = lax.axis_size(axis)
    shifts = [[(i, (i + k) % count) for i in range(count)] for k in range(1, count)]
    return [lax.ppermute(own, axis, shift) for shift in shifts]


def together(first, second):
    both = lax.optimization_barrier((*first, *second))
    return both[: len(first)], both[len(first) :]


def exchange1(own, low, high, beside=()):
    from_low, from_high = exchange(high, low, "gx")
    own = jnp.concatenate([from_low, own, from_high], axis=0)
    below, above = exchange(own, own, "gy")
    if beside:
        (above,), beside = together((above,), exchange(*beside, "gz"))
    items = own.shape[0]
    message = (items // GROUP1, 2, 24, LANES)
    coloured, to_high, to_low = call(
        pack_z1, [(items, 2, 24, LANES), message, message], own, below, above
    )
    return (coloured, *exchange(to_high, to_low, "gz")), beside


def local(f, s, coarse_inverse):
    place = jnp.stack([lax.axis_index(axis) for axis in AXES]).astype(jnp.int32)
    low, high = exchange(
        jnp.concatenate([f[32 - H0 :], s[32 - H0 :]], axis=0),
        jnp.concatenate([f[:H0], s[:H0]], axis=0),
        "gx",
    )
    messages = call(pack_y0, [(2 * TILES, 8, LANES)] * 2, f, s, low, high)
    messages, others = together(messages, from_all(coarse_inverse, "gy"))
    inverse = jnp.concatenate([coarse_inverse, *others], axis=0)
    below, above = exchange(*messages, "gy")
    (below, above), others = together((below, above), from_all(inverse, "gx"))
    inverse = jnp.concatenate([inverse, *others], axis=0)
    groups = 2 * X0 // GROUP0
    line0, line1, line2 = (Y0, LANES), (24, LANES), (Y2, LANES)
    split, to_high, to_low = call(
        pack_z0,
        [(2 * X0, *line0), (groups // 2, *line0), (groups // 2, *line0)],
        *(f, s, low, high, below, above),
        scratch=[(16, *line0)],
    )
    level0, level1, level2 = (X0, 2, *line1), (X1, *line1), (X2, *line2)
    both1 = (X1, 2, *line1)
    matrices1 = jnp.asarray(halo_matrices1(), jnp.bfloat16)
    fr, fb, ir, ib, vb, own1 = call(
        down0,
        [Parked(level0, lambda ref, k=k: ref.at[k]) for k in range(5)] + [(16, 16, LANES)],
        split,
        *exchange(to_high, to_low, "gz"),
        jnp.asarray(lower_matrices(), jnp.bfloat16),
        scratch=[level0, (X0, *line1)],
        park=(56, *level0),
    )
    level1_parts, others = exchange1(own1, own1[:H1], own1[16 - H1 :], (inverse, inverse))
    inverse = (inverse, *others)
    (message,) = call(
        first_message,
        [(512, LANES)],
        *level1_parts,
        matrices1,
        scratch=[both1, both1, level1, level2, level2, level2, level1, (4, *line2)],
    )
    message = lax.all_to_all(message, AXES, 0, 0, tiled=True)
    f1, i1, b1, f2, i2, v2 = call(
        down12_first,
        [
            Parked(both1, lambda ref: ref.at[0]),
            Parked(both1, lambda ref: ref.at[1]),
            Parked(level1, lambda ref: ref.at[2, :, 0]),
            Parked(level2, lambda ref: ref.at[2, 0:X2, 1]),
            Parked(level2, lambda ref: ref.at[3, 0:X2, 0]),
            Parked(level2, lambda ref: ref.at[3, 0:X2, 1]),
        ],
        *level1_parts,
        matrices1,
        scratch=[level1],
        park=(60, *both1),
    )
    whole = (16, 16, LANES)
    work = [whole, whole, (8, 16, LANES), (X0 // 2, *line1), level2, level1, level1]
    work += [level0, level0, level0]
    i3, i4, bnew, own1, norm = call(
        middle,
        [whole, (8, 8, LANES), level0, (8, 16, LANES), (8, LANES)],
        message, place, *inverse, f2, i2, v2, f1, i1, b1, fr, fb, ir, ib, vb,
        scratch=work,
    )
    f1, b1, f2, v2, message = call(
        down12_next,
        [both1, level1, level2, level2, (256, LANES)],
        *exchange1(own1, own1, own1)[0],
        matrices1,
        i1,
        i2,
        scratch=[level1, (4, *line2)],
    )
    message = lax.all_to_all(message, AXES, 0, 0, tiled=True)
    sums, red, black = call(
        final,
        [(128, LANES), level0, level0],
        message, place, *inverse, f2, i2, v2, f1, i1, b1, fr, fb, ir, ib, bnew, i3, i4, norm,
        scratch=work[:-2],
    )
    sums = lax.all_to_all(sums, AXES, 0, 0, tiled=True)
    matrix = jnp.asarray(upper_matrix(), jnp.bfloat16)
    (field,) = call(weave, [(32, 32, LANES)], red, black, matrix)
    squares = jnp.sum(sums.reshape(128, 2, 64), axis=(0, 2))
    return field, jnp.sqrt(squares / CELLS)


def solution(mesh):
    return jax.shard_map(
        local,
        mesh=mesh,
        in_specs=(P("gx", "gy", "gz"), P("gx", "gy", "gz"), P(("gx", "gy", "gz"), None)),
        out_specs=(P("gx", "gy", "gz"), P()),
        check_vma=False,
    )
```

```python
import jax
import jax.numpy as jnp
import numpy as np
from jax import lax
from jax.experimental import pallas as pl
from jax.experimental.pallas import tpu as pltpu
from jax.sharding import PartitionSpec as P

AXES = ("gx", "gy", "gz")
F32 = jnp.float32
LANES = 128
OWN = 32
H0 = 8
X0, Y0 = 48, 48
H1 = 14
X1, Y1 = 44, 48
H2 = 6
X2, Y2 = 20, 24
GROUP0 = 8
GROUP1 = 4
BEGIN, END = 8, 36
CELLS = 16777216.0


def iota(shape, dim):
    return lax.broadcasted_iota(jnp.int32, shape, dim)


def roll(value, shift, axis):
    return pltpu.roll(value, shift % value.shape[axis], axis)


def pick(value, index):
    return jnp.take_along_axis(value, index, axis=1, mode="promise_in_bounds")


def loop(start, stop, body, unroll=4):
    def step(index, carry):
        body(index)
        return carry

    lax.fori_loop(start, stop, step, 0, unroll=unroll)


class Parked:
    def __init__(self, shape, place, whole=None):
        self.shape, self.place, self.whole = shape, place, whole

    def of(self, whole):
        return Parked(self.shape, self.place, whole)


def call(body, outs, *operands, scratch=(), park=None):
    inputs, input_at = [], []
    for operand in operands:
        array = operand.whole if isinstance(operand, Parked) else operand
        at = next((k for k, other in enumerate(inputs) if other is array), len(inputs))
        if at == len(inputs):
            inputs.append(array)
        input_at.append(at)
    far = [isinstance(item, Parked) for item in (*operands, *outs)]
    parked = [item for item in (*operands, *outs) if isinstance(item, Parked)]
    near_outs = [shape for shape in outs if not isinstance(shape, Parked)]
    far_arrays = [operand.whole for operand in operands if isinstance(operand, Parked)]

    def kernel(*refs):
        refs = list(refs)
        ins = [refs.pop(0) for _ in inputs]
        near = [refs.pop(0) for _ in near_outs]
        store = refs.pop(0) if park else None
        semaphores = refs.pop() if parked else None
        work, nears = refs[: len(scratch)], refs[len(scratch) :]
        ready, copies = [], {}
        for at, item in enumerate((*operands, *outs)):
            inward = at < len(operands)
            if far[at]:
                ref = nears.pop(0)
                place = item.place(ins[input_at[at]] if inward else store)
                ends = (place, ref) if inward else (ref, place)
                copies[at] = pltpu.make_async_copy(*ends, semaphores.at[len(copies)])
                if inward:
                    copies[at].start()
            else:
                ref = ins[input_at[at]] if inward else near.pop(0)
            ready.append(ref)
        body(*ready, *work, copies)
        for at in range(len(operands), len(far)):
            if far[at]:
                copies[at].wait()

    def spec(array):
        if any(array is other for other in far_arrays):
            return pl.BlockSpec(memory_space=pl.ANY)
        return pl.BlockSpec(memory_space=pltpu.SMEM if array.dtype == jnp.int32 else pltpu.VMEM)

    shapes = near_outs + ([park] if park else [])
    spaces = [pltpu.VMEM] * len(near_outs) + ([pl.ANY] if park else [])
    work = [pltpu.VMEM(shape, F32) for shape in scratch]
    work += [pltpu.VMEM(item.shape, F32) for item in parked]
    if parked:
        work.append(pltpu.SemaphoreType.DMA((len(parked),)))
    results = pl.pallas_call(
        kernel,
        out_shape=[jax.ShapeDtypeStruct(shape, F32) for shape in shapes],
        in_specs=[spec(array) for array in inputs],
        out_specs=[pl.BlockSpec(memory_space=space) for space in spaces],
        scratch_shapes=work,
        compiler_params=pltpu.CompilerParams(vmem_limit_bytes=20 * 1024 * 1024),
    )(*inputs)
    results = list(results)
    whole = results.pop() if park else None
    return [out.of(whole) if isinstance(out, Parked) else results.pop(0) for out in outs]


def lower_matrices():
    matrices = np.zeros((GROUP0, 256, 256), np.float32)
    for k in range(GROUP0):
        for z in range(-8, 136):
            if 0 <= z < 128:
                row = z
            elif z < 0:
                row = 128 + (16 * k + z) % 128
            else:
                row = 128 + 16 * k + z - 128
            matrices[k, row, 128 * (z % 2) + OWN + z // 2] = 1.0
    return matrices


def upper_matrix():
    matrix = np.zeros((256, 128), np.float32)
    for z in range(128):
        matrix[128 * (z % 2) + OWN + z // 2, z] = 1.0
    return matrix


def halo_matrices1():
    matrices = np.zeros((GROUP1, 384, 256), np.float32)
    for k in range(GROUP1):
        for half in (0, 1):
            for z in range(-H1, 64 + H1):
                if 0 <= z < 64:
                    row = (OWN + 64 * half + z) % 128
                elif z < 0:
                    row = 128 + 64 * half + 14 * k + z + H1
                else:
                    row = 256 + 64 * half + 14 * k + z - 64
                matrices[k, row, 128 * half + OWN + z] = 1.0
    return matrices


def thirds(value):
    high = value.astype(jnp.bfloat16)
    rest = value - high.astype(F32)
    mid = rest.astype(jnp.bfloat16)
    return (rest - mid.astype(F32)).astype(jnp.bfloat16), mid, high


def halves(value):
    high = value.astype(jnp.bfloat16)
    return (value - high.astype(F32)).astype(jnp.bfloat16), high


def move(pieces, matrix):
    total = None
    for parts in zip(*pieces):
        left = parts[0] if len(parts) == 1 else jnp.concatenate(parts, axis=1)
        term = jnp.dot(left, matrix, preferred_element_type=F32)
        total = term if total is None else total + term
    return total


def plane_pairs(first, last, body, unroll=4):
    def both(i):
        body(2 * i, 0)
        body(2 * i + 1, 1)

    loop(first // 2, last // 2, both, unroll)


def sum0(values, plane, parity, q, onto_red):
    mid, other = values[plane, q], values[plane, 1 - q]
    total = values[plane + 1, q] + values[plane - 1, q] + mid
    total = total + other + roll(other, 1 if q == 0 else -1, 0)
    high = ((parity + q) % 2 == 1) == onto_red
    return total + roll(mid, -1 if high else 1, 1)


def even_lanes(shape, parity):
    return (iota(shape, 1) + parity) % 2 == 0


def sum1(values, plane, parity, onto_red):
    mid = values[plane]
    total = values[plane + 1] + values[plane - 1] + mid
    total = total + roll(mid, 1, 1) + roll(mid, -1, 1)
    less, more = roll(mid, 1, 0), roll(mid, -1, 0)
    first, second = (less, more) if onto_red else (more, less)
    return total + jnp.where(even_lanes(mid.shape, parity), first, second)


def sum2(values, plane):
    mid = values[plane]
    total = values[plane + 1] + values[plane - 1]
    total = total + roll(mid, 1, 0) + roll(mid, -1, 0)
    return total + roll(mid, 1, 1) + roll(mid, -1, 1)


def is_red(shape, plane):
    return (iota(shape, 0) + iota(shape, 1) + plane) % 2 == 0


TILES = 40


def pack_y0(f, s, low, high, to_high, to_low, _):
    row = iota((8, LANES), 0)
    for field, own in enumerate((f, s)):
        at = field * TILES
        to_high[at : at + 32] = own[:, 24:32]
        to_low[at : at + 32] = own[:, 0:8]
        for side, halo in enumerate((low, high)):
            first = field * H0 + (H0 if side == 0 else -1)
            step = -1 if side == 0 else 1
            for dx in range(1, 5):
                near, far = first + step * dx, first + step * (8 - dx)
                tile = at + 32 + 4 * side + dx - 1
                above = roll(halo[far, 24:32], dx, 0)
                to_high[tile] = jnp.where(row >= dx, halo[near, 24:32], above)
                below = roll(halo[far, 0:8], 8 - dx, 0)
                to_low[tile] = jnp.where(row < 8 - dx, halo[near, 0:8], below)


def rows_y0(tiles, field, plane, above):
    at = field * TILES
    if H0 <= plane < H0 + 32:
        return tiles[at + plane - H0]
    side = 0 if plane < H0 else 1
    dx = H0 - plane if side == 0 else plane - H0 - 31
    tile = at + 31 + 4 * side
    if dx <= 4:
        return tiles[tile + dx]
    near = max(8 - dx, 1)
    return roll(tiles[tile + near], near - 8 if above else -near, 0)


def pack_z0(f, s, low, high, below, above, split, to_high, to_low, rows, _):
    lane = iota((Y0, LANES), 1)
    block = (lane + 8) % LANES // 16
    last = lane // 8 % 2 == 1
    pair = []
    for group in range(2 * X0 // GROUP0):
        packed = jnp.zeros((Y0, LANES), F32)
        for k in range(GROUP0):
            item = group * GROUP0 + k
            field, plane = divmod(item, X0)
            own = (f, s)[field]
            slot = item % 16
            rows[slot, 0:8, :] = rows_y0(below, field, plane, False)
            if plane < H0:
                rows[slot, 8:40, :] = low[field * H0 + plane]
            elif plane < H0 + 32:
                rows[slot, 8:40, :] = own[plane - H0]
            else:
                rows[slot, 8:40, :] = high[field * H0 + plane - H0 - 32]
            rows[slot, 40:48, :] = rows_y0(above, field, plane, True)
            even = rows[slot, pl.ds(0, 24, stride=2), :]
            odd = rows[slot, pl.ds(1, 24, stride=2), :]
            value = jnp.concatenate([even, odd], axis=0)
            split[item] = value
            packed = jnp.where(block == k, roll(value, 16 * k, 1), packed)
        pair.append(packed)
        if len(pair) == 2:
            to_high[group // 2] = jnp.where(last, pair[0], roll(pair[1], 8, 1))
            to_low[group // 2] = jnp.where(last, roll(pair[1], -8, 1), pair[0])
            pair = []


def down0(split, from_low, from_high, matrices, fr, fb, ir, ib, vb, own1, red, screen, copies):
    lane = iota((Y0, LANES), 1)
    groups = 2 * X0 // GROUP0
    merged = []
    for half in range(groups // 2):
        left, right = from_low[half], from_high[half]
        merged.append(jnp.where(lane // 8 % 2 == 1, left, right))
        merged.append(jnp.where(lane // 8 % 2 == 1, roll(left, -8, 1), roll(right, 8, 1)))
    merged = halves(jnp.concatenate(merged, axis=0))
    for k in range(GROUP0):
        own = [split[group * GROUP0 + k] for group in range(groups)]
        result = move([halves(jnp.concatenate(own, axis=0)), merged], matrices[k])
        for group in range(groups):
            field, plane = divmod(group * GROUP0 + k, X0)
            part = result[Y0 * group : Y0 * group + Y0]
            even, odd = part[:, :LANES], part[:, LANES:]
            if field == 1:
                screen[plane] = even[:24] + odd[:24] + even[24:] + odd[24:]
            for q in (0, 1):
                reds, blacks = (even, odd) if (k + q) % 2 == 0 else (odd, even)
                reds, blacks = reds[24 * q : 24 * q + 24], blacks[24 * q : 24 * q + 24]
                if field == 0:
                    fr[plane, q] = reds
                    fb[plane, q] = blacks
                else:
                    ir[plane, q] = 1.0 / (6.0 + reds)
                    ib[plane, q] = 1.0 / (6.0 + blacks)

    for at in range(4, 8):
        copies[at].start()

    def first(p):
        red[p] = fr[p] * ir[p]

    loop(0, X0, first, 4)

    def black(p, parity):
        for q in (0, 1):
            vb[p, q] = (fb[p, q] + sum0(red, p, parity, q, False)) * ib[p, q]

    black(1, 1)
    plane_pairs(2, X0 - 2, black)
    black(X0 - 2, 0)
    copies[8].start()

    def restrict(i):
        plane = 2 * i + H0
        source = 0.5 * below_sum(vb, plane)
        own = (iota((16, LANES), 1) + 128 - OWN) % LANES < 64
        screens = 0.5 * (screen[plane] + screen[plane + 1])[4:20]
        own1[i] = jnp.where(own, source[4:20], roll(screens, 64, 1))

    loop(0, 16, restrict)


def below_sum(values, plane):
    total = sum0(values, plane, 0, 0, True) + sum0(values, plane, 0, 1, True)
    total = total + sum0(values, plane + 1, 1, 0, True)
    return total + sum0(values, plane + 1, 1, 1, True)


def pack_z1(own, below, above, coloured, to_high, to_low, _):
    block = iota((24, LANES), 1) % 64 // 14
    for group in range(own.shape[0] // GROUP1):
        up = [jnp.zeros((24, LANES), F32)] * 2
        down = [jnp.zeros((24, LANES), F32)] * 2
        for k in range(GROUP1):
            item = group * GROUP1 + k
            even, odd = [
                jnp.concatenate([ref[item, pl.ds(q, 8, stride=2), :] for ref in (below, own, above)], axis=0)
                for q in (0, 1)
            ]
            here = even_lanes((24, LANES), item)
            for colour in (0, 1):
                first, second = (even, odd) if colour == 0 else (odd, even)
                value = jnp.where(here, first, second)
                coloured[item, colour] = value
                up[colour] = jnp.where(block == k, roll(value, 14 * k - 82, 1), up[colour])
                down[colour] = jnp.where(block == k, roll(value, 14 * k - 32, 1), down[colour])
        for colour in (0, 1):
            to_high[group, colour] = up[colour]
            to_low[group, colour] = down[colour]


def unpack1(coloured, from_low, from_high, matrices, store, first, last):
    groups = range(first // GROUP1, last // GROUP1)
    rows = len(groups) * 48
    halos = [
        halves(ref[groups.start : groups.stop].reshape(rows, LANES))
        for ref in (from_low, from_high)
    ]
    for k in range(GROUP1):
        own = [coloured[GROUP1 * g + k, colour] for g in groups for colour in (0, 1)]
        result = move([halves(jnp.concatenate(own, axis=0)), *halos], matrices[k])
        for at in range(2 * len(groups)):
            part = result[24 * at : 24 * at + 24]
            item = GROUP1 * groups[at // 2] + k
            store(item, at % 2, (part[:, :LANES], part[:, LANES:]))


def pair_index(rows):
    return jnp.clip(2 * iota((rows, LANES), 1) - OWN, 0, 127)


def spread_index(rows):
    return (iota((rows, LANES), 1) - OWN) // 2 + OWN


def coarse12(total):
    pairs = total + roll(total, -1, 1)
    return 0.5 * pick(pairs, pair_index(Y2))


def down12(f1, i1, b1, f2, i2, v2, red, begin, end):
    def first(p):
        red[p] = f1[p, 0] * i1[p, 0]

    loop(begin, end, first, 4)

    def black(p, parity):
        b1[p] = (f1[p, 1] + sum1(red, p, parity, False)) * i1[p, 1]

    black(begin + 1, 1)
    plane_pairs(begin + 2, end - 2, black)
    black(end - 2, 0)

    def restrict(i):
        plane = 2 * i + 2
        f2[i] = coarse12(sum1(b1, plane, 0, True) + sum1(b1, plane + 1, 1, True))

    begin2, end2 = begin // 2, end // 2 - 2
    loop(begin2, end2, restrict, 4)

    def red2(p):
        v2[p] = jnp.where(is_red((Y2, LANES), p), f2[p] * i2[p], 0.0)

    def black2(p):
        fresh = (f2[p] + sum2(v2, p)) * i2[p]
        v2[p] = jnp.where(is_red((Y2, LANES), p), v2[p], fresh)

    loop(begin2, end2, red2, 4)
    loop(begin2 + 1, end2 - 1, black2, 3)


def coarse23(total, sums, x3):
    sums[x3] = total
    pairs = sums[x3, pl.ds(8, 8, stride=2), :] + sums[x3, pl.ds(9, 8, stride=2), :]
    pairs = pairs + roll(pairs, -1, 1)
    lane = iota((8, LANES), 1)
    spread = pick(pairs, OWN + 2 * (lane % 16))
    here = lane // 16 == (x3 % 2) * 4 + iota((8, LANES), 0)
    here = jnp.logical_and(here, iota((8, LANES), 0) < 4)
    return 0.5 * jnp.sum(jnp.where(here, spread, 0.0), axis=0, keepdims=True)


def source3(v2, sums):
    rows = []
    for x3 in range(4):
        plane = 2 * x3 + H2
        total = jnp.zeros((Y2, LANES), F32)
        for p in (plane, plane + 1):
            total += jnp.where(is_red((Y2, LANES), p), sum2(v2, p), 0.0)
        rows.append(coarse23(total, sums, x3))
    return [rows[0] + rows[1], rows[2] + rows[3]]


def screens12(coloured, from_low, from_high, matrices, f1, i1, i2, begin, end):
    def store(plane, colour, halves):
        f1[plane, colour], i1[plane, colour] = halves

    unpack1(coloured, from_low, from_high, matrices, store, begin, end)

    def screen2(i):
        plane = 2 * i + 2
        total = i1[plane, 0] + i1[plane, 1] + i1[plane + 1, 0] + i1[plane + 1, 1]
        i2[i] = coarse12(total)

    loop(begin // 2, end // 2 - 2, screen2, 4)


def invert12(i1, i2, begin, end):
    def invert1(p):
        i1[p] = 1.0 / (6.0 + i1[p])

    def invert2(p):
        i2[p] = 1.0 / (6.0 + i2[p])

    loop(begin, end, invert1, 4)
    loop(begin // 2, end // 2 - 2, invert2, 4)


def first_message(
    coloured, from_low, from_high, matrices, message, f1, i1, b1, f2, i2, v2, red, sums, _
):
    screens12(coloured, from_low, from_high, matrices, f1, i1, i2, BEGIN, END)
    rows = []
    for x3 in range(4):
        plane = 2 * x3 + H2
        rows.append(coarse23(i2[plane] + i2[plane + 1], sums, x3))
    invert12(i1, i2, BEGIN, END)
    down12(f1, i1, b1, f2, i2, v2, red, BEGIN, END)
    tile = source3(v2, sums) + [rows[0] + rows[1], rows[2] + rows[3]]
    tile = jnp.concatenate(tile + tile, axis=0)
    for i in range(64):
        message[8 * i : 8 * i + 8, :] = tile


def down12_first(
    coloured, from_low, from_high, matrices, f1, i1, b1, f2, i2, v2, red, copies
):
    screens12(coloured, from_low, from_high, matrices, f1, i1, i2, 0, X1)
    invert12(i1, i2, 0, X1)
    for at in (4, 5, 8):
        copies[at].start()
    down12(f1, i1, b1, f2, i2, v2, red, 0, X1)
    for at in (6, 7, 9):
        copies[at].start()


def sources12(coloured, from_low, from_high, matrices, f1):
    def store(item, colour, halves):
        block, i = divmod(item, 8)
        for half in (0, 1):
            plane = H1 + 16 * (block - 1) + 8 * half + i
            if 0 <= plane < X1:
                f1[plane, colour] = halves[half]

    unpack1(coloured, from_low, from_high, matrices, store, 0, 24)


def down12_next(
    coloured, from_low, from_high, matrices, i1, i2, f1, b1, f2, v2, message, red, sums, copies
):
    sources12(coloured, from_low, from_high, matrices, f1)
    for at in (4, 5):
        copies[at].wait()
    down12(f1, i1, b1, f2, i2, v2, red, 0, X1)
    tile = jnp.concatenate(source3(v2, sums) * 4, axis=0)
    for i in range(32):
        message[8 * i : 8 * i + 8, :] = tile


def unpack3(message, rows, first, into):
    sub, lane = iota((8, LANES), 0), iota((8, LANES), 1)
    for gx in range(4):
        for gy in range(4):
            for half in range(2):
                start = (gx * 4 + gy) * 8 * rows + first + half
                value = message[pl.ds(start, 8, stride=rows), :]
                for k in (1, 2, 4):
                    sub_high = (sub // k) % 2 == 1
                    lane_high = (lane // (16 * k)) % 2 == 1
                    from_below = roll(roll(value, -k, 0), 16 * k, 1)
                    from_above = roll(roll(value, k, 0), -16 * k, 1)
                    value = jnp.where(
                        sub_high == lane_high, value, jnp.where(sub_high, from_above, from_below)
                    )
                for x in range(2):
                    into[gx * 4 + 2 * half + x, gy * 4 : gy * 4 + 4, :] = value[4 * x : 4 * x + 4, :]


def turn(value, shift, axis):
    if axis == 0:
        return jnp.concatenate([value[-shift:], value[:-shift]], axis=0)
    return roll(value, shift, axis)


def sum_whole(value):
    total = turn(value, 1, 0) + turn(value, -1, 0)
    total = total + turn(value, 1, 1) + turn(value, -1, 1)
    return total + turn(value, 1, 2) + turn(value, -1, 2)


def red_whole(shape):
    return (iota(shape, 0) + iota(shape, 1) + iota(shape, 2)) % 2 == 0


def pick3(value, index):
    flat = value.reshape(-1, LANES)
    return pick(flat, jnp.broadcast_to(index, flat.shape)).reshape(value.shape)


def coarse34(value, wide):
    wide[...] = value.reshape(8, 2, 16, LANES).sum(axis=1)
    pairs = wide[:, pl.ds(0, 8, stride=2), :] + wide[:, pl.ds(1, 8, stride=2), :]
    pairs = pairs + roll(pairs, -1, 2)
    return 0.5 * pick3(pairs, 2 * (iota((1, LANES), 1) % 64))


def coarse_solve(f3, i3, i4, place, inverse, e3, wide):
    red3, red4 = red_whole((16, 16, LANES)), red_whole((8, 8, LANES))
    v3 = jnp.where(red3, f3 * i3, 0.0)
    v3 = jnp.where(red3, v3, (f3 + sum_whole(v3)) * i3)
    f4 = coarse34(jnp.where(red3, sum_whole(v3), 0.0), wide)
    v4 = jnp.where(red4, f4 * i4, 0.0)
    v4 = jnp.where(red4, v4, (f4 + sum_whole(v4)) * i4)
    r4 = jnp.where(red4, sum_whole(v4), 0.0).reshape(4, 2, 8, LANES).sum(axis=1)
    sub, lane = iota((8, LANES), 0), iota((8, LANES), 1)
    rows = []
    for x5 in range(4):
        pairs = r4[x5] + roll(r4[x5], -1, 1)
        spread = jnp.where(sub // 2 == lane // 32, pick(pairs, 2 * (lane % 32)), 0.0)
        rows.append(0.5 * jnp.sum(spread, axis=0, keepdims=True))
    vector = jnp.broadcast_to(jnp.concatenate(rows, axis=1), (8, 512))
    answer = lax.dot_general(
        vector,
        jnp.concatenate([ref[...] for ref in inverse] + [jnp.zeros((64, 512), F32)], axis=0),
        (((1,), (1,)), ((), ())),
        precision=lax.Precision.HIGHEST,
        preferred_element_type=F32,
    )
    planes = []
    for x5 in range(4):
        z5 = lane % 64 // 2
        index = (place[0] + 4 - x5) % 4 * 16 + (place[1] + 4 - sub // 2) % 4 * 4 + z5 % 4
        apart = (z5 // 4 + 8 - place[2]) % 8
        same = pick(answer[:, :LANES], index + jnp.where(apart == 7, 64, 0))
        part = jnp.where(apart == 1, pick(answer[:, LANES:], index), same)
        part = jnp.where(jnp.logical_or(apart <= 1, apart == 7), part, 0.0)
        planes += [part[None], part[None]]
    w4 = v4 + jnp.concatenate(planes, axis=0)
    w4 = jnp.where(red4, (f4 + sum_whole(w4)) * i4, w4)
    e4 = jnp.where(red4, w4, (f4 + sum_whole(w4)) * i4)
    e4 = pick3(e4, iota((1, LANES), 1) // 2)
    wide[:, pl.ds(0, 8, stride=2), :] = e4
    wide[:, pl.ds(1, 8, stride=2), :] = e4
    spread = jnp.broadcast_to(wide[...][:, None], (8, 2, 16, LANES)).reshape(16, 16, LANES)
    w3 = v3 + spread
    w3 = jnp.where(red3, (f3 + sum_whole(w3)) * i3, w3)
    e3[...] = jnp.where(red3, w3, (f3 + sum_whole(w3)) * i3)


def up21(place, e3, f2, i2, v2, f1, i1, b1, e2, er, eb, tall):
    shift_y = lax.rem(20 - 4 * place[1], 16)
    shift_z = lax.rem(160 - 16 * place[2], 128)

    def from3(i):
        value = e3[lax.rem(4 * place[0] + i + 13, 16)]
        value = pltpu.roll(pltpu.roll(value, shift_y, 0), shift_z, 1)
        value = pick(value, spread_index(16))[:12]
        tall[i, pl.ds(0, 12, stride=2), :] = value
        tall[i, pl.ds(1, 12, stride=2), :] = value
        value = tall[i]
        e2[2 * i] = v2[2 * i] + value
        e2[2 * i + 1] = v2[2 * i + 1] + value

    loop(0, X2 // 2, from3, 5)

    def red2(p):
        fresh = (f2[p] + sum2(e2, p)) * i2[p]
        e2[p] = jnp.where(is_red((Y2, LANES), p), fresh, e2[p])

    def black2(p):
        fresh = (f2[p] + sum2(e2, p)) * i2[p]
        e2[p] = jnp.where(is_red((Y2, LANES), p), e2[p], fresh)

    loop(1, X2 - 1, red2, 3)
    loop(2, X2 - 2, black2, 4)

    def from2(i):
        value = pick(e2[i], spread_index(Y2))
        eb[2 * i + 2] = b1[2 * i + 2] + value
        eb[2 * i + 3] = b1[2 * i + 3] + value

    loop(3, 17, from2, 7)

    def red1(p, parity):
        er[p] = (f1[p, 0] + sum1(eb, p, parity, True)) * i1[p, 0]

    def black1(p, parity):
        eb[p] = (f1[p, 1] + sum1(er, p, parity, False)) * i1[p, 1]

    plane_pairs(8, 36, red1)
    plane_pairs(10, 34, black1)


def add0(er, eb, b, w, tall):
    def from1(i):
        reds, blacks = er[i + 10, 6:18], eb[i + 10, 6:18]
        here = (iota((12, LANES), 1) + i) % 2 == 0
        tall[i, pl.ds(0, 12, stride=2), :] = jnp.where(here, reds, blacks)
        tall[i, pl.ds(1, 12, stride=2), :] = jnp.where(here, blacks, reds)
        value = tall[i]
        for p in (2 * i, 2 * i + 1):
            for q in (0, 1):
                w[p, q] = b[p, q] + value

    loop(0, X0 // 2, from1, 4)


def own_sum(total):
    row, lane = iota((24, LANES), 0), iota((24, LANES), 1)
    own = jnp.logical_and((row + 20) % 24 < 16, (lane + 128 - OWN) % LANES < 64)
    return jnp.sum(jnp.where(own, total, 0.0), axis=0, keepdims=True)


def sum_over(body):
    def step(i, total):
        return total + body(2 * i, 0) + body(2 * i + 1, 1)

    return lax.fori_loop(H0 // 2, H0 // 2 + 16, step, jnp.zeros((24, LANES), F32), unroll=2)


def middle(
    message, place, near, before, after, f2, i2, v2, f1, i1, b1, fr, fb, ir, ib, vb,
    i3, i4, bnew, own1, norm,
    f3, e3, wide, tall, e2, er, eb, w, r, rnew, copies,
):
    unpack3(message, 4, 0, f3)
    unpack3(message, 4, 2, e3)
    screen3 = e3[...]
    screen4 = coarse34(screen3, wide)
    i3[...] = 1.0 / (6.0 + screen3)
    i4[...] = 1.0 / (6.0 + screen4)
    coarse_solve(f3[...], i3[...], i4[...], place, (near, before, after), e3, wide)
    for at in range(5, 11):
        copies[at].wait()
    up21(place, e3, f2, i2, v2, f1, i1, b1, e2, er, eb, tall)
    for at in range(11, 16):
        copies[at].wait()
    add0(er, eb, vb, w, tall)

    def red_up(p, parity):
        for q in (0, 1):
            r[p, q] = (fr[p, q] + sum0(w, p, parity, q, True)) * ir[p, q]

    plane_pairs(2, X0 - 2, red_up)

    def black_up(p, parity):
        for q in (0, 1):
            w[p, q] = (fb[p, q] + sum0(r, p, parity, q, False)) * ib[p, q]

    black_up(3, 1)
    plane_pairs(4, X0 - 4, black_up)
    black_up(X0 - 4, 0)

    def red_down(p, parity):
        for q in (0, 1):
            rnew[p, q] = (fr[p, q] + sum0(w, p, parity, q, True)) * ir[p, q]

    plane_pairs(4, X0 - 4, red_down)

    def squares(p, parity):
        total = jnp.zeros((24, LANES), F32)
        for q in (0, 1):
            part = (rnew[p, q] - r[p, q]) / ir[p, q]
            total = total + part * part
        return total

    norm[...] = jnp.broadcast_to(own_sum(sum_over(squares)), (8, LANES))

    def black_down(p, parity):
        for q in (0, 1):
            fresh = (fb[p, q] + sum0(rnew, p, parity, q, False)) * ib[p, q]
            bnew[p, q] = fresh
            r[p, q] = fresh - w[p, q]

    black_down(5, 1)
    plane_pairs(6, X0 - 6, black_down)
    black_down(X0 - 6, 0)

    def restrict(i):
        low = 0.5 * below_sum(r, 2 * i + H0)[4:20]
        high = 0.5 * below_sum(r, 2 * i + H0 + 16)[4:20]
        own = (iota((16, LANES), 1) + 128 - OWN) % LANES < 64
        own1[i] = jnp.where(own, low, roll(high, 64, 1))

    loop(0, 8, restrict)


def final(
    message, place, near, before, after, f2, i2, v2, f1, i1, b1, fr, fb, ir, ib, b, i3, i4,
    norm,
    sums, r, last,
    f3, e3, wide, tall, e2, er, eb, w, copies,
):
    unpack3(message, 2, 0, f3)
    coarse_solve(f3[...], i3[...], i4[...], place, (near, before, after), e3, wide)
    for at in (6, 9):
        copies[at].wait()
    up21(place, e3, f2, i2, v2, f1, i1, b1, e2, er, eb, tall)
    for at in range(11, 15):
        copies[at].wait()
    add0(er, eb, b, w, tall)

    def red_up(p, parity):
        for q in (0, 1):
            r[p, q] = (fr[p, q] + sum0(w, p, parity, q, True)) * ir[p, q]

    plane_pairs(6, X0 - 6, red_up)

    def black_up(p, parity):
        for q in (0, 1):
            fresh = (fb[p, q] + sum0(r, p, parity, q, False)) * ib[p, q]
            last[p, q] = fresh
            w[p, q] = fresh - w[p, q]

    black_up(7, 1)
    plane_pairs(8, X0 - 8, black_up)
    black_up(X0 - 8, 0)

    def squares(p, parity):
        total = jnp.zeros((24, LANES), F32)
        for q in (0, 1):
            part = sum0(w, p, parity, q, True)
            total = total + part * part
        return total

    squared = own_sum(sum_over(squares))

    low = iota((1, LANES), 1) < 64
    both = jnp.where(low, roll(norm[0:1, :], -OWN, 1), roll(squared, 64 - OWN, 1))
    for i in range(16):
        sums[8 * i : 8 * i + 8, :] = jnp.broadcast_to(both, (8, LANES))


def weave(r, last, matrix, field, _):
    def finish(i):
        parts = []
        for x in (0, 1):
            for q in (0, 1):
                order = (r, last) if x == q else (last, r)
                parts.append(jnp.concatenate([ref[2 * i + x, q] for ref in order], axis=1))
        result = move([thirds(jnp.concatenate(parts, axis=0))], matrix[...])
        for at in range(4):
            rows = result[24 * at + 4 : 24 * at + 20]
            field[2 * i + at // 2 - H0, pl.ds(at % 2, 16, stride=2), :] = rows

    loop(H0 // 2, H0 // 2 + 16, finish)


def exchange(to_high, to_low, axis):
    count = lax.axis_size(axis)
    up = [(i, (i + 1) % count) for i in range(count)]
    down = [(j, i) for i, j in up]
    return lax.ppermute(to_high, axis, up), lax.ppermute(to_low, axis, down)


def from_all(own, axis):
    count = lax.axis_size(axis)
    shifts = [[(i, (i + k) % count) for i in range(count)] for k in range(1, count)]
    return [lax.ppermute(own, axis, shift) for shift in shifts]


def together(first, second):
    both = lax.optimization_barrier((*first, *second))
    return both[: len(first)], both[len(first) :]


def exchange1(own, low, high, beside=()):
    from_low, from_high = exchange(high, low, "gx")
    own = jnp.concatenate([from_low, own, from_high], axis=0)
    below, above = exchange(own, own, "gy")
    if beside:
        (above,), beside = together((above,), exchange(*beside, "gz"))
    items = own.shape[0]
    message = (items // GROUP1, 2, 24, LANES)
    coloured, to_high, to_low = call(
        pack_z1, [(items, 2, 24, LANES), message, message], own, below, above
    )
    return (coloured, *exchange(to_high, to_low, "gz")), beside


def local(f, s, coarse_inverse):
    place = jnp.stack([lax.axis_index(axis) for axis in AXES]).astype(jnp.int32)
    low, high = exchange(
        jnp.concatenate([f[32 - H0 :], s[32 - H0 :]], axis=0),
        jnp.concatenate([f[:H0], s[:H0]], axis=0),
        "gx",
    )
    messages = call(pack_y0, [(2 * TILES, 8, LANES)] * 2, f, s, low, high)
    messages, others = together(messages, from_all(coarse_inverse, "gy"))
    inverse = jnp.concatenate([coarse_inverse, *others], axis=0)
    below, above = exchange(*messages, "gy")
    (below, above), others = together((below, above), from_all(inverse, "gx"))
    inverse = jnp.concatenate([inverse, *others], axis=0)
    groups = 2 * X0 // GROUP0
    line0, line1, line2 = (Y0, LANES), (24, LANES), (Y2, LANES)
    split, to_high, to_low = call(
        pack_z0,
        [(2 * X0, *line0), (groups // 2, *line0), (groups // 2, *line0)],
        *(f, s, low, high, below, above),
        scratch=[(16, *line0)],
    )
    level0, level1, level2 = (X0, 2, *line1), (X1, *line1), (X2, *line2)
    both1 = (X1, 2, *line1)
    matrices1 = jnp.asarray(halo_matrices1(), jnp.bfloat16)
    fr, fb, ir, ib, vb, own1 = call(
        down0,
        [Parked(level0, lambda ref, k=k: ref.at[k]) for k in range(5)] + [(16, 16, LANES)],
        split,
        *exchange(to_high, to_low, "gz"),
        jnp.asarray(lower_matrices(), jnp.bfloat16),
        scratch=[level0, (X0, *line1)],
        park=(56, *level0),
    )
    level1_parts, others = exchange1(own1, own1[:H1], own1[16 - H1 :], (inverse, inverse))
    inverse = (inverse, *others)
    (message,) = call(
        first_message,
        [(512, LANES)],
        *level1_parts,
        matrices1,
        scratch=[both1, both1, level1, level2, level2, level2, level1, (4, *line2)],
    )
    message = lax.all_to_all(message, AXES, 0, 0, tiled=True)
    f1, i1, b1, f2, i2, v2 = call(
        down12_first,
        [
            Parked(both1, lambda ref: ref.at[0]),
            Parked(both1, lambda ref: ref.at[1]),
            Parked(level1, lambda ref: ref.at[2, :, 0]),
            Parked(level2, lambda ref: ref.at[2, 0:X2, 1]),
            Parked(level2, lambda ref: ref.at[3, 0:X2, 0]),
            Parked(level2, lambda ref: ref.at[3, 0:X2, 1]),
        ],
        *level1_parts,
        matrices1,
        scratch=[level1],
        park=(60, *both1),
    )
    whole = (16, 16, LANES)
    work = [whole, whole, (8, 16, LANES), (X0 // 2, *line1), level2, level1, level1]
    work += [level0, level0, level0]
    i3, i4, bnew, own1, norm = call(
        middle,
        [whole, (8, 8, LANES), level0, (8, 16, LANES), (8, LANES)],
        message, place, *inverse, f2, i2, v2, f1, i1, b1, fr, fb, ir, ib, vb,
        scratch=work,
    )
    f1, b1, f2, v2, message = call(
        down12_next,
        [both1, level1, level2, level2, (256, LANES)],
        *exchange1(own1, own1, own1)[0],
        matrices1,
        i1,
        i2,
        scratch=[level1, (4, *line2)],
    )
    message = lax.all_to_all(message, AXES, 0, 0, tiled=True)
    sums, red, black = call(
        final,
        [(128, LANES), level0, level0],
        message, place, *inverse, f2, i2, v2, f1, i1, b1, fr, fb, ir, ib, bnew, i3, i4, norm,
        scratch=work[:-2],
    )
    sums = lax.all_to_all(sums, AXES, 0, 0, tiled=True)
    matrix = jnp.asarray(upper_matrix(), jnp.bfloat16)
    (field,) = call(weave, [(32, 32, LANES)], red, black, matrix)
    squares = jnp.sum(sums.reshape(128, 2, 64), axis=(0, 2))
    return field, jnp.sqrt(squares / CELLS)


def solution(mesh):
    return jax.shard_map(
        local,
        mesh=mesh,
        in_specs=(P("gx", "gy", "gz"), P("gx", "gy", "gz"), P(("gx", "gy", "gz"), None)),
        out_specs=(P("gx", "gy", "gz"), P()),
        check_vma=False,
    )
```

```python
import jax
import jax.numpy as jnp
import numpy as np
from jax import lax
from jax.experimental import pallas as pl
from jax.experimental.pallas import tpu as pltpu
from jax.sharding import PartitionSpec as P

AXES = ("gx", "gy", "gz")
F32 = jnp.float32
LANES = 128
OWN = 32
H0 = 8
X0, Y0 = 48, 48
H1 = 14
X1, Y1 = 44, 48
H2 = 6
X2, Y2 = 20, 24
GROUP0 = 8
GROUP1 = 4
BEGIN, END = 8, 36
CELLS = 16777216.0


def iota(shape, dim):
    return lax.broadcasted_iota(jnp.int32, shape, dim)


def roll(value, shift, axis):
    return pltpu.roll(value, shift % value.shape[axis], axis)


def pick(value, index):
    return jnp.take_along_axis(value, index, axis=1, mode="promise_in_bounds")


def loop(start, stop, body, unroll=2):
    def step(index, carry):
        body(index)
        return carry

    lax.fori_loop(start, stop, step, 0, unroll=unroll)


class Parked:
    def __init__(self, shape, place, whole=None):
        self.shape, self.place, self.whole = shape, place, whole

    def of(self, whole):
        return Parked(self.shape, self.place, whole)


def call(body, outs, *operands, scratch=(), park=None):
    inputs, input_at = [], []
    for operand in operands:
        array = operand.whole if isinstance(operand, Parked) else operand
        at = next((k for k, other in enumerate(inputs) if other is array), len(inputs))
        if at == len(inputs):
            inputs.append(array)
        input_at.append(at)
    far = [isinstance(item, Parked) for item in (*operands, *outs)]
    parked = [item for item in (*operands, *outs) if isinstance(item, Parked)]
    near_outs = [shape for shape in outs if not isinstance(shape, Parked)]
    far_arrays = [operand.whole for operand in operands if isinstance(operand, Parked)]

    def kernel(*refs):
        refs = list(refs)
        ins = [refs.pop(0) for _ in inputs]
        near = [refs.pop(0) for _ in near_outs]
        store = refs.pop(0) if park else None
        semaphores = refs.pop() if parked else None
        work, nears = refs[: len(scratch)], refs[len(scratch) :]
        ready, copies = [], {}
        for at, item in enumerate((*operands, *outs)):
            inward = at < len(operands)
            if far[at]:
                ref = nears.pop(0)
                place = item.place(ins[input_at[at]] if inward else store)
                ends = (place, ref) if inward else (ref, place)
                copies[at] = pltpu.make_async_copy(*ends, semaphores.at[len(copies)])
                if inward:
                    copies[at].start()
            else:
                ref = ins[input_at[at]] if inward else near.pop(0)
            ready.append(ref)
        body(*ready, *work, copies)
        for at in range(len(operands), len(far)):
            if far[at]:
                copies[at].wait()

    def spec(array):
        if any(array is other for other in far_arrays):
            return pl.BlockSpec(memory_space=pl.ANY)
        return pl.BlockSpec(memory_space=pltpu.SMEM if array.dtype == jnp.int32 else pltpu.VMEM)

    shapes = near_outs + ([park] if park else [])
    spaces = [pltpu.VMEM] * len(near_outs) + ([pl.ANY] if park else [])
    work = [pltpu.VMEM(shape, F32) for shape in scratch]
    work += [pltpu.VMEM(item.shape, F32) for item in parked]
    if parked:
        work.append(pltpu.SemaphoreType.DMA((len(parked),)))
    results = pl.pallas_call(
        kernel,
        out_shape=[jax.ShapeDtypeStruct(shape, F32) for shape in shapes],
        in_specs=[spec(array) for array in inputs],
        out_specs=[pl.BlockSpec(memory_space=space) for space in spaces],
        scratch_shapes=work,
        compiler_params=pltpu.CompilerParams(vmem_limit_bytes=20 * 1024 * 1024),
    )(*inputs)
    results = list(results)
    whole = results.pop() if park else None
    return [out.of(whole) if isinstance(out, Parked) else results.pop(0) for out in outs]


def lower_matrices():
    matrices = np.zeros((GROUP0, 256, 256), np.float32)
    for k in range(GROUP0):
        for z in range(-8, 136):
            if 0 <= z < 128:
                row = z
            elif z < 0:
                row = 128 + (16 * k + z) % 128
            else:
                row = 128 + 16 * k + z - 128
            matrices[k, row, 128 * (z % 2) + OWN + z // 2] = 1.0
    return matrices


def upper_matrix():
    matrix = np.zeros((256, 128), np.float32)
    for z in range(128):
        matrix[128 * (z % 2) + OWN + z // 2, z] = 1.0
    return matrix


def halo_matrices1():
    matrices = np.zeros((GROUP1, 384, 256), np.float32)
    for k in range(GROUP1):
        for half in (0, 1):
            for z in range(-H1, 64 + H1):
                if 0 <= z < 64:
                    row = (OWN + 64 * half + z) % 128
                elif z < 0:
                    row = 128 + 64 * half + 14 * k + z + H1
                else:
                    row = 256 + 64 * half + 14 * k + z - 64
                matrices[k, row, 128 * half + OWN + z] = 1.0
    return matrices


def thirds(value):
    high = value.astype(jnp.bfloat16)
    rest = value - high.astype(F32)
    mid = rest.astype(jnp.bfloat16)
    return (rest - mid.astype(F32)).astype(jnp.bfloat16), mid, high


def halves(value):
    high = value.astype(jnp.bfloat16)
    return (value - high.astype(F32)).astype(jnp.bfloat16), high


def move(pieces, matrix):
    total = None
    for parts in zip(*pieces):
        left = parts[0] if len(parts) == 1 else jnp.concatenate(parts, axis=1)
        term = jnp.dot(left, matrix, preferred_element_type=F32)
        total = term if total is None else total + term
    return total


def plane_pairs(first, last, body, unroll=4):
    def both(i):
        body(2 * i, 0)
        body(2 * i + 1, 1)

    loop(first // 2, last // 2, both, unroll)


def sum0(values, plane, parity, q, onto_red):
    mid, other = values[plane, q], values[plane, 1 - q]
    total = values[plane + 1, q] + values[plane - 1, q] + mid
    total = total + other + roll(other, 1 if q == 0 else -1, 0)
    high = ((parity + q) % 2 == 1) == onto_red
    return total + roll(mid, -1 if high else 1, 1)


def even_lanes(shape, parity):
    return (iota(shape, 1) + parity) % 2 == 0


def sum1(values, plane, parity, onto_red):
    mid = values[plane]
    total = values[plane + 1] + values[plane - 1] + mid
    total = total + roll(mid, 1, 1) + roll(mid, -1, 1)
    less, more = roll(mid, 1, 0), roll(mid, -1, 0)
    first, second = (less, more) if onto_red else (more, less)
    return total + jnp.where(even_lanes(mid.shape, parity), first, second)


def sum2(values, plane):
    mid = values[plane]
    total = values[plane + 1] + values[plane - 1]
    total = total + roll(mid, 1, 0) + roll(mid, -1, 0)
    return total + roll(mid, 1, 1) + roll(mid, -1, 1)


def is_red(shape, plane):
    return (iota(shape, 0) + iota(shape, 1) + plane) % 2 == 0


TILES = 40


def pack_y0(f, s, low, high, to_high, to_low, _):
    row = iota((8, LANES), 0)
    for field, own in enumerate((f, s)):
        at = field * TILES
        to_high[at : at + 32] = own[:, 24:32]
        to_low[at : at + 32] = own[:, 0:8]
        for side, halo in enumerate((low, high)):
            first = field * H0 + (H0 if side == 0 else -1)
            step = -1 if side == 0 else 1
            for dx in range(1, 5):
                near, far = first + step * dx, first + step * (8 - dx)
                tile = at + 32 + 4 * side + dx - 1
                above = roll(halo[far, 24:32], dx, 0)
                to_high[tile] = jnp.where(row >= dx, halo[near, 24:32], above)
                below = roll(halo[far, 0:8], 8 - dx, 0)
                to_low[tile] = jnp.where(row < 8 - dx, halo[near, 0:8], below)


def rows_y0(tiles, field, plane, above):
    at = field * TILES
    if H0 <= plane < H0 + 32:
        return tiles[at + plane - H0]
    side = 0 if plane < H0 else 1
    dx = H0 - plane if side == 0 else plane - H0 - 31
    tile = at + 31 + 4 * side
    if dx <= 4:
        return tiles[tile + dx]
    near = max(8 - dx, 1)
    return roll(tiles[tile + near], near - 8 if above else -near, 0)


def pack_z0(f, s, low, high, below, above, split, to_high, to_low, rows, _):
    lane = iota((Y0, LANES), 1)
    block = (lane + 8) % LANES // 16
    last = lane // 8 % 2 == 1
    pair = []
    for group in range(2 * X0 // GROUP0):
        packed = jnp.zeros((Y0, LANES), F32)
        for k in range(GROUP0):
            item = group * GROUP0 + k
            field, plane = divmod(item, X0)
            own = (f, s)[field]
            slot = item % 16
            rows[slot, 0:8, :] = rows_y0(below, field, plane, False)
            if plane < H0:
                rows[slot, 8:40, :] = low[field * H0 + plane]
            elif plane < H0 + 32:
                rows[slot, 8:40, :] = own[plane - H0]
            else:
                rows[slot, 8:40, :] = high[field * H0 + plane - H0 - 32]
            rows[slot, 40:48, :] = rows_y0(above, field, plane, True)
            even = rows[slot, pl.ds(0, 24, stride=2), :]
            odd = rows[slot, pl.ds(1, 24, stride=2), :]
            value = jnp.concatenate([even, odd], axis=0)
            split[item] = value
            packed = jnp.where(block == k, roll(value, 16 * k, 1), packed)
        pair.append(packed)
        if len(pair) == 2:
            to_high[group // 2] = jnp.where(last, pair[0], roll(pair[1], 8, 1))
            to_low[group // 2] = jnp.where(last, roll(pair[1], -8, 1), pair[0])
            pair = []


def down0(split, from_low, from_high, matrices, fr, fb, ir, ib, vb, own1, red, screen, copies):
    lane = iota((Y0, LANES), 1)
    groups = 2 * X0 // GROUP0
    merged = []
    for half in range(groups // 2):
        left, right = from_low[half], from_high[half]
        merged.append(jnp.where(lane // 8 % 2 == 1, left, right))
        merged.append(jnp.where(lane // 8 % 2 == 1, roll(left, -8, 1), roll(right, 8, 1)))
    merged = halves(jnp.concatenate(merged, axis=0))
    for k in range(GROUP0):
        own = [split[group * GROUP0 + k] for group in range(groups)]
        result = move([halves(jnp.concatenate(own, axis=0)), merged], matrices[k])
        for group in range(groups):
            field, plane = divmod(group * GROUP0 + k, X0)
            part = result[Y0 * group : Y0 * group + Y0]
            even, odd = part[:, :LANES], part[:, LANES:]
            if field == 1:
                screen[plane] = even[:24] + odd[:24] + even[24:] + odd[24:]
            for q in (0, 1):
                reds, blacks = (even, odd) if (k + q) % 2 == 0 else (odd, even)
                reds, blacks = reds[24 * q : 24 * q + 24], blacks[24 * q : 24 * q + 24]
                if field == 0:
                    fr[plane, q] = reds
                    fb[plane, q] = blacks
                else:
                    ir[plane, q] = 1.0 / (6.0 + reds)
                    ib[plane, q] = 1.0 / (6.0 + blacks)

    for at in range(4, 8):
        copies[at].start()

    def first(p):
        red[p] = fr[p] * ir[p]

    loop(0, X0, first, 4)

    def black(p, parity):
        for q in (0, 1):
            vb[p, q] = (fb[p, q] + sum0(red, p, parity, q, False)) * ib[p, q]

    black(1, 1)
    plane_pairs(2, X0 - 2, black)
    black(X0 - 2, 0)
    copies[8].start()

    def restrict(i):
        plane = 2 * i + H0
        source = 0.5 * below_sum(vb, plane)
        own = (iota((16, LANES), 1) + 128 - OWN) % LANES < 64
        screens = 0.5 * (screen[plane] + screen[plane + 1])[4:20]
        own1[i] = jnp.where(own, source[4:20], roll(screens, 64, 1))

    loop(0, 16, restrict)


def below_sum(values, plane):
    total = sum0(values, plane, 0, 0, True) + sum0(values, plane, 0, 1, True)
    total = total + sum0(values, plane + 1, 1, 0, True)
    return total + sum0(values, plane + 1, 1, 1, True)


def pack_z1(own, halos, coloured, to_high, to_low, _):
    block = iota((24, LANES), 1) % 64 // 14
    for group in range(own.shape[0] // GROUP1):
        up = [jnp.zeros((24, LANES), F32)] * 2
        down = [jnp.zeros((24, LANES), F32)] * 2
        for k in range(GROUP1):
            item = group * GROUP1 + k
            even, odd = [
                jnp.concatenate(
                    [
                        ref[at, pl.ds(q, 8, stride=2), :]
                        for ref, at in ((halos, item), (own, item), (halos, own.shape[0] + item))
                    ],
                    axis=0,
                )
                for q in (0, 1)
            ]
            here = even_lanes((24, LANES), item)
            for colour in (0, 1):
                first, second = (even, odd) if colour == 0 else (odd, even)
                value = jnp.where(here, first, second)
                coloured[item, colour] = value
                up[colour] = jnp.where(block == k, roll(value, 14 * k - 82, 1), up[colour])
                down[colour] = jnp.where(block == k, roll(value, 14 * k - 32, 1), down[colour])
        for colour in (0, 1):
            to_high[group, colour] = up[colour]
            to_low[group, colour] = down[colour]


def unpack1(coloured, from_low, from_high, matrices, store, first, last):
    groups = range(first // GROUP1, last // GROUP1)
    rows = len(groups) * 48
    halos = [
        halves(ref[groups.start : groups.stop].reshape(rows, LANES))
        for ref in (from_low, from_high)
    ]
    for k in range(GROUP1):
        own = [coloured[GROUP1 * g + k, colour] for g in groups for colour in (0, 1)]
        result = move([halves(jnp.concatenate(own, axis=0)), *halos], matrices[k])
        for at in range(2 * len(groups)):
            part = result[24 * at : 24 * at + 24]
            item = GROUP1 * groups[at // 2] + k
            store(item, at % 2, (part[:, :LANES], part[:, LANES:]))


def pair_index(rows):
    return jnp.clip(2 * iota((rows, LANES), 1) - OWN, 0, 127)


def spread_index(rows):
    return (iota((rows, LANES), 1) - OWN) // 2 + OWN


def coarse12(total):
    pairs = total + roll(total, -1, 1)
    return 0.5 * pick(pairs, pair_index(Y2))


def down12(f1, i1, b1, f2, i2, v2, red, begin, end):
    def first(p):
        red[p] = f1[p, 0] * i1[p, 0]

    loop(begin, end, first, 4)

    def black(p, parity):
        b1[p] = (f1[p, 1] + sum1(red, p, parity, False)) * i1[p, 1]

    black(begin + 1, 1)
    plane_pairs(begin + 2, end - 2, black)
    black(end - 2, 0)

    def restrict(i):
        plane = 2 * i + 2
        f2[i] = coarse12(sum1(b1, plane, 0, True) + sum1(b1, plane + 1, 1, True))

    begin2, end2 = begin // 2, end // 2 - 2
    loop(begin2, end2, restrict, 4)

    def red2(p):
        v2[p] = jnp.where(is_red((Y2, LANES), p), f2[p] * i2[p], 0.0)

    def black2(p):
        fresh = (f2[p] + sum2(v2, p)) * i2[p]
        v2[p] = jnp.where(is_red((Y2, LANES), p), v2[p], fresh)

    loop(begin2, end2, red2, 4)
    loop(begin2 + 1, end2 - 1, black2, 3)


def coarse23(total, sums, x3):
    sums[x3] = total
    pairs = sums[x3, pl.ds(8, 8, stride=2), :] + sums[x3, pl.ds(9, 8, stride=2), :]
    pairs = pairs + roll(pairs, -1, 1)
    lane = iota((8, LANES), 1)
    spread = pick(pairs, OWN + 2 * (lane % 16))
    here = lane // 16 == (x3 % 2) * 4 + iota((8, LANES), 0)
    here = jnp.logical_and(here, iota((8, LANES), 0) < 4)
    return 0.5 * jnp.sum(jnp.where(here, spread, 0.0), axis=0, keepdims=True)


def source3(v2, sums):
    rows = []
    for x3 in range(4):
        plane = 2 * x3 + H2
        total = jnp.zeros((Y2, LANES), F32)
        for p in (plane, plane + 1):
            total += jnp.where(is_red((Y2, LANES), p), sum2(v2, p), 0.0)
        rows.append(coarse23(total, sums, x3))
    return [rows[0] + rows[1], rows[2] + rows[3]]


def screens12(coloured, from_low, from_high, matrices, f1, i1, i2, begin, end):
    def store(plane, colour, halves):
        f1[plane, colour], i1[plane, colour] = halves

    unpack1(coloured, from_low, from_high, matrices, store, begin, end)

    def screen2(i):
        plane = 2 * i + 2
        total = i1[plane, 0] + i1[plane, 1] + i1[plane + 1, 0] + i1[plane + 1, 1]
        i2[i] = coarse12(total)

    loop(begin // 2, end // 2 - 2, screen2, 4)


def invert12(i1, i2, begin, end):
    def invert1(p):
        i1[p] = 1.0 / (6.0 + i1[p])

    def invert2(p):
        i2[p] = 1.0 / (6.0 + i2[p])

    loop(begin, end, invert1, 4)
    loop(begin // 2, end // 2 - 2, invert2, 4)


def first_message(
    coloured, from_low, from_high, matrices, message, f1, i1, b1, f2, i2, v2, red, sums, _
):
    screens12(coloured, from_low, from_high, matrices, f1, i1, i2, BEGIN, END)
    rows = []
    for x3 in range(4):
        plane = 2 * x3 + H2
        rows.append(coarse23(i2[plane] + i2[plane + 1], sums, x3))
    invert12(i1, i2, BEGIN, END)
    down12(f1, i1, b1, f2, i2, v2, red, BEGIN, END)
    tile = source3(v2, sums) + [rows[0] + rows[1], rows[2] + rows[3]]
    tile = jnp.concatenate(tile + tile, axis=0)
    for i in range(64):
        message[8 * i : 8 * i + 8, :] = tile


def down12_first(
    coloured, from_low, from_high, matrices, f1, i1, b1, f2, i2, v2, red, copies
):
    screens12(coloured, from_low, from_high, matrices, f1, i1, i2, 0, X1)
    invert12(i1, i2, 0, X1)
    for at in (4, 5, 8):
        copies[at].start()
    down12(f1, i1, b1, f2, i2, v2, red, 0, X1)
    for at in (6, 7, 9):
        copies[at].start()


def sources12(coloured, from_low, from_high, matrices, f1):
    def store(item, colour, halves):
        block, i = divmod(item, 8)
        for half in (0, 1):
            plane = H1 + 16 * (block - 1) + 8 * half + i
            if 0 <= plane < X1:
                f1[plane, colour] = halves[half]

    unpack1(coloured, from_low, from_high, matrices, store, 0, 24)


def down12_next(
    coloured, from_low, from_high, matrices, i1, i2, f1, b1, f2, v2, message, red, sums, copies
):
    sources12(coloured, from_low, from_high, matrices, f1)
    for at in (4, 5):
        copies[at].wait()
    down12(f1, i1, b1, f2, i2, v2, red, 0, X1)
    tile = jnp.concatenate(source3(v2, sums) * 4, axis=0)
    for i in range(32):
        message[8 * i : 8 * i + 8, :] = tile


def unpack3(message, rows, first, into):
    sub, lane = iota((8, LANES), 0), iota((8, LANES), 1)
    for gx in range(4):
        for gy in range(4):
            for half in range(2):
                start = (gx * 4 + gy) * 8 * rows + first + half
                value = message[pl.ds(start, 8, stride=rows), :]
                for k in (1, 2, 4):
                    sub_high = (sub // k) % 2 == 1
                    lane_high = (lane // (16 * k)) % 2 == 1
                    from_below = roll(roll(value, -k, 0), 16 * k, 1)
                    from_above = roll(roll(value, k, 0), -16 * k, 1)
                    value = jnp.where(
                        sub_high == lane_high, value, jnp.where(sub_high, from_above, from_below)
                    )
                for x in range(2):
                    into[gx * 4 + 2 * half + x, gy * 4 : gy * 4 + 4, :] = value[4 * x : 4 * x + 4, :]


def turn(value, shift, axis):
    if axis == 0:
        return jnp.concatenate([value[-shift:], value[:-shift]], axis=0)
    return roll(value, shift, axis)


def sum_whole(value):
    total = turn(value, 1, 0) + turn(value, -1, 0)
    total = total + turn(value, 1, 1) + turn(value, -1, 1)
    return total + turn(value, 1, 2) + turn(value, -1, 2)


def red_whole(shape):
    return (iota(shape, 0) + iota(shape, 1) + iota(shape, 2)) % 2 == 0


def pick3(value, index):
    flat = value.reshape(-1, LANES)
    return pick(flat, jnp.broadcast_to(index, flat.shape)).reshape(value.shape)


def coarse34(value, wide):
    wide[...] = value.reshape(8, 2, 16, LANES).sum(axis=1)
    pairs = wide[:, pl.ds(0, 8, stride=2), :] + wide[:, pl.ds(1, 8, stride=2), :]
    pairs = pairs + roll(pairs, -1, 2)
    return 0.5 * pick3(pairs, 2 * (iota((1, LANES), 1) % 64))


def coarse_solve(f3, i3, i4, place, inverse, e3, wide):
    red3, red4 = red_whole((16, 16, LANES)), red_whole((8, 8, LANES))
    v3 = jnp.where(red3, f3 * i3, 0.0)
    v3 = jnp.where(red3, v3, (f3 + sum_whole(v3)) * i3)
    f4 = coarse34(jnp.where(red3, sum_whole(v3), 0.0), wide)
    v4 = jnp.where(red4, f4 * i4, 0.0)
    v4 = jnp.where(red4, v4, (f4 + sum_whole(v4)) * i4)
    r4 = jnp.where(red4, sum_whole(v4), 0.0).reshape(4, 2, 8, LANES).sum(axis=1)
    sub, lane = iota((8, LANES), 0), iota((8, LANES), 1)
    rows = []
    for x5 in range(4):
        pairs = r4[x5] + roll(r4[x5], -1, 1)
        spread = jnp.where(sub // 2 == lane // 32, pick(pairs, 2 * (lane % 32)), 0.0)
        rows.append(0.5 * jnp.sum(spread, axis=0, keepdims=True))
    vector = jnp.broadcast_to(jnp.concatenate(rows, axis=1), (8, 512))
    answer = lax.dot_general(
        vector,
        jnp.concatenate([ref[...] for ref in inverse] + [jnp.zeros((64, 512), F32)], axis=0),
        (((1,), (1,)), ((), ())),
        precision=lax.Precision.HIGHEST,
        preferred_element_type=F32,
    )
    planes = []
    for x5 in range(4):
        z5 = lane % 64 // 2
        index = (place[0] + 4 - x5) % 4 * 16 + (place[1] + 4 - sub // 2) % 4 * 4 + z5 % 4
        apart = (z5 // 4 + 8 - place[2]) % 8
        same = pick(answer[:, :LANES], index + jnp.where(apart == 7, 64, 0))
        part = jnp.where(apart == 1, pick(answer[:, LANES:], index), same)
        part = jnp.where(jnp.logical_or(apart <= 1, apart == 7), part, 0.0)
        planes += [part[None], part[None]]
    w4 = v4 + jnp.concatenate(planes, axis=0)
    w4 = jnp.where(red4, (f4 + sum_whole(w4)) * i4, w4)
    e4 = jnp.where(red4, w4, (f4 + sum_whole(w4)) * i4)
    e4 = pick3(e4, iota((1, LANES), 1) // 2)
    wide[:, pl.ds(0, 8, stride=2), :] = e4
    wide[:, pl.ds(1, 8, stride=2), :] = e4
    spread = jnp.broadcast_to(wide[...][:, None], (8, 2, 16, LANES)).reshape(16, 16, LANES)
    w3 = v3 + spread
    w3 = jnp.where(red3, (f3 + sum_whole(w3)) * i3, w3)
    e3[...] = jnp.where(red3, w3, (f3 + sum_whole(w3)) * i3)


def up21(place, e3, f2, i2, v2, f1, i1, b1, e2, er, eb, tall):
    shift_y = lax.rem(20 - 4 * place[1], 16)
    shift_z = lax.rem(160 - 16 * place[2], 128)

    def from3(i):
        value = e3[lax.rem(4 * place[0] + i + 13, 16)]
        value = pltpu.roll(pltpu.roll(value, shift_y, 0), shift_z, 1)
        value = pick(value, spread_index(16))[:12]
        tall[i, pl.ds(0, 12, stride=2), :] = value
        tall[i, pl.ds(1, 12, stride=2), :] = value
        value = tall[i]
        e2[2 * i] = v2[2 * i] + value
        e2[2 * i + 1] = v2[2 * i + 1] + value

    loop(0, X2 // 2, from3, 5)

    def red2(p):
        fresh = (f2[p] + sum2(e2, p)) * i2[p]
        e2[p] = jnp.where(is_red((Y2, LANES), p), fresh, e2[p])

    def black2(p):
        fresh = (f2[p] + sum2(e2, p)) * i2[p]
        e2[p] = jnp.where(is_red((Y2, LANES), p), e2[p], fresh)

    loop(1, X2 - 1, red2, 3)
    loop(2, X2 - 2, black2, 4)

    def from2(i):
        value = pick(e2[i], spread_index(Y2))
        eb[2 * i + 2] = b1[2 * i + 2] + value
        eb[2 * i + 3] = b1[2 * i + 3] + value

    loop(3, 17, from2, 7)

    def red1(p, parity):
        er[p] = (f1[p, 0] + sum1(eb, p, parity, True)) * i1[p, 0]

    def black1(p, parity):
        eb[p] = (f1[p, 1] + sum1(er, p, parity, False)) * i1[p, 1]

    plane_pairs(8, 36, red1)
    plane_pairs(10, 34, black1)


def add0(er, eb, b, w, tall):
    def from1(i):
        reds, blacks = er[i + 10, 6:18], eb[i + 10, 6:18]
        here = (iota((12, LANES), 1) + i) % 2 == 0
        tall[i, pl.ds(0, 12, stride=2), :] = jnp.where(here, reds, blacks)
        tall[i, pl.ds(1, 12, stride=2), :] = jnp.where(here, blacks, reds)
        value = tall[i]
        for p in (2 * i, 2 * i + 1):
            for q in (0, 1):
                w[p, q] = b[p, q] + value

    loop(0, X0 // 2, from1, 4)


def own_sum(total):
    row, lane = iota((24, LANES), 0), iota((24, LANES), 1)
    own = jnp.logical_and((row + 20) % 24 < 16, (lane + 128 - OWN) % LANES < 64)
    return jnp.sum(jnp.where(own, total, 0.0), axis=0, keepdims=True)


def sum_over(body):
    def step(i, total):
        return total + body(2 * i, 0) + body(2 * i + 1, 1)

    return lax.fori_loop(H0 // 2, H0 // 2 + 16, step, jnp.zeros((24, LANES), F32), unroll=2)


def middle(
    message, place, near, before, after, f2, i2, v2, f1, i1, b1, fr, fb, ir, ib, vb,
    i3, i4, bnew, own1, norm,
    f3, e3, wide, tall, e2, er, eb, w, r, rnew, copies,
):
    unpack3(message, 4, 0, f3)
    unpack3(message, 4, 2, e3)
    screen3 = e3[...]
    screen4 = coarse34(screen3, wide)
    i3[...] = 1.0 / (6.0 + screen3)
    i4[...] = 1.0 / (6.0 + screen4)
    coarse_solve(f3[...], i3[...], i4[...], place, (near, before, after), e3, wide)
    for at in range(5, 11):
        copies[at].wait()
    up21(place, e3, f2, i2, v2, f1, i1, b1, e2, er, eb, tall)
    for at in range(11, 16):
        copies[at].wait()
    add0(er, eb, vb, w, tall)

    def red_up(p, parity):
        for q in (0, 1):
            r[p, q] = (fr[p, q] + sum0(w, p, parity, q, True)) * ir[p, q]

    plane_pairs(2, X0 - 2, red_up)

    def black_up(p, parity):
        for q in (0, 1):
            w[p, q] = (fb[p, q] + sum0(r, p, parity, q, False)) * ib[p, q]

    black_up(3, 1)
    plane_pairs(4, X0 - 4, black_up)
    black_up(X0 - 4, 0)

    def red_down(p, parity):
        for q in (0, 1):
            rnew[p, q] = (fr[p, q] + sum0(w, p, parity, q, True)) * ir[p, q]

    plane_pairs(4, X0 - 4, red_down)

    def squares(p, parity):
        total = jnp.zeros((24, LANES), F32)
        for q in (0, 1):
            part = (rnew[p, q] - r[p, q]) / ir[p, q]
            total = total + part * part
        return total

    norm[...] = jnp.broadcast_to(own_sum(sum_over(squares)), (8, LANES))

    def black_down(p, parity):
        for q in (0, 1):
            fresh = (fb[p, q] + sum0(rnew, p, parity, q, False)) * ib[p, q]
            bnew[p, q] = fresh
            r[p, q] = fresh - w[p, q]

    black_down(5, 1)
    plane_pairs(6, X0 - 6, black_down)
    black_down(X0 - 6, 0)

    def restrict(i):
        low = 0.5 * below_sum(r, 2 * i + H0)[4:20]
        high = 0.5 * below_sum(r, 2 * i + H0 + 16)[4:20]
        own = (iota((16, LANES), 1) + 128 - OWN) % LANES < 64
        own1[i] = jnp.where(own, low, roll(high, 64, 1))

    loop(0, 8, restrict)


def final(
    message, place, near, before, after, f2, i2, v2, f1, i1, b1, fr, fb, ir, ib, b, i3, i4,
    norm,
    sums, r, last,
    f3, e3, wide, tall, e2, er, eb, w, copies,
):
    unpack3(message, 2, 0, f3)
    coarse_solve(f3[...], i3[...], i4[...], place, (near, before, after), e3, wide)
    for at in (6, 9):
        copies[at].wait()
    up21(place, e3, f2, i2, v2, f1, i1, b1, e2, er, eb, tall)
    for at in range(11, 15):
        copies[at].wait()
    add0(er, eb, b, w, tall)

    def red_up(p, parity):
        for q in (0, 1):
            r[p, q] = (fr[p, q] + sum0(w, p, parity, q, True)) * ir[p, q]

    plane_pairs(6, X0 - 6, red_up)

    def black_up(p, parity):
        for q in (0, 1):
            fresh = (fb[p, q] + sum0(r, p, parity, q, False)) * ib[p, q]
            last[p, q] = fresh
            w[p, q] = fresh - w[p, q]

    black_up(7, 1)
    plane_pairs(8, X0 - 8, black_up)
    black_up(X0 - 8, 0)

    def squares(p, parity):
        total = jnp.zeros((24, LANES), F32)
        for q in (0, 1):
            part = sum0(w, p, parity, q, True)
            total = total + part * part
        return total

    squared = own_sum(sum_over(squares))

    low = iota((1, LANES), 1) < 64
    both = jnp.where(low, roll(norm[0:1, :], -OWN, 1), roll(squared, 64 - OWN, 1))
    for i in range(16):
        sums[8 * i : 8 * i + 8, :] = jnp.broadcast_to(both, (8, LANES))


def weave(r, last, matrix, field, _):
    def finish(i):
        parts = []
        for x in (0, 1):
            for q in (0, 1):
                order = (r, last) if x == q else (last, r)
                parts.append(jnp.concatenate([ref[2 * i + x, q] for ref in order], axis=1))
        result = move([thirds(jnp.concatenate(parts, axis=0))], matrix[...])
        for at in range(4):
            rows = result[24 * at + 4 : 24 * at + 20]
            field[2 * i + at // 2 - H0, pl.ds(at % 2, 16, stride=2), :] = rows

    loop(H0 // 2, H0 // 2 + 16, finish)


def exchange(to_high, to_low, axis):
    count = lax.axis_size(axis)
    up = [(i, (i + 1) % count) for i in range(count)]
    down = [(j, i) for i, j in up]
    return lax.ppermute(to_high, axis, up), lax.ppermute(to_low, axis, down)


def from_all(own, axis):
    count = lax.axis_size(axis)
    shifts = [[(i, (i + k) % count) for i in range(count)] for k in range(1, count)]
    return [lax.ppermute(own, axis, shift) for shift in shifts]


def together(first, second):
    both = lax.optimization_barrier((*first, *second))
    return both[: len(first)], both[len(first) :]


def exchange1(own, low, high, beside=()):
    from_low, from_high = exchange(high, low, "gx")
    own = jnp.concatenate([from_low, own, from_high], axis=0)
    below, above = exchange(own, own, "gy")
    if beside:
        (above,), beside = together((above,), exchange(*beside, "gz"))
    items = own.shape[0]
    message = (items // GROUP1, 2, 24, LANES)
    coloured, to_high, to_low = call(
        pack_z1, [(items, 2, 24, LANES), message, message], own, jnp.concatenate([below, above])
    )
    return (coloured, *exchange(to_high, to_low, "gz")), beside


def local(f, s, coarse_inverse):
    place = jnp.stack([lax.axis_index(axis) for axis in AXES]).astype(jnp.int32)
    low, high = exchange(
        jnp.concatenate([f[32 - H0 :], s[32 - H0 :]], axis=0),
        jnp.concatenate([f[:H0], s[:H0]], axis=0),
        "gx",
    )
    messages = call(pack_y0, [(2 * TILES, 8, LANES)] * 2, f, s, low, high)
    messages, others = together(messages, from_all(coarse_inverse, "gy"))
    inverse = jnp.concatenate([coarse_inverse, *others], axis=0)
    below, above = exchange(*messages, "gy")
    (below, above), others = together((below, above), from_all(inverse, "gx"))
    inverse = jnp.concatenate([inverse, *others], axis=0)
    groups = 2 * X0 // GROUP0
    line0, line1, line2 = (Y0, LANES), (24, LANES), (Y2, LANES)
    split, to_high, to_low = call(
        pack_z0,
        [(2 * X0, *line0), (groups // 2, *line0), (groups // 2, *line0)],
        *(f, s, low, high, below, above),
        scratch=[(16, *line0)],
    )
    level0, level1, level2 = (X0, 2, *line1), (X1, *line1), (X2, *line2)
    both1 = (X1, 2, *line1)
    matrices1 = jnp.asarray(halo_matrices1(), jnp.bfloat16)
    fr, fb, ir, ib, vb, own1 = call(
        down0,
        [Parked(level0, lambda ref, k=k: ref.at[k]) for k in range(5)] + [(16, 16, LANES)],
        split,
        *exchange(to_high, to_low, "gz"),
        jnp.asarray(lower_matrices(), jnp.bfloat16),
        scratch=[level0, (X0, *line1)],
        park=(56, *level0),
    )
    level1_parts, others = exchange1(own1, own1[:H1], own1[16 - H1 :], (inverse, inverse))
    inverse = (inverse, *others)
    (message,) = call(
        first_message,
        [(512, LANES)],
        *level1_parts,
        matrices1,
        scratch=[both1, both1, level1, level2, level2, level2, level1, (4, *line2)],
    )
    message = lax.all_to_all(message, AXES, 0, 0, tiled=True)
    f1, i1, b1, f2, i2, v2 = call(
        down12_first,
        [
            Parked(both1, lambda ref: ref.at[0]),
            Parked(both1, lambda ref: ref.at[1]),
            Parked(level1, lambda ref: ref.at[2, :, 0]),
            Parked(level2, lambda ref: ref.at[2, 0:X2, 1]),
            Parked(level2, lambda ref: ref.at[3, 0:X2, 0]),
            Parked(level2, lambda ref: ref.at[3, 0:X2, 1]),
        ],
        *level1_parts,
        matrices1,
        scratch=[level1],
        park=(60, *both1),
    )
    whole = (16, 16, LANES)
    work = [whole, whole, (8, 16, LANES), (X0 // 2, *line1), level2, level1, level1]
    work += [level0, level0, level0]
    i3, i4, bnew, own1, norm = call(
        middle,
        [whole, (8, 8, LANES), level0, (8, 16, LANES), (8, LANES)],
        message, place, *inverse, f2, i2, v2, f1, i1, b1, fr, fb, ir, ib, vb,
        scratch=work,
    )
    f1, b1, f2, v2, message = call(
        down12_next,
        [both1, level1, level2, level2, (256, LANES)],
        *exchange1(own1, own1, own1)[0],
        matrices1,
        i1,
        i2,
        scratch=[level1, (4, *line2)],
    )
    message = lax.all_to_all(message, AXES, 0, 0, tiled=True)
    sums, red, black = call(
        final,
        [(128, LANES), level0, level0],
        message, place, *inverse, f2, i2, v2, f1, i1, b1, fr, fb, ir, ib, bnew, i3, i4, norm,
        scratch=work[:-2],
    )
    sums = lax.all_to_all(sums, AXES, 0, 0, tiled=True)
    matrix = jnp.asarray(upper_matrix(), jnp.bfloat16)
    (field,) = call(weave, [(32, 32, LANES)], red, black, matrix)
    squares = jnp.sum(sums.reshape(128, 2, 64), axis=(0, 2))
    return field, jnp.sqrt(squares / CELLS)


def solution(mesh):
    return jax.shard_map(
        local,
        mesh=mesh,
        in_specs=(P("gx", "gy", "gz"), P("gx", "gy", "gz"), P(("gx", "gy", "gz"), None)),
        out_specs=(P("gx", "gy", "gz"), P()),
        check_vma=False,
    )
```

```python
import jax
import jax.numpy as jnp
import numpy as np
from jax import lax
from jax.experimental import pallas as pl
from jax.experimental.pallas import tpu as pltpu
from jax.sharding import PartitionSpec as P

AXES = ("gx", "gy", "gz")
F32 = jnp.float32
LANES = 128
OWN = 32
H0 = 8
X0, Y0 = 48, 48
H1 = 14
X1, Y1 = 44, 48
H2 = 6
X2, Y2 = 20, 24
GROUP0 = 8
GROUP1 = 4
BEGIN, END = 8, 36
CELLS = 16777216.0


def iota(shape, dim):
    return lax.broadcasted_iota(jnp.int32, shape, dim)


def roll(value, shift, axis):
    return pltpu.roll(value, shift % value.shape[axis], axis)


def pick(value, index):
    return jnp.take_along_axis(value, index, axis=1, mode="promise_in_bounds")


def loop(start, stop, body, unroll=2):
    def step(index, carry):
        body(index)
        return carry

    lax.fori_loop(start, stop, step, 0, unroll=unroll)


class Parked:
    def __init__(self, shape, place, whole=None):
        self.shape, self.place, self.whole = shape, place, whole

    def of(self, whole):
        return Parked(self.shape, self.place, whole)


def call(body, outs, *operands, scratch=(), park=None):
    inputs, input_at = [], []
    for operand in operands:
        array = operand.whole if isinstance(operand, Parked) else operand
        at = next((k for k, other in enumerate(inputs) if other is array), len(inputs))
        if at == len(inputs):
            inputs.append(array)
        input_at.append(at)
    far = [isinstance(item, Parked) for item in (*operands, *outs)]
    parked = [item for item in (*operands, *outs) if isinstance(item, Parked)]
    near_outs = [shape for shape in outs if not isinstance(shape, Parked)]
    far_arrays = [operand.whole for operand in operands if isinstance(operand, Parked)]

    def kernel(*refs):
        refs = list(refs)
        ins = [refs.pop(0) for _ in inputs]
        near = [refs.pop(0) for _ in near_outs]
        store = refs.pop(0) if park else None
        semaphores = refs.pop() if parked else None
        work, nears = refs[: len(scratch)], refs[len(scratch) :]
        ready, copies = [], {}
        for at, item in enumerate((*operands, *outs)):
            inward = at < len(operands)
            if far[at]:
                ref = nears.pop(0)
                place = item.place(ins[input_at[at]] if inward else store)
                ends = (place, ref) if inward else (ref, place)
                copies[at] = pltpu.make_async_copy(*ends, semaphores.at[len(copies)])
                if inward:
                    copies[at].start()
            else:
                ref = ins[input_at[at]] if inward else near.pop(0)
            ready.append(ref)
        body(*ready, *work, copies)
        for at in range(len(operands), len(far)):
            if far[at]:
                copies[at].wait()

    def spec(array):
        if any(array is other for other in far_arrays):
            return pl.BlockSpec(memory_space=pl.ANY)
        return pl.BlockSpec(memory_space=pltpu.SMEM if array.dtype == jnp.int32 else pltpu.VMEM)

    shapes = near_outs + ([park] if park else [])
    spaces = [pltpu.VMEM] * len(near_outs) + ([pl.ANY] if park else [])
    work = [pltpu.VMEM(shape, F32) for shape in scratch]
    work += [pltpu.VMEM(item.shape, F32) for item in parked]
    if parked:
        work.append(pltpu.SemaphoreType.DMA((len(parked),)))
    results = pl.pallas_call(
        kernel,
        out_shape=[jax.ShapeDtypeStruct(shape, F32) for shape in shapes],
        in_specs=[spec(array) for array in inputs],
        out_specs=[pl.BlockSpec(memory_space=space) for space in spaces],
        scratch_shapes=work,
        compiler_params=pltpu.CompilerParams(vmem_limit_bytes=20 * 1024 * 1024),
    )(*inputs)
    results = list(results)
    whole = results.pop() if park else None
    return [out.of(whole) if isinstance(out, Parked) else results.pop(0) for out in outs]


def lower_matrices():
    matrices = np.zeros((GROUP0, 256, 256), np.float32)
    for k in range(GROUP0):
        for z in range(-8, 136):
            if 0 <= z < 128:
                row = z
            elif z < 0:
                row = 128 + (16 * k + z) % 128
            else:
                row = 128 + 16 * k + z - 128
            matrices[k, row, 128 * (z % 2) + OWN + z // 2] = 1.0
    return matrices


def upper_matrix():
    matrix = np.zeros((256, 128), np.float32)
    for z in range(128):
        matrix[128 * (z % 2) + OWN + z // 2, z] = 1.0
    return matrix


def halo_matrices1():
    matrices = np.zeros((GROUP1, 384, 256), np.float32)
    for k in range(GROUP1):
        for half in (0, 1):
            for z in range(-H1, 64 + H1):
                if 0 <= z < 64:
                    row = (OWN + 64 * half + z) % 128
                elif z < 0:
                    row = 128 + 64 * half + 14 * k + z + H1
                else:
                    row = 256 + 64 * half + 14 * k + z - 64
                matrices[k, row, 128 * half + OWN + z] = 1.0
    return matrices


def thirds(value):
    high = value.astype(jnp.bfloat16)
    rest = value - high.astype(F32)
    mid = rest.astype(jnp.bfloat16)
    return (rest - mid.astype(F32)).astype(jnp.bfloat16), mid, high


def halves(value):
    high = value.astype(jnp.bfloat16)
    return (value - high.astype(F32)).astype(jnp.bfloat16), high


def move(pieces, matrix):
    total = None
    for parts in zip(*pieces):
        left = parts[0] if len(parts) == 1 else jnp.concatenate(parts, axis=1)
        term = jnp.dot(left, matrix, preferred_element_type=F32)
        total = term if total is None else total + term
    return total


def plane_pairs(first, last, body, unroll=4):
    def both(i):
        body(2 * i, 0)
        body(2 * i + 1, 1)

    loop(first // 2, last // 2, both, unroll)


def sum0(values, plane, parity, q, onto_red):
    mid, other = values[plane, q], values[plane, 1 - q]
    total = values[plane + 1, q] + values[plane - 1, q] + mid
    total = total + other + roll(other, 1 if q == 0 else -1, 0)
    high = ((parity + q) % 2 == 1) == onto_red
    return total + roll(mid, -1 if high else 1, 1)


def even_lanes(shape, parity):
    return (iota(shape, 1) + parity) % 2 == 0


def sum1(values, plane, parity, onto_red):
    mid = values[plane]
    total = values[plane + 1] + values[plane - 1] + mid
    total = total + roll(mid, 1, 1) + roll(mid, -1, 1)
    less, more = roll(mid, 1, 0), roll(mid, -1, 0)
    first, second = (less, more) if onto_red else (more, less)
    return total + jnp.where(even_lanes(mid.shape, parity), first, second)


def sum2(values, plane):
    mid = values[plane]
    total = values[plane + 1] + values[plane - 1]
    total = total + roll(mid, 1, 0) + roll(mid, -1, 0)
    return total + roll(mid, 1, 1) + roll(mid, -1, 1)


def is_red(shape, plane):
    return (iota(shape, 0) + iota(shape, 1) + plane) % 2 == 0


TILES = 40


def pack_y0(f, s, low, high, to_high, to_low, _):
    row = iota((8, LANES), 0)
    for field, own in enumerate((f, s)):
        at = field * TILES
        to_high[at : at + 32] = own[:, 24:32]
        to_low[at : at + 32] = own[:, 0:8]
        for side, halo in enumerate((low, high)):
            first = field * H0 + (H0 if side == 0 else -1)
            step = -1 if side == 0 else 1
            for dx in range(1, 5):
                near, far = first + step * dx, first + step * (8 - dx)
                tile = at + 32 + 4 * side + dx - 1
                above = roll(halo[far, 24:32], dx, 0)
                to_high[tile] = jnp.where(row >= dx, halo[near, 24:32], above)
                below = roll(halo[far, 0:8], 8 - dx, 0)
                to_low[tile] = jnp.where(row < 8 - dx, halo[near, 0:8], below)


def rows_y0(tiles, field, plane, above):
    at = field * TILES
    if H0 <= plane < H0 + 32:
        return tiles[at + plane - H0]
    side = 0 if plane < H0 else 1
    dx = H0 - plane if side == 0 else plane - H0 - 31
    tile = at + 31 + 4 * side
    if dx <= 4:
        return tiles[tile + dx]
    near = max(8 - dx, 1)
    return roll(tiles[tile + near], near - 8 if above else -near, 0)


def pack_z0(f, s, low, high, below, above, split, to_high, to_low, rows, _):
    lane = iota((Y0, LANES), 1)
    block = (lane + 8) % LANES // 16
    last = lane // 8 % 2 == 1
    pair = []
    for group in range(2 * X0 // GROUP0):
        packed = jnp.zeros((Y0, LANES), F32)
        for k in range(GROUP0):
            item = group * GROUP0 + k
            field, plane = divmod(item, X0)
            own = (f, s)[field]
            slot = item % 16
            rows[slot, 0:8, :] = rows_y0(below, field, plane, False)
            if plane < H0:
                rows[slot, 8:40, :] = low[field * H0 + plane]
            elif plane < H0 + 32:
                rows[slot, 8:40, :] = own[plane - H0]
            else:
                rows[slot, 8:40, :] = high[field * H0 + plane - H0 - 32]
            rows[slot, 40:48, :] = rows_y0(above, field, plane, True)
            even = rows[slot, pl.ds(0, 24, stride=2), :]
            odd = rows[slot, pl.ds(1, 24, stride=2), :]
            value = jnp.concatenate([even, odd], axis=0)
            split[item] = value
            packed = jnp.where(block == k, roll(value, 16 * k, 1), packed)
        pair.append(packed)
        if len(pair) == 2:
            to_high[group // 2] = jnp.where(last, pair[0], roll(pair[1], 8, 1))
            to_low[group // 2] = jnp.where(last, roll(pair[1], -8, 1), pair[0])
            pair = []


def down0(split, from_low, from_high, matrices, fr, fb, ir, ib, vb, own1, red, screen, copies):
    lane = iota((Y0, LANES), 1)
    groups = 2 * X0 // GROUP0
    merged = []
    for half in range(groups // 2):
        left, right = from_low[half], from_high[half]
        merged.append(jnp.where(lane // 8 % 2 == 1, left, right))
        merged.append(jnp.where(lane // 8 % 2 == 1, roll(left, -8, 1), roll(right, 8, 1)))
    merged = halves(jnp.concatenate(merged, axis=0))
    for k in range(GROUP0):
        own = [split[group * GROUP0 + k] for group in range(groups)]
        result = move([halves(jnp.concatenate(own, axis=0)), merged], matrices[k])
        for group in range(groups):
            field, plane = divmod(group * GROUP0 + k, X0)
            part = result[Y0 * group : Y0 * group + Y0]
            even, odd = part[:, :LANES], part[:, LANES:]
            if field == 1:
                screen[plane] = even[:24] + odd[:24] + even[24:] + odd[24:]
            for q in (0, 1):
                reds, blacks = (even, odd) if (k + q) % 2 == 0 else (odd, even)
                reds, blacks = reds[24 * q : 24 * q + 24], blacks[24 * q : 24 * q + 24]
                if field == 0:
                    fr[plane, q] = reds
                    fb[plane, q] = blacks
                else:
                    ir[plane, q] = 1.0 / (6.0 + reds)
                    ib[plane, q] = 1.0 / (6.0 + blacks)

    for at in range(4, 8):
        copies[at].start()

    def first(p):
        red[p] = fr[p] * ir[p]

    loop(0, X0, first, 4)

    def black(p, parity):
        for q in (0, 1):
            vb[p, q] = (fb[p, q] + sum0(red, p, parity, q, False)) * ib[p, q]

    black(1, 1)
    plane_pairs(2, X0 - 2, black)
    black(X0 - 2, 0)
    copies[8].start()

    def restrict(i):
        plane = 2 * i + H0
        source = 0.5 * below_sum(vb, plane)
        own = (iota((16, LANES), 1) + 128 - OWN) % LANES < 64
        screens = 0.5 * (screen[plane] + screen[plane + 1])[4:20]
        own1[i] = jnp.where(own, source[4:20], roll(screens, 64, 1))

    loop(0, 16, restrict)


def below_sum(values, plane):
    total = sum0(values, plane, 0, 0, True) + sum0(values, plane, 0, 1, True)
    total = total + sum0(values, plane + 1, 1, 0, True)
    return total + sum0(values, plane + 1, 1, 1, True)


def pack_z1(own, halos, coloured, to_high, to_low, _):
    block = iota((24, LANES), 1) % 64 // 14
    for group in range(own.shape[0] // GROUP1):
        up = [jnp.zeros((24, LANES), F32)] * 2
        down = [jnp.zeros((24, LANES), F32)] * 2
        for k in range(GROUP1):
            item = group * GROUP1 + k
            even, odd = [
                jnp.concatenate(
                    [
                        ref[at, pl.ds(q, 8, stride=2), :]
                        for ref, at in ((halos, item), (own, item), (halos, own.shape[0] + item))
                    ],
                    axis=0,
                )
                for q in (0, 1)
            ]
            here = even_lanes((24, LANES), item)
            for colour in (0, 1):
                first, second = (even, odd) if colour == 0 else (odd, even)
                value = jnp.where(here, first, second)
                coloured[item, colour] = value
                up[colour] = jnp.where(block == k, roll(value, 14 * k - 82, 1), up[colour])
                down[colour] = jnp.where(block == k, roll(value, 14 * k - 32, 1), down[colour])
        for colour in (0, 1):
            to_high[group, colour] = up[colour]
            to_low[group, colour] = down[colour]


def unpack1(coloured, from_low, from_high, matrices, store, first, last):
    groups = range(first // GROUP1, last // GROUP1)
    rows = len(groups) * 48
    halos = [
        halves(ref[groups.start : groups.stop].reshape(rows, LANES))
        for ref in (from_low, from_high)
    ]
    for k in range(GROUP1):
        own = [coloured[GROUP1 * g + k, colour] for g in groups for colour in (0, 1)]
        result = move([halves(jnp.concatenate(own, axis=0)), *halos], matrices[k])
        for at in range(2 * len(groups)):
            part = result[24 * at : 24 * at + 24]
            item = GROUP1 * groups[at // 2] + k
            store(item, at % 2, (part[:, :LANES], part[:, LANES:]))


def pair_index(rows):
    return jnp.clip(2 * iota((rows, LANES), 1) - OWN, 0, 127)


def spread_index(rows):
    return (iota((rows, LANES), 1) - OWN) // 2 + OWN


def coarse12(total):
    pairs = total + roll(total, -1, 1)
    return 0.5 * pick(pairs, pair_index(Y2))


def down12(f1, i1, b1, f2, i2, v2, red, begin, end):
    def first(p):
        red[p] = f1[p, 0] * i1[p, 0]

    loop(begin, end, first, 4)

    def black(p, parity):
        b1[p] = (f1[p, 1] + sum1(red, p, parity, False)) * i1[p, 1]

    black(begin + 1, 1)
    plane_pairs(begin + 2, end - 2, black)
    black(end - 2, 0)

    def restrict(i):
        plane = 2 * i + 2
        f2[i] = coarse12(sum1(b1, plane, 0, True) + sum1(b1, plane + 1, 1, True))

    begin2, end2 = begin // 2, end // 2 - 2
    loop(begin2, end2, restrict, 4)

    def red2(p):
        v2[p] = jnp.where(is_red((Y2, LANES), p), f2[p] * i2[p], 0.0)

    def black2(p):
        fresh = (f2[p] + sum2(v2, p)) * i2[p]
        v2[p] = jnp.where(is_red((Y2, LANES), p), v2[p], fresh)

    loop(begin2, end2, red2, 4)
    loop(begin2 + 1, end2 - 1, black2, 3)


def coarse23(total, sums, x3):
    sums[x3] = total
    pairs = sums[x3, pl.ds(8, 8, stride=2), :] + sums[x3, pl.ds(9, 8, stride=2), :]
    pairs = pairs + roll(pairs, -1, 1)
    lane = iota((8, LANES), 1)
    spread = pick(pairs, OWN + 2 * (lane % 16))
    here = lane // 16 == (x3 % 2) * 4 + iota((8, LANES), 0)
    here = jnp.logical_and(here, iota((8, LANES), 0) < 4)
    return 0.5 * jnp.sum(jnp.where(here, spread, 0.0), axis=0, keepdims=True)


def source3(v2, sums):
    rows = []
    for x3 in range(4):
        plane = 2 * x3 + H2
        total = jnp.zeros((Y2, LANES), F32)
        for p in (plane, plane + 1):
            total += jnp.where(is_red((Y2, LANES), p), sum2(v2, p), 0.0)
        rows.append(coarse23(total, sums, x3))
    return [rows[0] + rows[1], rows[2] + rows[3]]


def screens12(coloured, from_low, from_high, matrices, f1, i1, i2, begin, end):
    def store(plane, colour, halves):
        f1[plane, colour], i1[plane, colour] = halves

    unpack1(coloured, from_low, from_high, matrices, store, begin, end)

    def screen2(i):
        plane = 2 * i + 2
        total = i1[plane, 0] + i1[plane, 1] + i1[plane + 1, 0] + i1[plane + 1, 1]
        i2[i] = coarse12(total)

    loop(begin // 2, end // 2 - 2, screen2, 4)


def invert12(i1, i2, begin, end):
    def invert1(p):
        i1[p] = 1.0 / (6.0 + i1[p])

    def invert2(p):
        i2[p] = 1.0 / (6.0 + i2[p])

    loop(begin, end, invert1, 4)
    loop(begin // 2, end // 2 - 2, invert2, 4)


def first_message(
    coloured, from_low, from_high, matrices, message, f1, i1, b1, f2, i2, v2, red, sums, _
):
    screens12(coloured, from_low, from_high, matrices, f1, i1, i2, BEGIN, END)
    rows = []
    for x3 in range(4):
        plane = 2 * x3 + H2
        rows.append(coarse23(i2[plane] + i2[plane + 1], sums, x3))
    invert12(i1, i2, BEGIN, END)
    down12(f1, i1, b1, f2, i2, v2, red, BEGIN, END)
    tile = source3(v2, sums) + [rows[0] + rows[1], rows[2] + rows[3]]
    tile = jnp.concatenate(tile + tile, axis=0)
    for i in range(64):
        message[8 * i : 8 * i + 8, :] = tile


def down12_first(
    coloured, from_low, from_high, matrices, f1, i1, b1, f2, i2, v2, red, copies
):
    screens12(coloured, from_low, from_high, matrices, f1, i1, i2, 0, X1)
    invert12(i1, i2, 0, X1)
    for at in (4, 5, 8):
        copies[at].start()
    down12(f1, i1, b1, f2, i2, v2, red, 0, X1)
    for at in (6, 7, 9):
        copies[at].start()


def sources12(coloured, from_low, from_high, matrices, f1):
    def store(item, colour, halves):
        block, i = divmod(item, 8)
        for half in (0, 1):
            plane = H1 + 16 * (block - 1) + 8 * half + i
            if 0 <= plane < X1:
                f1[plane, colour] = halves[half]

    unpack1(coloured, from_low, from_high, matrices, store, 0, 24)


def down12_next(
    coloured, from_low, from_high, matrices, i1, i2, f1, b1, f2, v2, message, red, sums, copies
):
    sources12(coloured, from_low, from_high, matrices, f1)
    for at in (4, 5):
        copies[at].wait()
    down12(f1, i1, b1, f2, i2, v2, red, 0, X1)
    tile = jnp.concatenate(source3(v2, sums) * 4, axis=0)
    for i in range(32):
        message[8 * i : 8 * i + 8, :] = tile


def unpack3(message, rows, first, into):
    sub, lane = iota((8, LANES), 0), iota((8, LANES), 1)
    for gx in range(4):
        for gy in range(4):
            for half in range(2):
                start = (gx * 4 + gy) * 8 * rows + first + half
                value = message[pl.ds(start, 8, stride=rows), :]
                for k in (1, 2, 4):
                    sub_high = (sub // k) % 2 == 1
                    lane_high = (lane // (16 * k)) % 2 == 1
                    from_below = roll(roll(value, -k, 0), 16 * k, 1)
                    from_above = roll(roll(value, k, 0), -16 * k, 1)
                    value = jnp.where(
                        sub_high == lane_high, value, jnp.where(sub_high, from_above, from_below)
                    )
                for x in range(2):
                    into[gx * 4 + 2 * half + x, gy * 4 : gy * 4 + 4, :] = value[4 * x : 4 * x + 4, :]


def turn(value, shift, axis):
    if axis == 0:
        return jnp.concatenate([value[-shift:], value[:-shift]], axis=0)
    return roll(value, shift, axis)


def sum_whole(value):
    total = turn(value, 1, 0) + turn(value, -1, 0)
    total = total + turn(value, 1, 1) + turn(value, -1, 1)
    return total + turn(value, 1, 2) + turn(value, -1, 2)


def red_whole(shape):
    return (iota(shape, 0) + iota(shape, 1) + iota(shape, 2)) % 2 == 0


def pick3(value, index):
    flat = value.reshape(-1, LANES)
    return pick(flat, jnp.broadcast_to(index, flat.shape)).reshape(value.shape)


def coarse34(value, wide):
    wide[...] = value.reshape(8, 2, 16, LANES).sum(axis=1)
    pairs = wide[:, pl.ds(0, 8, stride=2), :] + wide[:, pl.ds(1, 8, stride=2), :]
    pairs = pairs + roll(pairs, -1, 2)
    return 0.5 * pick3(pairs, 2 * (iota((1, LANES), 1) % 64))


def coarse_solve(f3, i3, i4, place, inverse, e3, wide):
    red3, red4 = red_whole((16, 16, LANES)), red_whole((8, 8, LANES))
    v3 = jnp.where(red3, f3 * i3, 0.0)
    v3 = jnp.where(red3, v3, (f3 + sum_whole(v3)) * i3)
    f4 = coarse34(jnp.where(red3, sum_whole(v3), 0.0), wide)
    v4 = jnp.where(red4, f4 * i4, 0.0)
    v4 = jnp.where(red4, v4, (f4 + sum_whole(v4)) * i4)
    r4 = jnp.where(red4, sum_whole(v4), 0.0).reshape(4, 2, 8, LANES).sum(axis=1)
    sub, lane = iota((8, LANES), 0), iota((8, LANES), 1)
    rows = []
    for x5 in range(4):
        pairs = r4[x5] + roll(r4[x5], -1, 1)
        spread = jnp.where(sub // 2 == lane // 32, pick(pairs, 2 * (lane % 32)), 0.0)
        rows.append(0.5 * jnp.sum(spread, axis=0, keepdims=True))
    vector = jnp.broadcast_to(jnp.concatenate(rows, axis=1), (8, 512))
    rows = jnp.concatenate([ref[...] for ref in inverse] + [jnp.zeros((64, 512), F32)], axis=0)
    (low, high), (rows_low, rows_high) = halves(vector), halves(rows)
    answer = jnp.zeros((8, 256), F32)
    for left, right in ((low, rows_high), (high, rows_low), (high, rows_high)):
        answer = answer + lax.dot_general(
            left, right, (((1,), (1,)), ((), ())), preferred_element_type=F32
        )
    planes = []
    for x5 in range(4):
        z5 = lane % 64 // 2
        index = (place[0] + 4 - x5) % 4 * 16 + (place[1] + 4 - sub // 2) % 4 * 4 + z5 % 4
        apart = (z5 // 4 + 8 - place[2]) % 8
        same = pick(answer[:, :LANES], index + jnp.where(apart == 7, 64, 0))
        part = jnp.where(apart == 1, pick(answer[:, LANES:], index), same)
        part = jnp.where(jnp.logical_or(apart <= 1, apart == 7), part, 0.0)
        planes += [part[None], part[None]]
    w4 = v4 + jnp.concatenate(planes, axis=0)
    w4 = jnp.where(red4, (f4 + sum_whole(w4)) * i4, w4)
    e4 = jnp.where(red4, w4, (f4 + sum_whole(w4)) * i4)
    e4 = pick3(e4, iota((1, LANES), 1) // 2)
    wide[:, pl.ds(0, 8, stride=2), :] = e4
    wide[:, pl.ds(1, 8, stride=2), :] = e4
    spread = jnp.broadcast_to(wide[...][:, None], (8, 2, 16, LANES)).reshape(16, 16, LANES)
    w3 = v3 + spread
    w3 = jnp.where(red3, (f3 + sum_whole(w3)) * i3, w3)
    e3[...] = jnp.where(red3, w3, (f3 + sum_whole(w3)) * i3)


def up21(place, e3, f2, i2, v2, f1, i1, b1, e2, er, eb, tall):
    shift_y = lax.rem(20 - 4 * place[1], 16)
    shift_z = lax.rem(160 - 16 * place[2], 128)

    def from3(i):
        value = e3[lax.rem(4 * place[0] + i + 13, 16)]
        value = pltpu.roll(pltpu.roll(value, shift_y, 0), shift_z, 1)
        value = pick(value, spread_index(16))[:12]
        tall[i, pl.ds(0, 12, stride=2), :] = value
        tall[i, pl.ds(1, 12, stride=2), :] = value
        value = tall[i]
        e2[2 * i] = v2[2 * i] + value
        e2[2 * i + 1] = v2[2 * i + 1] + value

    loop(0, X2 // 2, from3, 5)

    def red2(p):
        fresh = (f2[p] + sum2(e2, p)) * i2[p]
        e2[p] = jnp.where(is_red((Y2, LANES), p), fresh, e2[p])

    def black2(p):
        fresh = (f2[p] + sum2(e2, p)) * i2[p]
        e2[p] = jnp.where(is_red((Y2, LANES), p), e2[p], fresh)

    loop(1, X2 - 1, red2, 3)
    loop(2, X2 - 2, black2, 4)

    def from2(i):
        value = pick(e2[i], spread_index(Y2))
        eb[2 * i + 2] = b1[2 * i + 2] + value
        eb[2 * i + 3] = b1[2 * i + 3] + value

    loop(3, 17, from2, 7)

    def red1(p, parity):
        er[p] = (f1[p, 0] + sum1(eb, p, parity, True)) * i1[p, 0]

    def black1(p, parity):
        eb[p] = (f1[p, 1] + sum1(er, p, parity, False)) * i1[p, 1]

    plane_pairs(8, 36, red1)
    plane_pairs(10, 34, black1)


def add0(er, eb, b, w, tall):
    def from1(i):
        reds, blacks = er[i + 10, 6:18], eb[i + 10, 6:18]
        here = (iota((12, LANES), 1) + i) % 2 == 0
        tall[i, pl.ds(0, 12, stride=2), :] = jnp.where(here, reds, blacks)
        tall[i, pl.ds(1, 12, stride=2), :] = jnp.where(here, blacks, reds)
        value = tall[i]
        for p in (2 * i, 2 * i + 1):
            for q in (0, 1):
                w[p, q] = b[p, q] + value

    loop(0, X0 // 2, from1, 4)


def own_sum(total):
    row, lane = iota((24, LANES), 0), iota((24, LANES), 1)
    own = jnp.logical_and((row + 20) % 24 < 16, (lane + 128 - OWN) % LANES < 64)
    return jnp.sum(jnp.where(own, total, 0.0), axis=0, keepdims=True)


def sum_over(body):
    def step(i, total):
        return total + body(2 * i, 0) + body(2 * i + 1, 1)

    return lax.fori_loop(H0 // 2, H0 // 2 + 16, step, jnp.zeros((24, LANES), F32), unroll=2)


def middle(
    message, place, near, before, after, f2, i2, v2, f1, i1, b1, fr, fb, ir, ib, vb,
    i3, i4, bnew, own1, norm,
    f3, e3, wide, tall, e2, er, eb, w, r, rnew, copies,
):
    unpack3(message, 4, 0, f3)
    unpack3(message, 4, 2, e3)
    screen3 = e3[...]
    screen4 = coarse34(screen3, wide)
    i3[...] = 1.0 / (6.0 + screen3)
    i4[...] = 1.0 / (6.0 + screen4)
    coarse_solve(f3[...], i3[...], i4[...], place, (near, before, after), e3, wide)
    for at in range(5, 11):
        copies[at].wait()
    up21(place, e3, f2, i2, v2, f1, i1, b1, e2, er, eb, tall)
    for at in range(11, 16):
        copies[at].wait()
    add0(er, eb, vb, w, tall)

    def red_up(p, parity):
        for q in (0, 1):
            r[p, q] = (fr[p, q] + sum0(w, p, parity, q, True)) * ir[p, q]

    plane_pairs(2, X0 - 2, red_up)

    def black_up(p, parity):
        for q in (0, 1):
            w[p, q] = (fb[p, q] + sum0(r, p, parity, q, False)) * ib[p, q]

    black_up(3, 1)
    plane_pairs(4, X0 - 4, black_up)
    black_up(X0 - 4, 0)

    def red_down(p, parity):
        for q in (0, 1):
            rnew[p, q] = (fr[p, q] + sum0(w, p, parity, q, True)) * ir[p, q]

    plane_pairs(4, X0 - 4, red_down)

    def squares(p, parity):
        total = jnp.zeros((24, LANES), F32)
        for q in (0, 1):
            part = (rnew[p, q] - r[p, q]) / ir[p, q]
            total = total + part * part
        return total

    norm[...] = jnp.broadcast_to(own_sum(sum_over(squares)), (8, LANES))

    def black_down(p, parity):
        for q in (0, 1):
            fresh = (fb[p, q] + sum0(rnew, p, parity, q, False)) * ib[p, q]
            bnew[p, q] = fresh
            r[p, q] = fresh - w[p, q]

    black_down(5, 1)
    plane_pairs(6, X0 - 6, black_down)
    black_down(X0 - 6, 0)

    def restrict(i):
        low = 0.5 * below_sum(r, 2 * i + H0)[4:20]
        high = 0.5 * below_sum(r, 2 * i + H0 + 16)[4:20]
        own = (iota((16, LANES), 1) + 128 - OWN) % LANES < 64
        own1[i] = jnp.where(own, low, roll(high, 64, 1))

    loop(0, 8, restrict)


def final(
    message, place, near, before, after, f2, i2, v2, f1, i1, b1, fr, fb, ir, ib, b, i3, i4,
    norm,
    sums, r, last,
    f3, e3, wide, tall, e2, er, eb, w, copies,
):
    unpack3(message, 2, 0, f3)
    coarse_solve(f3[...], i3[...], i4[...], place, (near, before, after), e3, wide)
    for at in (6, 9):
        copies[at].wait()
    up21(place, e3, f2, i2, v2, f1, i1, b1, e2, er, eb, tall)
    for at in range(11, 15):
        copies[at].wait()
    add0(er, eb, b, w, tall)

    def red_up(p, parity):
        for q in (0, 1):
            r[p, q] = (fr[p, q] + sum0(w, p, parity, q, True)) * ir[p, q]

    plane_pairs(6, X0 - 6, red_up)

    def black_up(p, parity):
        for q in (0, 1):
            fresh = (fb[p, q] + sum0(r, p, parity, q, False)) * ib[p, q]
            last[p, q] = fresh
            w[p, q] = fresh - w[p, q]

    black_up(7, 1)
    plane_pairs(8, X0 - 8, black_up)
    black_up(X0 - 8, 0)

    def squares(p, parity):
        total = jnp.zeros((24, LANES), F32)
        for q in (0, 1):
            part = sum0(w, p, parity, q, True)
            total = total + part * part
        return total

    squared = own_sum(sum_over(squares))

    low = iota((1, LANES), 1) < 64
    both = jnp.where(low, roll(norm[0:1, :], -OWN, 1), roll(squared, 64 - OWN, 1))
    for i in range(16):
        sums[8 * i : 8 * i + 8, :] = jnp.broadcast_to(both, (8, LANES))


def weave(r, last, matrix, field, _):
    def finish(i):
        parts = []
        for x in (0, 1):
            for q in (0, 1):
                order = (r, last) if x == q else (last, r)
                parts.append(jnp.concatenate([ref[2 * i + x, q] for ref in order], axis=1))
        result = move([thirds(jnp.concatenate(parts, axis=0))], matrix[...])
        for at in range(4):
            rows = result[24 * at + 4 : 24 * at + 20]
            field[2 * i + at // 2 - H0, pl.ds(at % 2, 16, stride=2), :] = rows

    loop(H0 // 2, H0 // 2 + 16, finish)


def exchange(to_high, to_low, axis):
    count = lax.axis_size(axis)
    up = [(i, (i + 1) % count) for i in range(count)]
    down = [(j, i) for i, j in up]
    return lax.ppermute(to_high, axis, up), lax.ppermute(to_low, axis, down)


def from_all(own, axis):
    count = lax.axis_size(axis)
    shifts = [[(i, (i + k) % count) for i in range(count)] for k in range(1, count)]
    return [lax.ppermute(own, axis, shift) for shift in shifts]


def together(first, second):
    both = lax.optimization_barrier((*first, *second))
    return both[: len(first)], both[len(first) :]


def exchange1(own, low, high, beside=()):
    from_low, from_high = exchange(high, low, "gx")
    own = jnp.concatenate([from_low, own, from_high], axis=0)
    below, above = exchange(own, own, "gy")
    if beside:
        (above,), beside = together((above,), exchange(*beside, "gz"))
    items = own.shape[0]
    message = (items // GROUP1, 2, 24, LANES)
    coloured, to_high, to_low = call(
        pack_z1, [(items, 2, 24, LANES), message, message], own, jnp.concatenate([below, above])
    )
    return (coloured, *exchange(to_high, to_low, "gz")), beside


def local(f, s, coarse_inverse):
    place = jnp.stack([lax.axis_index(axis) for axis in AXES]).astype(jnp.int32)
    low, high = exchange(
        jnp.concatenate([f[32 - H0 :], s[32 - H0 :]], axis=0),
        jnp.concatenate([f[:H0], s[:H0]], axis=0),
        "gx",
    )
    messages = call(pack_y0, [(2 * TILES, 8, LANES)] * 2, f, s, low, high)
    messages, others = together(messages, from_all(coarse_inverse, "gy"))
    inverse = jnp.concatenate([coarse_inverse, *others], axis=0)
    below, above = exchange(*messages, "gy")
    (below, above), others = together((below, above), from_all(inverse, "gx"))
    inverse = jnp.concatenate([inverse, *others], axis=0)
    groups = 2 * X0 // GROUP0
    line0, line1, line2 = (Y0, LANES), (24, LANES), (Y2, LANES)
    split, to_high, to_low = call(
        pack_z0,
        [(2 * X0, *line0), (groups // 2, *line0), (groups // 2, *line0)],
        *(f, s, low, high, below, above),
        scratch=[(16, *line0)],
    )
    level0, level1, level2 = (X0, 2, *line1), (X1, *line1), (X2, *line2)
    both1 = (X1, 2, *line1)
    matrices1 = jnp.asarray(halo_matrices1(), jnp.bfloat16)
    fr, fb, ir, ib, vb, own1 = call(
        down0,
        [Parked(level0, lambda ref, k=k: ref.at[k]) for k in range(5)] + [(16, 16, LANES)],
        split,
        *exchange(to_high, to_low, "gz"),
        jnp.asarray(lower_matrices(), jnp.bfloat16),
        scratch=[level0, (X0, *line1)],
        park=(56, *level0),
    )
    level1_parts, others = exchange1(own1, own1[:H1], own1[16 - H1 :], (inverse, inverse))
    inverse = (inverse, *others)
    (message,) = call(
        first_message,
        [(512, LANES)],
        *level1_parts,
        matrices1,
        scratch=[both1, both1, level1, level2, level2, level2, level1, (4, *line2)],
    )
    message = lax.all_to_all(message, AXES, 0, 0, tiled=True)
    f1, i1, b1, f2, i2, v2 = call(
        down12_first,
        [
            Parked(both1, lambda ref: ref.at[0]),
            Parked(both1, lambda ref: ref.at[1]),
            Parked(level1, lambda ref: ref.at[2, :, 0]),
            Parked(level2, lambda ref: ref.at[2, 0:X2, 1]),
            Parked(level2, lambda ref: ref.at[3, 0:X2, 0]),
            Parked(level2, lambda ref: ref.at[3, 0:X2, 1]),
        ],
        *level1_parts,
        matrices1,
        scratch=[level1],
        park=(60, *both1),
    )
    whole = (16, 16, LANES)
    work = [whole, whole, (8, 16, LANES), (X0 // 2, *line1), level2, level1, level1]
    work += [level0, level0, level0]
    i3, i4, bnew, own1, norm = call(
        middle,
        [whole, (8, 8, LANES), level0, (8, 16, LANES), (8, LANES)],
        message, place, *inverse, f2, i2, v2, f1, i1, b1, fr, fb, ir, ib, vb,
        scratch=work,
    )
    f1, b1, f2, v2, message = call(
        down12_next,
        [both1, level1, level2, level2, (256, LANES)],
        *exchange1(own1, own1, own1)[0],
        matrices1,
        i1,
        i2,
        scratch=[level1, (4, *line2)],
    )
    message = lax.all_to_all(message, AXES, 0, 0, tiled=True)
    sums, red, black = call(
        final,
        [(128, LANES), level0, level0],
        message, place, *inverse, f2, i2, v2, f1, i1, b1, fr, fb, ir, ib, bnew, i3, i4, norm,
        scratch=work[:-2],
    )
    sums = lax.all_to_all(sums, AXES, 0, 0, tiled=True)
    matrix = jnp.asarray(upper_matrix(), jnp.bfloat16)
    (field,) = call(weave, [(32, 32, LANES)], red, black, matrix)
    squares = jnp.sum(sums.reshape(128, 2, 64), axis=(0, 2))
    return field, jnp.sqrt(squares / CELLS)


def solution(mesh):
    return jax.shard_map(
        local,
        mesh=mesh,
        in_specs=(P("gx", "gy", "gz"), P("gx", "gy", "gz"), P(("gx", "gy", "gz"), None)),
        out_specs=(P("gx", "gy", "gz"), P()),
        check_vma=False,
    )
```
